128 devices in a mesh: lat: 8 (over y, core), lon: 16 (over x, z).
Axes of the slice: x: 4, y: 4, z: 4, core: 2. Of those that a mesh axis runs over, the one named last changes fastest.
Arguments:
- probes: float32 [128, 256, 4096], P(None, 'lat', 'lon'), may hold values from -6 to 6
- kappa: float32 [256, 4096], P('lat', 'lon'), may hold values from 0.12 to 0.24
- sweep_counts: int32 [256], P('lat'), may hold values from 1 to 4
- obs_cell: int32 [49152], P(('lat', 'lon')), may hold values from 0 to 8191
- obs_owner: int32 [49152, 1], P(('lat', 'lon')), may hold values from 0 to 15; in each aligned block of 384 rows (0 to 383, 384 to 767, ...) at most 48 rows name the same one
- obs_count: int32 [8, 16], P('lat', 'lon'), may hold values from 288 to 384
- r_inv: float32 [8, 16, 768, 768], P('lat', 'lon'), may hold values from -8 to 32
Outputs:
- sketch: float32 [128, 256, 4096], P(None, 'lat', 'lon')
- r_factor: float32 [128, 128], replicated
The draws below stay inside these ranges and needn't reach their ends.
All inputs are finite; a program needn't handle non-finite values.
Results may differ from the reference program's by a relative error of at most 0.00013.
Values sent between devices are 32-bit elements; how exact they have to be, the bound alone decides.
No kernel may reach another device: no remote copies, remote signals or barrier semaphores. Data moves between devices by JAX's collectives and lax.ppermute only.
A program may use at most 64 MiB of HBM per device.

```python
import math
import jax
import jax.numpy as jnp
import numpy as np
from jax import lax

K = 128
SWEEPS = 4
CAP = 48
CLAT = 32
CLON = 256
OBS_DEV = 384
NLAT = 256
NLON = 4096
M = 768
N_LAT = 8
N_LON = 16


def draw_sweep_counts(key, part):
    key = jax.random.fold_in(key, 3)
    first_key, second_key = jax.random.split(key)
    lower_counts = jax.random.randint(first_key, (NLAT,), 1, SWEEPS + 1)
    keep_lower = jax.random.randint(second_key, (NLAT,), 0, 4) == 0
    return jnp.where(keep_lower, lower_counts, SWEEPS).astype(jnp.int32)


def draw_obs_cell(key, part):
    key = jax.random.fold_in(key, 7)
    side_key, depth_key, row_key, col_key, spread_key = jax.random.split(key, 5)
    total_slots = N_LAT * N_LON * OBS_DEV
    side_ids = jax.random.randint(side_key, (total_slots,), 0, 4)
    depth_ids = jax.random.randint(depth_key, (total_slots,), 0, SWEEPS)
    along_row = jax.random.randint(row_key, (total_slots,), 0, CLAT)
    along_col = jax.random.randint(col_key, (total_slots,), 0, CLON)
    row_ids = jnp.where(side_ids == 0, depth_ids, jnp.where(side_ids == 1, CLAT - 1 - depth_ids, along_row))
    col_ids = jnp.where(side_ids == 2, depth_ids, jnp.where(side_ids == 3, CLON - 1 - depth_ids, along_col))
    anywhere = jax.random.randint(spread_key, (total_slots,), 0, 8) == 0
    row_ids = jnp.where(anywhere, along_row, row_ids)
    col_ids = jnp.where(anywhere, along_col, col_ids)
    return (row_ids * CLON + col_ids).astype(jnp.int32)


def draw_obs_count(key, part):
    key = jax.random.fold_in(key, 5)
    first_key, second_key = jax.random.split(key)
    counts_drawn = jax.random.randint(first_key, (N_LAT, N_LON), 3 * OBS_DEV // 4, OBS_DEV + 1)
    chosen = jax.random.randint(second_key, (), 0, N_LAT * N_LON)
    flat_ids = jnp.arange(N_LAT * N_LON).reshape(N_LAT, N_LON)
    return jnp.where(flat_ids == chosen, OBS_DEV, counts_drawn).astype(jnp.int32)


def draw_r_inv(key, part):
    key = jax.random.fold_in(key, 9)
    first_key, second_key = jax.random.split(key)
    off_part = jax.random.normal(first_key, (N_LAT, N_LON, M, M), jnp.float32) * (5.0 / math.sqrt(M))
    diagonal_part = jax.random.uniform(second_key, (N_LAT, N_LON, M), jnp.float32, 8.0, 32.0)
    on_diagonal = jnp.arange(M)[:, None] == jnp.arange(M)[None, :]
    return jnp.where(on_diagonal, diagonal_part[..., :, None], off_part).astype(jnp.float32)


def steps_of(own_key, extent, pieces, smallest, top_value):
    level, own = 1.0, jax.random.fold_in(own_key, 6)
    for dim, shards_of in pieces:
        steps = jnp.exp(jax.random.uniform(jax.random.fold_in(own, dim), (shards_of,), jnp.float32, smallest / len(pieces), top_value / len(pieces)))
        level = level * jnp.repeat(steps, extent[dim] // shards_of).reshape([-1 if axis == dim else 1 for axis in range(len(extent))])
    return level


def assign_block(rng, own, number, rows, amount, top, most, lean):
    ranking = jax.random.permutation(rng, amount)
    crowded, common = portions_of(amount, rows * top, most, lean, True), portions_of(amount, rows * top, most, lean, False)
    places = jnp.arange(amount)

    def named(tallies, turn):
        used = int((tallies > 0).sum())
        fixed = max(1, used // 4)
        shifted = fixed + (places - fixed + turn * (used - fixed)) % max(1, amount - fixed)
        return jnp.zeros((amount,), jnp.int32).at[ranking[jnp.where(places < fixed, places, shifted)]].set(jnp.asarray(tallies, jnp.int32))

    tallies = jnp.where(number % 4 == 0, named(crowded, number // 4), named(common, number - number // 4 - 1))
    mixed = jax.random.permutation(jax.random.fold_in(own, 3), amount)
    giver, sink = mixed[0:amount // 2 * 2:2], mixed[1:amount // 2 * 2:2]
    margin = jnp.minimum(tallies[giver] - 1, most - tallies[sink]) // 2
    margin = jnp.where((giver == ranking[0]) | (sink == ranking[0]) | (tallies[sink] == 0), 0, jnp.maximum(margin, 0))
    shifted = jax.random.randint(jax.random.fold_in(own, 4), (amount // 2,), 0, 1 << 20) % (margin + 1)
    tallies = tallies.at[giver].add(-shifted).at[sink].add(shifted)
    items = jnp.searchsorted(jnp.cumsum(tallies), jnp.arange(rows * top), side="right").astype(jnp.int32)
    grid = items.reshape(top, rows).T
    grid = grid[jax.random.permutation(jax.random.fold_in(own, 1), rows)]
    turn = jax.random.randint(jax.random.fold_in(own, 2), (rows, 1), 0, top)
    return jnp.take_along_axis(grid, (jnp.arange(top)[None, :] + turn) % top, axis=1)


def portions_of(number_of, total, most, lean, full):
    weights = [(1 << 20) // math.isqrt(grade ** lean) + 1 for grade in range(1, number_of + 1)]
    largest = most if full else min(most, max(-(-total // number_of), total * weights[0] // sum(weights)))
    least = 1 if total - largest >= number_of - 1 else 0
    counts, rest = [largest] + [least] * (number_of - 1), total - largest - least * (number_of - 1)
    while rest > 0:
        free = [i for i in range(1, number_of) if counts[i] < largest] or [i for i in range(1, number_of) if counts[i] < most]
        whole, remaining = sum([weights[i] for i in free]), rest
        for i in free:
            addition = min(most - counts[i], max(1, remaining * weights[i] // whole), rest)
            counts[i] = counts[i] + addition
            rest = rest - addition
    return np.array(counts)


def centred(own_key, shape, scale, limit, cuts=(), held_as=jnp.bfloat16):
    loudness = steps_of(own_key, shape, cuts, -0.22, 0.18) if cuts else 1.0
    drawn = jax.random.normal(own_key, shape, jnp.float32) * scale * loudness
    return jnp.minimum(jnp.maximum(drawn, -limit), limit).astype(held_as)


def setup_inputs(seed: int = 0) -> dict:
    key_of = jax.random.split(jax.random.key(seed), 8)
    probes = centred(key_of[0], (K, NLAT, NLON), 1.0, 6.0, ((1, 8), (2, 16)), jnp.float32)
    kappa = jnp.clip(jnp.exp(math.log(0.24) - 0.6931472 * jax.random.uniform(key_of[1], (NLAT, NLON), jnp.float32) ** steps_of(key_of[1], (NLAT, NLON), ((0, 8), (1, 16)), -0.2, 0.2)), 0.12, 0.24)
    sweep_counts = draw_sweep_counts(jax.random.fold_in(key_of[7], 71), 0)
    obs_cell = draw_obs_cell(jax.random.fold_in(key_of[7], 71), 0)
    obs_owner_keys = jax.random.split(jax.random.fold_in(key_of[4], 1), (N_LAT * N_LON * OBS_DEV) // OBS_DEV)
    obs_owner_turns = jax.random.permutation(jax.random.fold_in(key_of[4], 3), (N_LAT * N_LON * OBS_DEV) // OBS_DEV)
    obs_owner = jax.vmap(lambda own, number: assign_block(jax.random.fold_in(key_of[4], 2), own, number, OBS_DEV, N_LON, 1, CAP, 2))(obs_owner_keys, obs_owner_turns).reshape((N_LAT * N_LON * OBS_DEV, 1))
    obs_count = draw_obs_count(jax.random.fold_in(key_of[7], 71), 0)
    r_inv = draw_r_inv(jax.random.fold_in(key_of[7], 71), 0)
    return dict(probes=probes, kappa=kappa, sweep_counts=sweep_counts, obs_cell=obs_cell, obs_owner=obs_owner, obs_count=obs_count, r_inv=r_inv)


def diffuse(state_field, kappa, sweep_counts):
    for sweep_step in range(SWEEPS):
        padded = jnp.pad(state_field, ((0, 0), (1, 1), (1, 1)))
        center = padded[:, 1:-1, 1:-1]
        laplace_sum = padded[:, :-2, 1:-1] + padded[:, 2:, 1:-1] + padded[:, 1:-1, :-2] + padded[:, 1:-1, 2:] - 4.0 * center
        active = (sweep_counts > sweep_step)[:, None]
        state_field = center + jnp.where(active, kappa * laplace_sum, 0.0)
    return state_field

def reference(probes, kappa, sweep_counts, obs_cell, obs_owner, obs_count, r_inv):
    devices_all = N_LAT * N_LON
    smoothed = diffuse(probes, kappa, sweep_counts)
    owner_ids = obs_owner.reshape(devices_all, OBS_DEV)
    cell_ids = obs_cell.reshape(devices_all, OBS_DEV)
    counts_all = obs_count.reshape(devices_all)
    slot_ids = jnp.arange(OBS_DEV, dtype=jnp.int32)
    is_live = slot_ids[None, :] < counts_all[:, None]
    owner_hit = ((owner_ids[:, :, None] == jnp.arange(N_LON, dtype=jnp.int32)[None, None, :]) & is_live[:, :, None]).astype(jnp.int32)
    slot_rank = jnp.sum(jnp.cumsum(owner_hit, axis=1) * owner_hit, axis=2) - 1
    device_ids = jnp.arange(devices_all, dtype=jnp.int32)
    band_lat = device_ids // N_LON
    band_lon = device_ids % N_LON
    lat_rows = band_lat[:, None] * CLAT + cell_ids // CLON
    lon_cols = band_lon[:, None] * CLON + cell_ids % CLON
    place_ids = jnp.where(is_live, band_lon[:, None] * CAP + slot_rank, 0).astype(jnp.int32)
    owner_dev = (band_lat[:, None] * N_LON + owner_ids).astype(jnp.int32)
    picked = jnp.where(is_live[None], smoothed[:, lat_rows, lon_cols], 0.0)
    owner_buffer = jnp.zeros((K, devices_all, M), jnp.float32).at[:, owner_dev, place_ids].add(picked)
    weighted = jnp.einsum('kdm,dmn->kdn', owner_buffer, r_inv.reshape(devices_all, M, M), precision=lax.Precision.HIGHEST)
    answered = jnp.where(is_live[None], weighted[:, owner_dev, place_ids], 0.0)
    adjoint = jnp.zeros((K, NLAT, NLON), jnp.float32).at[:, lat_rows, lon_cols].add(answered)
    sketch = probes + diffuse(adjoint, kappa, sweep_counts)
    flat_sketch = sketch.reshape(K, NLAT * NLON)
    gram = jnp.dot(flat_sketch.astype(jnp.float32), flat_sketch.T.astype(jnp.float32), precision=lax.Precision.HIGHEST, preferred_element_type=jnp.float32) / (NLAT * NLON)
    r_factor = jnp.linalg.cholesky(gram).T
    return (sketch, r_factor)
```

```python
import functools

import jax
import jax.numpy as jnp
from jax import lax
from jax.experimental import pallas as pl
from jax.experimental.pallas import tpu as pltpu
from jax.sharding import PartitionSpec as P

SWEEPS = 4
CAP = 48
K = 128
R = 32
C = 256
H = 4
RE = R + 2 * H
CB = C + 16
NROW = RE * CB
OFF = 8
SLOTS = 384
PLACES = 768
LANES = 128
VMEM_LIMIT = 30 * 1024 * 1024
LAT_ROWS = H * C + 16
OWN_ROWS = R * H + R


def vmem_spec():
    return pl.BlockSpec(memory_space=pltpu.VMEM)


def smem_spec():
    return pl.BlockSpec(memory_space=pltpu.SMEM)


def hbm_spec():
    return pl.BlockSpec(memory_space=pltpu.HBM)


def params():
    return pltpu.CompilerParams(vmem_limit_bytes=VMEM_LIMIT)


def f32(*shape):
    return jax.ShapeDtypeStruct(shape, jnp.float32)


def at(r, c):
    return OFF + r * CB + c


def edge_pack_kernel(flags, counts, kappa_ref, p_hbm, pay_a, pay_b, chunk, sems):
    odd = flags[0]
    first = (jnp.where(odd == 1, 0, R - H), jnp.where(odd == 1, R - H, 0))
    copies = []
    for side in range(2):
        block = pl.multiple_of(jnp.where(first[side] == 0, 0, R - 8), 8)
        for half in range(2):
            n = side * 2 + half
            copies.append(pltpu.make_async_copy(
                p_hbm.at[:, pl.ds(block, 8), pl.ds(half * LANES, LANES)], chunk.at[n], sems.at[n]))
            copies[-1].start()
    flat = chunk.reshape(4 * K * 8, LANES)
    for side, pay in ((0, pay_a), (1, pay_b)):
        within = jnp.where(first[side] == 0, 0, 8 - H)
        for r in range(H):
            for half in range(2):
                lanes = slice(half * LANES, (half + 1) * LANES)
                pay[H * C + 2 * r + half:H * C + 2 * r + half + 1, :] = jnp.where(
                    first[side] == 0, kappa_ref[r:r + 1, lanes], kappa_ref[R - H + r:R - H + r + 1, lanes])
            value = counts[first[side] + r].astype(jnp.float32)
            pay[H * C + 8 + r:H * C + 9 + r, :] = jnp.full((1, K), value, jnp.float32)
        pay[H * C + 8 + H:, :] = jnp.zeros((4, K), jnp.float32)
        for half in range(2):
            n = side * 2 + half
            copies[n].wait()
            for r in range(H):
                pay[r * C + half * LANES:r * C + (half + 1) * LANES, :] = flat[
                    pl.ds(n * K * 8 + within + r, K, stride=8), :].T


def edge_pack(flags, counts, kappa, probes):
    return pl.pallas_call(
        edge_pack_kernel,
        in_specs=[smem_spec(), smem_spec(), vmem_spec(), hbm_spec()],
        out_specs=[vmem_spec()] * 2,
        out_shape=[f32(LAT_ROWS, K)] * 2,
        scratch_shapes=[pltpu.VMEM((4, K, 8, LANES), jnp.float32), pltpu.SemaphoreType.DMA((4,))],
        compiler_params=pltpu.CompilerParams(vmem_limit_bytes=8 * 1024 * 1024),
        name="edge_pack",
    )(flags, counts, kappa, probes)


def turn_kernel(flags, kappa_ref, p_hbm, y_ref, own_a, own_b, chunk, sems):
    def copy(n):
        half, block = n // 4, n % 4
        return pltpu.make_async_copy(
            p_hbm.at[:, pl.ds(block * 8, 8), pl.ds(half * LANES, LANES)], chunk.at[n], sems.at[n])

    for n in range(8):
        copy(n).start()
    flat = chunk.reshape(8 * K * 8, LANES)
    for n in range(8):
        copy(n).wait()
        half, block = n // 4, n % 4
        for i in range(8):
            r = block * 8 + i
            y_ref[r, half * LANES:(half + 1) * LANES, :] = flat[pl.ds(n * K * 8 + i, K, stride=8), :].T
    odd = flags[2]
    for own, low in ((own_a, odd), (own_b, 1 - odd)):
        col = jnp.where(low == 1, 0, C - H)
        lane = pl.multiple_of(jnp.where(low == 1, 0, LANES), LANES)
        for r in range(R):
            own[r * H:(r + 1) * H, :] = y_ref[r, pl.ds(col, H), :]
        own[R * H:, :] = kappa_ref[:, pl.ds(lane, LANES)]


def turn(flags, kappa, probes):
    return pl.pallas_call(
        turn_kernel,
        in_specs=[smem_spec(), vmem_spec(), hbm_spec()],
        out_specs=[vmem_spec()] * 3,
        out_shape=[f32(R, C, K), f32(OWN_ROWS, K), f32(OWN_ROWS, K)],
        scratch_shapes=[pltpu.VMEM((8, K, 8, LANES), jnp.float32), pltpu.SemaphoreType.DMA((8,))],
        compiler_params=pltpu.CompilerParams(vmem_limit_bytes=12 * 1024 * 1024),
        cost_estimate=pl.CostEstimate(flops=0, bytes_accessed=12 * 1024 * 1024, transcendentals=0),
        name="turn",
    )(flags, kappa, probes)


def corner_kernel(flags, own_a, own_b, lat_a, lat_b, pay_a, pay_b):
    odd = flags[2]
    own_rows = own_a.shape[0]
    for own, pay, low in ((own_a, pay_a, odd), (own_b, pay_b, 1 - odd)):
        col = jnp.where(low == 1, 0, C - H)
        pay[:own_rows, :] = own[...]
        base = own_rows
        for lat in (lat_a, lat_b):
            for r in range(H):
                pay[base:base + H, :] = lat[pl.ds(r * C + col, H), :]
                base += H
        if own_rows > R * H:
            for lat in (lat_a, lat_b):
                for r in range(H):
                    pay[base:base + 1, :] = lat[pl.ds(H * C + 2 * r + 1 - low, 1), :]
                    base += 1


def corner(flags, own_a, own_b, lat_a, lat_b):
    rows = own_a.shape[0] + 2 * H * H + (2 * H if own_a.shape[0] > R * H else 0)
    return pl.pallas_call(
        corner_kernel,
        in_specs=[smem_spec()] + [vmem_spec()] * 4,
        out_specs=[vmem_spec()] * 2,
        out_shape=[f32(rows, K)] * 2,
        compiler_params=pltpu.CompilerParams(vmem_limit_bytes=8 * 1024 * 1024),
        name="corner",
    )(flags, own_a, own_b, lat_a, lat_b)


def put_halos(buf, flags, lat_a, lat_b, lon_a, lon_b):
    odd = flags[0]
    lon_odd = flags[2]
    lat_ok = (None, flags[1] == 1)
    lon_ok = (None, flags[3] == 1)
    lat_row = (jnp.where(odd == 1, 0, R + H), jnp.where(odd == 1, R + H, 0))
    lon_col = (jnp.where(lon_odd == 1, 0, C + H), jnp.where(lon_odd == 1, C + H, 0))

    def keep(ok, x):
        return x if ok is None else jnp.where(ok, x, 0.0)

    own_rows = lon_a.shape[0] - 2 * H * H
    own_rows = R * H if own_rows == R * H else OWN_ROWS
    for n, lat in ((0, lat_a), (1, lat_b)):
        for r in range(H):
            start = pl.multiple_of(OFF + (lat_row[n] + r) * CB + 8, 8)
            buf[pl.ds(start, C), :] = keep(lat_ok[n], lat[r * C:(r + 1) * C, :])
    for m, lon in ((0, lon_a), (1, lon_b)):
        for r in range(R):
            start = at(r + H, 4) + lon_col[m]
            buf[pl.ds(start, H), :] = keep(lon_ok[m], lon[r * H:(r + 1) * H, :])
        for n in range(2):
            for r in range(H):
                part = own_rows + (n * H + r) * H
                start = OFF + (lat_row[n] + r) * CB + 4 + lon_col[m]
                buf[pl.ds(start, H), :] = keep(lat_ok[n], keep(lon_ok[m], lon[part:part + H, :]))


def put_kappa(kap, act, flags, counts, kappa_ref, lat_a, lat_b, lon_a, lon_b):
    odd = flags[0]
    lon_odd = flags[2]
    lat_ok = (None, flags[1] == 1)
    lat_row = (jnp.where(odd == 1, 0, R + H), jnp.where(odd == 1, R + H, 0))
    lon_col = (jnp.where(lon_odd == 1, 0, C + H), jnp.where(lon_odd == 1, C + H, 0))
    kap_t = kappa_ref[...].T
    for r in range(R):
        kap[pl.ds(at(r + H, 8), C), :] = jnp.broadcast_to(kap_t[:, r:r + 1], (C, K))
    for n, lat in ((0, lat_a), (1, lat_b)):
        turned = lat[H * C:H * C + 8, :].T
        if n == 1:
            turned = jnp.where(lat_ok[1], turned, 0.0)
        for r in range(H):
            for h in range(2):
                start = pl.multiple_of(OFF + (lat_row[n] + r) * CB + 8 + h * LANES, 8)
                kap[pl.ds(start, LANES), :] = jnp.broadcast_to(turned[:, 2 * r + h:2 * r + h + 1], (LANES, K))
        for r in range(H):
            wide = jnp.broadcast_to(lat[H * C + 8 + r:H * C + 9 + r, :], (8, K))
            for s in range(SWEEPS):
                act[s, lat_row[n] + r] = jnp.where(wide > s, 1.0, 0.0)
    for r in range(R):
        for s in range(SWEEPS):
            act[s, r + H] = jnp.full((8, K), jnp.where(counts[r] > s, 1.0, 0.0), jnp.float32)
    for m, lon in ((0, lon_a), (1, lon_b)):
        src = (jnp.where(lon_odd == 1, LANES - H, 0), jnp.where(lon_odd == 1, 0, LANES - H))[m]
        own = lon[R * H:R * H + R, :].T
        tail = lon[OWN_ROWS + 2 * H * H:, :].T
        low, high = own[:H, :], own[LANES - H:, :]
        edge = jnp.where(src == 0, low, high)
        tail = jnp.where(src == 0, tail[:H, :], tail[LANES - H:, :])
        if m == 1:
            edge = jnp.where(flags[3] == 1, edge, 0.0)
            tail = jnp.where(flags[3] == 1, tail, 0.0)
        for r in range(R):
            kap[pl.ds(at(r + H, 4) + lon_col[m], H), :] = jnp.broadcast_to(edge[:, r:r + 1], (H, K))
        for n in range(2):
            for r in range(H):
                part = jnp.broadcast_to(tail[:, n * H + r:n * H + r + 1], (H, K))
                if n == 1:
                    part = jnp.where(lat_ok[1], part, 0.0)
                kap[pl.ds(OFF + (lat_row[n] + r) * CB + 4 + lon_col[m], H), :] = part


def sweep(src, dst, kap, act, s):
    first = s + 1
    count = RE - 2 * first

    def body(i, _):
        r = first + 2 * i
        base = pl.multiple_of(r * CB, 8)
        a0 = act[s, r]
        a1 = act[s, r + 1]
        for t in range(CB // 8):
            o = base + OFF + t * 8
            up = src[pl.ds(o - CB, 8), :]
            c0 = src[pl.ds(o, 8), :]
            c1 = src[pl.ds(o + CB, 8), :]
            dn = src[pl.ds(o + 2 * CB, 8), :]
            l0 = src[pl.ds(o - 1, 8), :]
            r0 = src[pl.ds(o + 1, 8), :]
            l1 = src[pl.ds(o + CB - 1, 8), :]
            r1 = src[pl.ds(o + CB + 1, 8), :]
            lap0 = (up + c1) + (l0 + r0) - 4.0 * c0
            lap1 = (c0 + dn) + (l1 + r1) - 4.0 * c1
            dst[pl.ds(o, 8), :] = c0 + (a0 * kap[pl.ds(o, 8), :]) * lap0
            dst[pl.ds(o + CB, 8), :] = c1 + (a1 * kap[pl.ds(o + CB, 8), :]) * lap1
        return 0

    lax.fori_loop(0, count // 2, body, 0)


def smooth_kernel(flags, counts, cell_ref, place_ref, y_ref, kap_ref, lat_a, lat_b, lon_a, lon_b,
                  out_ref, kap, act, buf_a, buf_b, rows_ref):
    for r in range(R):
        buf_a[pl.ds(at(r + H, 8), C), :] = y_ref[r]
    put_halos(buf_a, flags, lat_a, lat_b, lon_a, lon_b)
    put_kappa(kap, act, flags, counts, kap_ref, lat_a, lat_b, lon_a, lon_b)
    bufs = (buf_a, buf_b)
    for s in range(SWEEPS):
        sweep(bufs[s % 2], bufs[(s + 1) % 2], kap, act, s)
    rows_ref[...] = jnp.zeros_like(rows_ref)

    def copy(i, _):
        for j in range(8):
            t = i * 8 + j
            rows_ref[pl.ds(place_ref[t], 1), :] = buf_a[pl.ds(cell_ref[t], 1), :]
        return 0

    lax.fori_loop(0, SLOTS // 8, copy, 0)
    out_ref[...] = rows_ref[:PLACES]


def smooth(flags, counts, cell, place, y, kappa, halos):
    return pl.pallas_call(
        smooth_kernel,
        in_specs=[smem_spec()] * 4 + [vmem_spec()] * 6,
        out_specs=[vmem_spec()] * 3,
        out_shape=[f32(PLACES, K), f32(NROW + 16, K), f32(SWEEPS, RE, 8, K)],
        scratch_shapes=[
            pltpu.VMEM((NROW + 16, K), jnp.float32),
            pltpu.VMEM((NROW + 16, K), jnp.float32),
            pltpu.VMEM((PLACES + 8, K), jnp.float32),
        ],
        compiler_params=params(),
        name="smooth",
    )(flags, counts, cell, place, y, kappa, *halos)


def split_kernel(r_ref, high_ref, low_ref):
    for i in range(PLACES // LANES):
        part = r_ref[:, i * LANES:(i + 1) * LANES].T
        high = part.astype(jnp.bfloat16)
        high_ref[i * LANES:(i + 1) * LANES, :] = high
        low_ref[i * LANES:(i + 1) * LANES, :] = (part - high.astype(jnp.float32)).astype(jnp.bfloat16)


def split(r):
    return pl.pallas_call(
        split_kernel,
        in_specs=[vmem_spec()],
        out_specs=[vmem_spec()] * 2,
        out_shape=[jax.ShapeDtypeStruct((PLACES, PLACES), jnp.bfloat16)] * 2,
        compiler_params=pltpu.CompilerParams(vmem_limit_bytes=8 * 1024 * 1024),
        cost_estimate=pl.CostEstimate(flops=0, bytes_accessed=6 * 1024 * 1024, transcendentals=0),
        name="split",
    )(r)


def weigh_kernel(high_ref, low_ref, b_ref, out_ref):
    b = b_ref[...]
    high = b.astype(jnp.bfloat16)
    low = (b - high.astype(jnp.float32)).astype(jnp.bfloat16)
    both = jnp.concatenate([high, low], axis=1)
    one = jnp.dot(high_ref[...], both, preferred_element_type=jnp.float32)
    two = jnp.dot(low_ref[...], high, preferred_element_type=jnp.float32)
    out_ref[...] = one[:, :K] + (one[:, K:] + two)


def weigh(high, low, buffer):
    return pl.pallas_call(
        weigh_kernel,
        in_specs=[vmem_spec()] * 3,
        out_specs=vmem_spec(),
        out_shape=f32(PLACES, K),
        compiler_params=pltpu.CompilerParams(vmem_limit_bytes=12 * 1024 * 1024),
        name="weigh",
    )(high, low, buffer)


def spread_kernel(flags, cell_ref, place_ref, count_ref, ret_ref, field, pay_a, pay_b, own_a, own_b):
    field[...] = jnp.zeros_like(field)

    def add(t, _):
        i = pl.ds(cell_ref[t], 1)
        field[i, :] = field[i, :] + ret_ref[pl.ds(place_ref[t], 1), :]
        return 0

    lax.fori_loop(0, count_ref[0], add, 0)
    odd = flags[0]
    lon_odd = flags[2]
    for pay, low in ((pay_a, odd), (pay_b, 1 - odd)):
        first = jnp.where(low == 1, H, R)
        for r in range(H):
            start = pl.multiple_of(OFF + (first + r) * CB + 8, 8)
            pay[r * C:(r + 1) * C, :] = field[pl.ds(start, C), :]
    for own, low in ((own_a, lon_odd), (own_b, 1 - lon_odd)):
        col = jnp.where(low == 1, 8, 4 + C)
        for r in range(R):
            own[r * H:(r + 1) * H, :] = field[pl.ds(at(r + H, 0) + col, H), :]


def spread(flags, cell, place, count, returned):
    return pl.pallas_call(
        spread_kernel,
        in_specs=[smem_spec()] * 4 + [vmem_spec()],
        out_specs=[vmem_spec()] * 5,
        out_shape=[f32(NROW + 16, K), f32(H * C, K), f32(H * C, K), f32(R * H, K), f32(R * H, K)],
        compiler_params=pltpu.CompilerParams(vmem_limit_bytes=10 * 1024 * 1024),
        name="spread",
    )(flags, cell, place, count, returned)


def finish_kernel(flags, field, kap, act, lat_a, lat_b, lon_a, lon_b, p_hbm, out_hbm, gram_ref,
                  buf_a, buf_b, chunk, in_sems, out_sems):
    def part(ref, n):
        half, block = n // 4, n % 4
        return ref.at[:, pl.ds(block * 8, 8), pl.ds(half * LANES, LANES)]

    def copy_in(n):
        return pltpu.make_async_copy(part(p_hbm, n), chunk.at[n], in_sems.at[n])

    def copy_out(n):
        return pltpu.make_async_copy(chunk.at[n], part(out_hbm, n), out_sems.at[n])

    for n in range(8):
        copy_in(n).start()
    buf_a[...] = field[...]
    put_halos(buf_a, flags, lat_a, lat_b, lon_a, lon_b)
    bufs = (buf_a, buf_b)
    for s in range(SWEEPS):
        sweep(bufs[s % 2], bufs[(s + 1) % 2], kap, act, s)
    flat = chunk.reshape(8 * K * 8, LANES)
    contract = (((1,), (1,)), ((), ()))
    hh = jnp.zeros((K, K), jnp.float32)
    hl = jnp.zeros((K, K), jnp.float32)
    for n in range(8):
        half, block = n // 4, n % 4
        copy_in(n).wait()
        for i in range(0, 8, 2):
            parts = []
            for j in range(2):
                where = pl.ds(n * K * 8 + i + j, K, stride=8)
                start = at(block * 8 + i + j + H, 8) + half * LANES
                sk = flat[where, :] + buf_a[pl.ds(start, LANES), :].T
                flat[where, :] = sk
                parts.append(sk)
            sk = jnp.concatenate(parts, axis=1)
            high = sk.astype(jnp.bfloat16)
            low = (sk - high.astype(jnp.float32)).astype(jnp.bfloat16)
            hh = hh + lax.dot_general(high, high, contract, preferred_element_type=jnp.float32)
            hl = hl + lax.dot_general(high, low, contract, preferred_element_type=jnp.float32)
        copy_out(n).start()
    gram_ref[...] = hh + (hl + hl.T)
    for n in range(8):
        copy_out(n).wait()


def finish(flags, field, kap, act, halos, probes):
    return pl.pallas_call(
        finish_kernel,
        in_specs=[smem_spec()] + [vmem_spec()] * 7 + [hbm_spec()],
        out_specs=[hbm_spec(), vmem_spec()],
        out_shape=[f32(K, R, C), f32(K, K)],
        scratch_shapes=[
            pltpu.VMEM((NROW + 16, K), jnp.float32),
            pltpu.VMEM((NROW + 16, K), jnp.float32),
            pltpu.VMEM((8, K, 8, LANES), jnp.float32),
            pltpu.SemaphoreType.DMA((8,)),
            pltpu.SemaphoreType.DMA((8,)),
        ],
        compiler_params=params(),
        name="finish",
    )(flags, field, kap, act, *halos, probes)


def pairs(size, first):
    return [(i, (i + 1) % size if (i - first) % 2 == 0 else (i - 1) % size) for i in range(size)]


def swap(a, b, axis):
    size = lax.axis_size(axis)
    return lax.ppermute(a, axis, pairs(size, 0)), lax.ppermute(b, axis, pairs(size, 1))


def sum_everywhere(x):
    n_lat, n_lon = lax.axis_size("lat"), lax.axis_size("lon")

    def stage(x, axis, perms):
        got = [lax.ppermute(x, axis, p) for p in perms]
        for g in got:
            x = x + g
        return x

    x = stage(x, "lat", [[(i, i ^ 1) for i in range(n_lat)]])
    x = stage(x, "lat", [[(i, i ^ (2 * d)) for i in range(n_lat)] for d in (1, 2, 3)])
    x = stage(x, "lon", [[(i, i ^ d) for i in range(n_lon)] for d in (1, 2, 3)])
    return stage(x, "lon", [[(i, i ^ (4 * d)) for i in range(n_lon)] for d in (1, 2, 3)])


def shards(probes, kappa, sweep_counts, obs_cell, obs_owner, obs_count, r_inv):
    n_lat, n_lon = lax.axis_size("lat"), lax.axis_size("lon")
    lat, lon = lax.axis_index("lat"), lax.axis_index("lon")
    flags = jnp.stack([
        lat % 2, ((lat > 0) & (lat < n_lat - 1)).astype(jnp.int32),
        lon % 2, ((lon > 0) & (lon < n_lon - 1)).astype(jnp.int32),
    ]).astype(jnp.int32)
    lat_a, lat_b = swap(*edge_pack(flags, sweep_counts, kappa, probes), "lat")
    y, own_a, own_b = turn(flags, kappa, probes)
    high, low = split(r_inv[0, 0])
    halos = (lat_a, lat_b) + swap(*corner(flags, own_a, own_b, lat_a, lat_b), "lon")

    count = obs_count.reshape(1)
    slot_ids = jnp.arange(SLOTS, dtype=jnp.int32)
    is_live = slot_ids < count
    owner_ids = obs_owner[:, 0]
    owner_hit = (
        (owner_ids[:, None] == jnp.arange(n_lon, dtype=jnp.int32)[None, :]) & is_live[:, None]
    ).astype(jnp.int32)
    slot_rank = jnp.sum(jnp.cumsum(owner_hit, axis=0) * owner_hit, axis=1) - 1
    place = jnp.where(is_live, owner_ids * CAP + slot_rank, PLACES)
    cell = OFF + (obs_cell // C + H) * CB + 8 + obs_cell % C

    outgoing, kap, act = smooth(flags, sweep_counts, cell, place, y, kappa, halos)
    buffer = lax.all_to_all(outgoing, "lon", split_axis=0, concat_axis=0, tiled=True)
    mixed = weigh(high, low, buffer)
    returned = lax.all_to_all(mixed, "lon", split_axis=0, concat_axis=0, tiled=True)
    field, pay_a, pay_b, own_a, own_b = spread(flags, cell, place, count, returned)
    lat_a, lat_b = swap(pay_a, pay_b, "lat")
    back = (lat_a, lat_b) + swap(*corner(flags, own_a, own_b, lat_a, lat_b), "lon")
    sketch, gram = finish(flags, field, kap, act, back, probes)
    cells_all = R * C * n_lat * n_lon
    r_factor = jnp.linalg.cholesky(sum_everywhere(gram) / cells_all, symmetrize_input=False).T
    return (sketch, r_factor)


def solution(mesh):
    return jax.shard_map(
        shards,
        mesh=mesh,
        in_specs=(
            P(None, "lat", "lon"),
            P("lat", "lon"),
            P("lat"),
            P(("lat", "lon")),
            P(("lat", "lon"), None),
            P("lat", "lon"),
            P("lat", "lon", None, None),
        ),
        out_specs=(P(None, "lat", "lon"), P()),
        check_vma=False,
    )
```

```python
import functools

import jax
import jax.numpy as jnp
from jax import lax
from jax.experimental import pallas as pl
from jax.experimental.pallas import tpu as pltpu
from jax.sharding import PartitionSpec as P

SWEEPS = 4
CAP = 48
K = 128
R = 32
C = 256
H = 4
RE = R + 2 * H
CB = C + 16
NROW = RE * CB
OFF = 8
SLOTS = 384
PLACES = 768
LANES = 128
VMEM_LIMIT = 30 * 1024 * 1024
LAT_ROWS = H * C + 16
OWN_ROWS = R * H + R
LON_OWNERS = 16
WEIGH_PARTS = 3


def vmem_spec():
    return pl.BlockSpec(memory_space=pltpu.VMEM)


def smem_spec():
    return pl.BlockSpec(memory_space=pltpu.SMEM)


def hbm_spec():
    return pl.BlockSpec(memory_space=pltpu.HBM)


def params():
    return pltpu.CompilerParams(vmem_limit_bytes=VMEM_LIMIT)


def f32(*shape):
    return jax.ShapeDtypeStruct(shape, jnp.float32)


def held(*shape):
    return pltpu.VMEM(shape, jnp.float32)


def in_vmem(*arrays):
    return tuple(pltpu.with_memory_space_constraint(a, pltpu.VMEM) for a in arrays)


def in_hbm(array):
    return pltpu.with_memory_space_constraint(array, pltpu.HBM)


def at(r, c):
    return OFF + r * CB + c


def edge_pack_kernel(flags, counts, kappa_ref, p_hbm, pay_a, pay_b, chunk, sems):
    odd = flags[0]
    first = (jnp.where(odd == 1, 0, R - H), jnp.where(odd == 1, R - H, 0))
    copies = []
    for side in range(2):
        block = pl.multiple_of(jnp.where(first[side] == 0, 0, R - 8), 8)
        for half in range(2):
            n = side * 2 + half
            copies.append(pltpu.make_async_copy(
                p_hbm.at[:, pl.ds(block, 8), pl.ds(half * LANES, LANES)], chunk.at[n], sems.at[n]))
            copies[-1].start()
    flat = chunk.reshape(4 * K * 8, LANES)
    for side, pay in ((0, pay_a), (1, pay_b)):
        within = jnp.where(first[side] == 0, 0, 8 - H)
        for r in range(H):
            for half in range(2):
                lanes = slice(half * LANES, (half + 1) * LANES)
                pay[H * C + 2 * r + half:H * C + 2 * r + half + 1, :] = jnp.where(
                    first[side] == 0, kappa_ref[r:r + 1, lanes], kappa_ref[R - H + r:R - H + r + 1, lanes])
            value = counts[first[side] + r].astype(jnp.float32)
            pay[H * C + 8 + r:H * C + 9 + r, :] = jnp.full((1, K), value, jnp.float32)
        pay[H * C + 8 + H:, :] = jnp.zeros((4, K), jnp.float32)
        for half in range(2):
            n = side * 2 + half
            copies[n].wait()
            for r in range(H):
                pay[r * C + half * LANES:r * C + (half + 1) * LANES, :] = flat[
                    pl.ds(n * K * 8 + within + r, K, stride=8), :].T


def edge_pack(flags, counts, kappa, probes):
    return pl.pallas_call(
        edge_pack_kernel,
        in_specs=[smem_spec(), smem_spec(), vmem_spec(), hbm_spec()],
        out_specs=[vmem_spec()] * 2,
        out_shape=[f32(LAT_ROWS, K)] * 2,
        scratch_shapes=[pltpu.VMEM((4, K, 8, LANES), jnp.float32), pltpu.SemaphoreType.DMA((4,))],
        compiler_params=pltpu.CompilerParams(vmem_limit_bytes=8 * 1024 * 1024),
        name="edge_pack",
    )(flags, counts, kappa, in_hbm(probes))


def turn_kernel(flags, kappa_ref, p_hbm, y_ref, own_a, own_b, chunk, sems):
    def copy(n):
        half, block = n // 4, n % 4
        return pltpu.make_async_copy(
            p_hbm.at[:, pl.ds(block * 8, 8), pl.ds(half * LANES, LANES)], chunk.at[n], sems.at[n])

    for n in range(8):
        copy(n).start()
    flat = chunk.reshape(8 * K * 8, LANES)
    for n in range(8):
        copy(n).wait()
        half, block = n // 4, n % 4
        for i in range(8):
            r = block * 8 + i
            y_ref[r, half * LANES:(half + 1) * LANES, :] = flat[pl.ds(n * K * 8 + i, K, stride=8), :].T
    odd = flags[2]
    for own, low in ((own_a, odd), (own_b, 1 - odd)):
        col = jnp.where(low == 1, 0, C - H)
        lane = pl.multiple_of(jnp.where(low == 1, 0, LANES), LANES)
        for r in range(R):
            own[r * H:(r + 1) * H, :] = y_ref[r, pl.ds(col, H), :]
        own[R * H:, :] = kappa_ref[:, pl.ds(lane, LANES)]


def turn(flags, kappa, probes):
    return pl.pallas_call(
        turn_kernel,
        in_specs=[smem_spec(), vmem_spec(), hbm_spec()],
        out_specs=[vmem_spec()] * 3,
        out_shape=[held(R, C, K), held(OWN_ROWS, K), held(OWN_ROWS, K)],
        scratch_shapes=[pltpu.VMEM((8, K, 8, LANES), jnp.float32), pltpu.SemaphoreType.DMA((8,))],
        compiler_params=pltpu.CompilerParams(vmem_limit_bytes=12 * 1024 * 1024),
        cost_estimate=pl.CostEstimate(flops=0, bytes_accessed=12 * 1024 * 1024, transcendentals=0),
        name="turn",
    )(flags, kappa, in_hbm(probes))


def corner_kernel(flags, own_a, own_b, lat_a, lat_b, pay_a, pay_b):
    odd = flags[2]
    own_rows = own_a.shape[0]
    for own, pay, low in ((own_a, pay_a, odd), (own_b, pay_b, 1 - odd)):
        col = jnp.where(low == 1, 0, C - H)
        pay[:own_rows, :] = own[...]
        base = own_rows
        for lat in (lat_a, lat_b):
            for r in range(H):
                pay[base:base + H, :] = lat[pl.ds(r * C + col, H), :]
                base += H
        if own_rows > R * H:
            for lat in (lat_a, lat_b):
                for r in range(H):
                    pay[base:base + 1, :] = lat[pl.ds(H * C + 2 * r + 1 - low, 1), :]
                    base += 1


def corner(flags, own_a, own_b, lat_a, lat_b):
    rows = own_a.shape[0] + 2 * H * H + (2 * H if own_a.shape[0] > R * H else 0)
    return pl.pallas_call(
        corner_kernel,
        in_specs=[smem_spec()] + [vmem_spec()] * 4,
        out_specs=[vmem_spec()] * 2,
        out_shape=[f32(rows, K)] * 2,
        compiler_params=pltpu.CompilerParams(vmem_limit_bytes=8 * 1024 * 1024),
        name="corner",
    )(flags, *in_vmem(own_a, own_b), lat_a, lat_b)


def put_halos(buf, flags, lat_a, lat_b, lon_a, lon_b):
    odd = flags[0]
    lon_odd = flags[2]
    lat_ok = (None, flags[1] == 1)
    lon_ok = (None, flags[3] == 1)
    lat_row = (jnp.where(odd == 1, 0, R + H), jnp.where(odd == 1, R + H, 0))
    lon_col = (jnp.where(lon_odd == 1, 0, C + H), jnp.where(lon_odd == 1, C + H, 0))

    def keep(ok, x):
        return x if ok is None else jnp.where(ok, x, 0.0)

    own_rows = lon_a.shape[0] - 2 * H * H
    own_rows = R * H if own_rows == R * H else OWN_ROWS
    for n, lat in ((0, lat_a), (1, lat_b)):
        for r in range(H):
            start = pl.multiple_of(OFF + (lat_row[n] + r) * CB + 8, 8)
            buf[pl.ds(start, C), :] = keep(lat_ok[n], lat[r * C:(r + 1) * C, :])
    for m, lon in ((0, lon_a), (1, lon_b)):
        for r in range(R):
            start = at(r + H, 4) + lon_col[m]
            buf[pl.ds(start, H), :] = keep(lon_ok[m], lon[r * H:(r + 1) * H, :])
        for n in range(2):
            for r in range(H):
                part = own_rows + (n * H + r) * H
                start = OFF + (lat_row[n] + r) * CB + 4 + lon_col[m]
                buf[pl.ds(start, H), :] = keep(lat_ok[n], keep(lon_ok[m], lon[part:part + H, :]))


def coeffs_kernel(flags, counts, kappa_ref, tail_a, tail_b, lon_a, lon_b, after, kap, act):
    odd = flags[0]
    lon_odd = flags[2]
    lat_ok = (None, flags[1] == 1)
    lat_row = (jnp.where(odd == 1, 0, R + H), jnp.where(odd == 1, R + H, 0))
    lon_col = (jnp.where(lon_odd == 1, 0, C + H), jnp.where(lon_odd == 1, C + H, 0))
    kap_t = kappa_ref[...].T
    for r in range(R):
        kap[pl.ds(at(r + H, 8), C), :] = jnp.broadcast_to(kap_t[:, r:r + 1], (C, K))
    for n, lat in ((0, tail_a), (1, tail_b)):
        turned = lat[:8, :].T
        if n == 1:
            turned = jnp.where(lat_ok[1], turned, 0.0)
        for r in range(H):
            for h in range(2):
                start = pl.multiple_of(OFF + (lat_row[n] + r) * CB + 8 + h * LANES, 8)
                kap[pl.ds(start, LANES), :] = jnp.broadcast_to(turned[:, 2 * r + h:2 * r + h + 1], (LANES, K))
        for r in range(H):
            wide = jnp.broadcast_to(lat[8 + r:9 + r, :], (8, K))
            for s in range(SWEEPS):
                act[s, lat_row[n] + r] = jnp.where(wide > s, 1.0, 0.0)
    for r in range(R):
        for s in range(SWEEPS):
            act[s, r + H] = jnp.full((8, K), jnp.where(counts[r] > s, 1.0, 0.0), jnp.float32)
    for m, lon in ((0, lon_a), (1, lon_b)):
        src = (jnp.where(lon_odd == 1, LANES - H, 0), jnp.where(lon_odd == 1, 0, LANES - H))[m]
        own = lon[R * H:R * H + R, :].T
        tail = lon[OWN_ROWS + 2 * H * H:, :].T
        low, high = own[:H, :], own[LANES - H:, :]
        edge = jnp.where(src == 0, low, high)
        tail = jnp.where(src == 0, tail[:H, :], tail[LANES - H:, :])
        if m == 1:
            edge = jnp.where(flags[3] == 1, edge, 0.0)
            tail = jnp.where(flags[3] == 1, tail, 0.0)
        for r in range(R):
            kap[pl.ds(at(r + H, 4) + lon_col[m], H), :] = jnp.broadcast_to(edge[:, r:r + 1], (H, K))
        for n in range(2):
            for r in range(H):
                part = jnp.broadcast_to(tail[:, n * H + r:n * H + r + 1], (H, K))
                if n == 1:
                    part = jnp.where(lat_ok[1], part, 0.0)
                kap[pl.ds(OFF + (lat_row[n] + r) * CB + 4 + lon_col[m], H), :] = part


def sweep(src, dst, kap, act, s):
    first = s + 1
    count = RE - 2 * first

    def body(i, _):
        r = first + 2 * i
        base = pl.multiple_of(r * CB, 8)
        a0 = act[s, r]
        a1 = act[s, r + 1]
        for t in range(CB // 8):
            o = base + OFF + t * 8
            up = src[pl.ds(o - CB, 8), :]
            c0 = src[pl.ds(o, 8), :]
            c1 = src[pl.ds(o + CB, 8), :]
            dn = src[pl.ds(o + 2 * CB, 8), :]
            l0 = src[pl.ds(o - 1, 8), :]
            r0 = src[pl.ds(o + 1, 8), :]
            l1 = src[pl.ds(o + CB - 1, 8), :]
            r1 = src[pl.ds(o + CB + 1, 8), :]
            lap0 = (up + c1) + (l0 + r0) - 4.0 * c0
            lap1 = (c0 + dn) + (l1 + r1) - 4.0 * c1
            dst[pl.ds(o, 8), :] = c0 + (a0 * kap[pl.ds(o, 8), :]) * lap0
            dst[pl.ds(o + CB, 8), :] = c1 + (a1 * kap[pl.ds(o + CB, 8), :]) * lap1
        return 0

    lax.fori_loop(0, count // 2, body, 0)


def coeffs(flags, counts, kappa, tail_a, tail_b, lon_a, lon_b, after):
    return pl.pallas_call(
        coeffs_kernel,
        in_specs=[smem_spec()] * 2 + [vmem_spec()] * 5 + [pl.BlockSpec(memory_space=pl.ANY)],
        out_specs=[vmem_spec()] * 2,
        out_shape=[held(NROW + 16, K), held(SWEEPS, RE, 8, K)],
        compiler_params=pltpu.CompilerParams(vmem_limit_bytes=8 * 1024 * 1024),
        cost_estimate=pl.CostEstimate(flops=0, bytes_accessed=4 * 1024 * 1024, transcendentals=0),
        name="coeffs",
    )(flags, counts, kappa, tail_a, tail_b, lon_a, lon_b, after)


def places_kernel(count_ref, cell_ref, owner_ref, row_ref, place_ref, seen):
    for i in range(LON_OWNERS):
        seen[i] = 0
    count = count_ref[0]

    def one(t, _):
        owner = owner_ref[0, t]
        rank = seen[owner]
        live = t < count
        seen[owner] = rank + jnp.where(live, 1, 0)
        place_ref[t] = jnp.where(live, owner * CAP + rank, PLACES)
        cell = cell_ref[t]
        row_ref[t] = OFF + 8 + H * CB + (cell >> 8) * CB + (cell & (C - 1))
        return 0

    lax.fori_loop(0, SLOTS, one, 0, unroll=8)


def places(count, cell, owner):
    return pl.pallas_call(
        places_kernel,
        in_specs=[smem_spec()] * 3,
        out_specs=[smem_spec()] * 2,
        out_shape=[jax.ShapeDtypeStruct((SLOTS,), jnp.int32)] * 2,
        scratch_shapes=[pltpu.SMEM((LON_OWNERS,), jnp.int32)],
        cost_estimate=pl.CostEstimate(flops=0, bytes_accessed=4 * 1024 * 1024, transcendentals=0),
        compiler_params=pltpu.CompilerParams(vmem_limit_bytes=1024 * 1024),
        name="places",
    )(count, cell, owner)


def smooth_kernel(flags, cell_ref, place_ref, y_ref, kap, act, lat_a, lat_b, lon_a, lon_b,
                  out_ref, tail_a, tail_b, buf_a, buf_b, rows_ref):
    for r in range(R):
        buf_a[pl.ds(at(r + H, 8), C), :] = y_ref[r]
    put_halos(buf_a, flags, lat_a, lat_b, lon_a, lon_b)
    tail_a[...] = lat_a[H * C:, :]
    tail_b[...] = lat_b[H * C:, :]
    bufs = (buf_a, buf_b)
    for s in range(SWEEPS):
        sweep(bufs[s % 2], bufs[(s + 1) % 2], kap, act, s)
    rows_ref[...] = jnp.zeros_like(rows_ref)

    def copy(i, _):
        for j in range(8):
            t = i * 8 + j
            rows_ref[pl.ds(place_ref[t], 1), :] = buf_a[pl.ds(cell_ref[t], 1), :]
        return 0

    lax.fori_loop(0, SLOTS // 8, copy, 0)
    out_ref[...] = rows_ref[:PLACES]


def smooth(flags, cell, place, y, kap, act, halos):
    return pl.pallas_call(
        smooth_kernel,
        in_specs=[smem_spec()] * 3 + [vmem_spec()] * 7,
        out_specs=[vmem_spec()] * 3,
        out_shape=[f32(PLACES, K), f32(16, K), f32(16, K)],
        scratch_shapes=[
            pltpu.VMEM((NROW + 16, K), jnp.float32),
            pltpu.VMEM((NROW + 16, K), jnp.float32),
            pltpu.VMEM((PLACES + 8, K), jnp.float32),
        ],
        compiler_params=params(),
        name="smooth",
    )(flags, cell, place, *in_vmem(y, kap, act), *halos)


def weigh_kernel(b_ref, r_hbm, out_ref, r_ref, sems):
    width = PLACES // WEIGH_PARTS

    def copy(n):
        return pltpu.make_async_copy(r_hbm.at[:, pl.ds(n * width, width)], r_ref.at[n], sems.at[n])

    for n in range(WEIGH_PARTS):
        copy(n).start()
    b = b_ref[...].T
    high = b.astype(jnp.bfloat16)
    low = (b - high.astype(jnp.float32)).astype(jnp.bfloat16)
    both = jnp.concatenate([high, low], axis=0)
    for n in range(WEIGH_PARTS):
        copy(n).wait()
        r = r_ref[n]
        r_high = r.astype(jnp.bfloat16)
        r_low = (r - r_high.astype(jnp.float32)).astype(jnp.bfloat16)
        one = jnp.dot(both, r_high, preferred_element_type=jnp.float32)
        two = jnp.dot(high, r_low, preferred_element_type=jnp.float32)
        out_ref[n * width:(n + 1) * width, :] = (one[:K] + (one[K:] + two)).T


def weigh(buffer, r):
    return pl.pallas_call(
        weigh_kernel,
        in_specs=[vmem_spec(), hbm_spec()],
        out_specs=vmem_spec(),
        out_shape=f32(PLACES, K),
        scratch_shapes=[
            pltpu.VMEM((WEIGH_PARTS, PLACES, PLACES // WEIGH_PARTS), jnp.float32),
            pltpu.SemaphoreType.DMA((WEIGH_PARTS,)),
        ],
        compiler_params=pltpu.CompilerParams(vmem_limit_bytes=12 * 1024 * 1024),
        name="weigh",
    )(buffer, in_hbm(r))


def spread_kernel(flags, cell_ref, place_ref, count_ref, ret_ref, field, pay_a, pay_b, own_a, own_b):
    field[...] = jnp.zeros_like(field)

    def add(t, _):
        i = pl.ds(cell_ref[t], 1)
        field[i, :] = field[i, :] + ret_ref[pl.ds(place_ref[t], 1), :]
        return 0

    lax.fori_loop(0, count_ref[0], add, 0)
    odd = flags[0]
    lon_odd = flags[2]
    for pay, low in ((pay_a, odd), (pay_b, 1 - odd)):
        first = jnp.where(low == 1, H, R)
        for r in range(H):
            start = pl.multiple_of(OFF + (first + r) * CB + 8, 8)
            pay[r * C:(r + 1) * C, :] = field[pl.ds(start, C), :]
    for own, low in ((own_a, lon_odd), (own_b, 1 - lon_odd)):
        col = jnp.where(low == 1, 8, 4 + C)
        for r in range(R):
            own[r * H:(r + 1) * H, :] = field[pl.ds(at(r + H, 0) + col, H), :]


def spread(flags, cell, place, count, returned):
    return pl.pallas_call(
        spread_kernel,
        in_specs=[smem_spec()] * 4 + [vmem_spec()],
        out_specs=[vmem_spec()] * 5,
        out_shape=[held(NROW + 16, K), f32(H * C, K), f32(H * C, K), held(R * H, K), held(R * H, K)],
        compiler_params=pltpu.CompilerParams(vmem_limit_bytes=10 * 1024 * 1024),
        name="spread",
    )(flags, cell, place, count, returned)


def finish_kernel(flags, field, kap, act, lat_a, lat_b, lon_a, lon_b, p_hbm, out_hbm, gram_ref,
                  buf_a, buf_b, chunk, in_sems, out_sems):
    def part(ref, n):
        half, block = n // 4, n % 4
        return ref.at[:, pl.ds(block * 8, 8), pl.ds(half * LANES, LANES)]

    def copy_in(n):
        return pltpu.make_async_copy(part(p_hbm, n), chunk.at[n], in_sems.at[n])

    def copy_out(n):
        return pltpu.make_async_copy(chunk.at[n], part(out_hbm, n), out_sems.at[n])

    for n in range(8):
        copy_in(n).start()
    buf_a[...] = field[...]
    put_halos(buf_a, flags, lat_a, lat_b, lon_a, lon_b)
    bufs = (buf_a, buf_b)
    for s in range(SWEEPS):
        sweep(bufs[s % 2], bufs[(s + 1) % 2], kap, act, s)
    flat = chunk.reshape(8 * K * 8, LANES)
    contract = (((1,), (1,)), ((), ()))
    hh = jnp.zeros((K, K), jnp.float32)
    hl = jnp.zeros((K, K), jnp.float32)
    for n in range(8):
        half, block = n // 4, n % 4
        copy_in(n).wait()
        for i in range(0, 8, 2):
            parts = []
            for j in range(2):
                where = pl.ds(n * K * 8 + i + j, K, stride=8)
                start = at(block * 8 + i + j + H, 8) + half * LANES
                sk = flat[where, :] + buf_a[pl.ds(start, LANES), :].T
                flat[where, :] = sk
                parts.append(sk)
            sk = jnp.concatenate(parts, axis=1)
            high = sk.astype(jnp.bfloat16)
            low = (sk - high.astype(jnp.float32)).astype(jnp.bfloat16)
            hh = hh + lax.dot_general(high, high, contract, preferred_element_type=jnp.float32)
            hl = hl + lax.dot_general(high, low, contract, preferred_element_type=jnp.float32)
        copy_out(n).start()
    gram_ref[...] = hh + (hl + hl.T)
    for n in range(8):
        copy_out(n).wait()


def finish(flags, field, kap, act, halos, probes):
    return pl.pallas_call(
        finish_kernel,
        in_specs=[smem_spec()] + [vmem_spec()] * 7 + [hbm_spec()],
        out_specs=[hbm_spec(), vmem_spec()],
        out_shape=[f32(K, R, C), f32(K, K)],
        scratch_shapes=[
            pltpu.VMEM((NROW + 16, K), jnp.float32),
            pltpu.VMEM((NROW + 16, K), jnp.float32),
            pltpu.VMEM((8, K, 8, LANES), jnp.float32),
            pltpu.SemaphoreType.DMA((8,)),
            pltpu.SemaphoreType.DMA((8,)),
        ],
        compiler_params=params(),
        name="finish",
    )(flags, *in_vmem(field, kap, act), *halos, in_hbm(probes))


def pairs(size, first):
    return [(i, (i + 1) % size if (i - first) % 2 == 0 else (i - 1) % size) for i in range(size)]


def swap(a, b, axis):
    size = lax.axis_size(axis)
    return lax.ppermute(a, axis, pairs(size, 0)), lax.ppermute(b, axis, pairs(size, 1))


def sum_everywhere(x):
    n_lat, n_lon = lax.axis_size("lat"), lax.axis_size("lon")

    def stage(x, axis, perms):
        got = [lax.ppermute(x, axis, p) for p in perms]
        for g in got:
            x = x + g
        return x

    x = stage(x, "lat", [[(i, i ^ 1) for i in range(n_lat)]])
    x = stage(x, "lat", [[(i, i ^ (2 * d)) for i in range(n_lat)] for d in (1, 2, 3)])
    x = stage(x, "lon", [[(i, i ^ d) for i in range(n_lon)] for d in (1, 2, 3)])
    return stage(x, "lon", [[(i, i ^ (4 * d)) for i in range(n_lon)] for d in (1, 2, 3)])


def shards(probes, kappa, sweep_counts, obs_cell, obs_owner, obs_count, r_inv):
    n_lat, n_lon = lax.axis_size("lat"), lax.axis_size("lon")
    lat, lon = lax.axis_index("lat"), lax.axis_index("lon")
    flags = jnp.stack([
        lat % 2, ((lat > 0) & (lat < n_lat - 1)).astype(jnp.int32),
        lon % 2, ((lon > 0) & (lon < n_lon - 1)).astype(jnp.int32),
    ]).astype(jnp.int32)
    lat_a, lat_b = swap(*edge_pack(flags, sweep_counts, kappa, probes), "lat")
    y, own_a, own_b = turn(flags, kappa, probes)
    count = obs_count.reshape(1)
    cell, place = places(count, obs_cell, obs_owner.reshape(1, SLOTS))
    lon_a, lon_b = swap(*corner(flags, own_a, own_b, lat_a, lat_b), "lon")
    kap, act = coeffs(flags, sweep_counts, kappa, lat_a[H * C:], lat_b[H * C:], lon_a, lon_b, count)
    outgoing, tail_a, tail_b = smooth(flags, cell, place, y, kap, act, (lat_a, lat_b, lon_a, lon_b))
    buffer = lax.all_to_all(outgoing, "lon", split_axis=0, concat_axis=0, tiled=True)
    mixed = weigh(buffer, r_inv[0, 0])
    returned = lax.all_to_all(mixed, "lon", split_axis=0, concat_axis=0, tiled=True)
    field, pay_a, pay_b, own_a, own_b = spread(flags, cell, place, count, returned)
    kap, act = coeffs(flags, sweep_counts, kappa, tail_a, tail_b, lon_a, lon_b, pay_a)
    lat_a, lat_b = swap(pay_a, pay_b, "lat")
    back = (lat_a, lat_b) + swap(*corner(flags, own_a, own_b, lat_a, lat_b), "lon")
    sketch, gram = finish(flags, field, kap, act, back, probes)
    cells_all = R * C * n_lat * n_lon
    r_factor = jnp.linalg.cholesky(sum_everywhere(gram) / cells_all, symmetrize_input=False).T
    return (sketch, r_factor)


def solution(mesh):
    return jax.shard_map(
        shards,
        mesh=mesh,
        in_specs=(
            P(None, "lat", "lon"),
            P("lat", "lon"),
            P("lat"),
            P(("lat", "lon")),
            P(("lat", "lon"), None),
            P("lat", "lon"),
            P("lat", "lon", None, None),
        ),
        out_specs=(P(None, "lat", "lon"), P()),
        check_vma=False,
    )
```

```python
import functools

import jax
import jax.numpy as jnp
from jax import lax
from jax.experimental import pallas as pl
from jax.experimental.pallas import tpu as pltpu
from jax.sharding import PartitionSpec as P

SWEEPS = 4
CAP = 48
K = 128
R = 32
C = 256
H = 4
RE = R + 2 * H
CB = C + 16
NROW = RE * CB
OFF = 8
SLOTS = 384
PLACES = 768
LANES = 128
VMEM_LIMIT = 30 * 1024 * 1024
LAT_ROWS = H * C + 16
OWN_ROWS = R * H + R
LON_OWNERS = 16
WEIGH_PARTS = 3
HALF = 64
EXACT = False


def vmem_spec():
    return pl.BlockSpec(memory_space=pltpu.VMEM)


def smem_spec():
    return pl.BlockSpec(memory_space=pltpu.SMEM)


def hbm_spec():
    return pl.BlockSpec(memory_space=pltpu.HBM)


def params():
    return pltpu.CompilerParams(vmem_limit_bytes=VMEM_LIMIT)


def f32(*shape):
    return jax.ShapeDtypeStruct(shape, jnp.float32)


def held(*shape):
    return pltpu.VMEM(shape, jnp.float32)


def in_vmem(*arrays):
    return tuple(pltpu.with_memory_space_constraint(a, pltpu.VMEM) for a in arrays)


def in_hbm(array):
    return pltpu.with_memory_space_constraint(array, pltpu.HBM)


def at(r, c):
    return OFF + r * CB + c


def edge_pack_kernel(counts_hbm, kappa_hbm, p_hbm, pay_a, pay_b, chunk, kappa_ref, counts, sems):
    odd = lax.axis_index("lat") % 2
    first = (jnp.where(odd == 1, 0, R - H), jnp.where(odd == 1, R - H, 0))
    copies = []
    for side in range(2):
        block = pl.multiple_of(jnp.where(first[side] == 0, 0, R - 8), 8)
        for half in range(2):
            n = side * 2 + half
            copies.append(pltpu.make_async_copy(
                p_hbm.at[:, pl.ds(block, 8), pl.ds(half * LANES, LANES)], chunk.at[n], sems.at[n]))
    small = [pltpu.make_async_copy(kappa_hbm, kappa_ref, sems.at[4]),
             pltpu.make_async_copy(counts_hbm, counts, sems.at[5])]
    for copy in small + copies:
        copy.start()
    for copy in small:
        copy.wait()
    flat = chunk.reshape(4 * K * 8, LANES)
    for side, pay in ((0, pay_a), (1, pay_b)):
        within = jnp.where(first[side] == 0, 0, 8 - H)
        for r in range(H):
            for half in range(2):
                lanes = slice(half * LANES, (half + 1) * LANES)
                pay[H * C + 2 * r + half:H * C + 2 * r + half + 1, :] = jnp.where(
                    first[side] == 0, kappa_ref[r:r + 1, lanes], kappa_ref[R - H + r:R - H + r + 1, lanes])
            value = counts[first[side] + r].astype(jnp.float32)
            pay[H * C + 8 + r:H * C + 9 + r, :] = jnp.full((1, K), value, jnp.float32)
        pay[H * C + 8 + H:, :] = jnp.zeros((4, K), jnp.float32)
        for half in range(2):
            n = side * 2 + half
            copies[n].wait()
            for r in range(H):
                pay[r * C + half * LANES:r * C + (half + 1) * LANES, :] = flat[
                    pl.ds(n * K * 8 + within + r, K, stride=8), :].T


def edge_pack(counts, kappa, probes):
    return pl.pallas_call(
        edge_pack_kernel,
        in_specs=[hbm_spec()] * 3,
        out_specs=[vmem_spec()] * 2,
        out_shape=[f32(LAT_ROWS, K)] * 2,
        scratch_shapes=[
            pltpu.VMEM((4, K, 8, LANES), jnp.float32),
            pltpu.VMEM((R, C), jnp.float32),
            pltpu.SMEM((R,), jnp.int32),
            pltpu.SemaphoreType.DMA((6,)),
        ],
        compiler_params=pltpu.CompilerParams(vmem_limit_bytes=8 * 1024 * 1024),
        name="edge_pack",
    )(in_hbm(counts), in_hbm(kappa), in_hbm(probes))


def turn_kernel(flags, kappa_ref, p_hbm, y_ref, own_a, own_b, chunk, sems):
    def copy(n):
        half, block = n // 4, n % 4
        return pltpu.make_async_copy(
            p_hbm.at[:, pl.ds(block * 8, 8), pl.ds(half * LANES, LANES)], chunk.at[n], sems.at[n])

    for n in range(8):
        copy(n).start()
    flat = chunk.reshape(8 * K * 8, LANES)
    for n in range(8):
        copy(n).wait()
        half, block = n // 4, n % 4
        for i in range(8):
            r = block * 8 + i
            y_ref[r, half * LANES:(half + 1) * LANES, :] = flat[pl.ds(n * K * 8 + i, K, stride=8), :].T
    odd = flags[2]
    for own, low in ((own_a, odd), (own_b, 1 - odd)):
        col = jnp.where(low == 1, 0, C - H)
        lane = pl.multiple_of(jnp.where(low == 1, 0, LANES), LANES)
        for r in range(R):
            own[r * H:(r + 1) * H, :] = y_ref[r, pl.ds(col, H), :]
        own[R * H:, :] = kappa_ref[:, pl.ds(lane, LANES)]


def turn(flags, kappa, probes):
    return pl.pallas_call(
        turn_kernel,
        in_specs=[smem_spec(), vmem_spec(), hbm_spec()],
        out_specs=[vmem_spec()] * 3,
        out_shape=[held(R, C, K), held(OWN_ROWS, K), held(OWN_ROWS, K)],
        scratch_shapes=[pltpu.VMEM((8, K, 8, LANES), jnp.float32), pltpu.SemaphoreType.DMA((8,))],
        compiler_params=pltpu.CompilerParams(vmem_limit_bytes=12 * 1024 * 1024),
        cost_estimate=pl.CostEstimate(flops=0, bytes_accessed=12 * 1024 * 1024, transcendentals=0),
        name="turn",
    )(flags, kappa, in_hbm(probes))


def corner_kernel(flags, own_a, own_b, lat_a, lat_b, after, pay_a, pay_b):
    odd = flags[2]
    own_rows = own_a.shape[0]
    for own, pay, low in ((own_a, pay_a, odd), (own_b, pay_b, 1 - odd)):
        col = jnp.where(low == 1, 0, C - H)
        pay[:own_rows, :] = own[...]
        base = own_rows
        for lat in (lat_a, lat_b):
            for r in range(H):
                pay[base:base + H, :] = lat[pl.ds(r * C + col, H), :]
                base += H
        if own_rows > R * H:
            for lat in (lat_a, lat_b):
                for r in range(H):
                    pay[base:base + 1, :] = lat[pl.ds(H * C + 2 * r + 1 - low, 1), :]
                    base += 1


def corner(flags, own_a, own_b, lat_a, lat_b, after):
    rows = own_a.shape[0] + 2 * H * H + (2 * H if own_a.shape[0] > R * H else 0)
    return pl.pallas_call(
        corner_kernel,
        in_specs=[smem_spec()] + [vmem_spec()] * 4 + [pl.BlockSpec(memory_space=pl.ANY)],
        out_specs=[vmem_spec()] * 2,
        out_shape=[f32(rows, K)] * 2,
        compiler_params=pltpu.CompilerParams(vmem_limit_bytes=8 * 1024 * 1024),
        name="corner",
    )(flags, *in_vmem(own_a, own_b), lat_a, lat_b, after)


def put_halos(buf, flags, lat_a, lat_b, lon_a, lon_b):
    odd = flags[0]
    lon_odd = flags[2]
    lat_ok = (None, flags[1] == 1)
    lon_ok = (None, flags[3] == 1)
    lat_row = (jnp.where(odd == 1, 0, R + H), jnp.where(odd == 1, R + H, 0))
    lon_col = (jnp.where(lon_odd == 1, 0, C + H), jnp.where(lon_odd == 1, C + H, 0))

    def keep(ok, x):
        return x if ok is None else jnp.where(ok, x, 0.0)

    own_rows = lon_a.shape[0] - 2 * H * H
    own_rows = R * H if own_rows == R * H else OWN_ROWS
    for n, lat in ((0, lat_a), (1, lat_b)):
        for r in range(H):
            start = pl.multiple_of(OFF + (lat_row[n] + r) * CB + 8, 8)
            buf[pl.ds(start, C), :] = keep(lat_ok[n], lat[r * C:(r + 1) * C, :])
    for m, lon in ((0, lon_a), (1, lon_b)):
        for r in range(R):
            start = at(r + H, 4) + lon_col[m]
            buf[pl.ds(start, H), :] = keep(lon_ok[m], lon[r * H:(r + 1) * H, :])
        for n in range(2):
            for r in range(H):
                part = own_rows + (n * H + r) * H
                start = OFF + (lat_row[n] + r) * CB + 4 + lon_col[m]
                buf[pl.ds(start, H), :] = keep(lat_ok[n], keep(lon_ok[m], lon[part:part + H, :]))


def coeffs_kernel(flags, counts, kappa_ref, tail_a, tail_b, after, *rest):
    *lon, kap, act = rest
    odd = flags[0]
    lat_ok = (None, flags[1] == 1)
    lat_row = (jnp.where(odd == 1, 0, R + H), jnp.where(odd == 1, R + H, 0))
    kap_t = kappa_ref[...].T
    for r in range(R):
        kap[pl.ds(at(r + H, 8), C), :] = jnp.broadcast_to(kap_t[:, r:r + 1], (C, K))
    for n, lat in ((0, tail_a), (1, tail_b)):
        turned = lat[:8, :].T
        if n == 1:
            turned = jnp.where(lat_ok[1], turned, 0.0)
        for r in range(H):
            for h in range(2):
                start = pl.multiple_of(OFF + (lat_row[n] + r) * CB + 8 + h * LANES, 8)
                kap[pl.ds(start, LANES), :] = jnp.broadcast_to(turned[:, 2 * r + h:2 * r + h + 1], (LANES, K))
        for r in range(H):
            wide = jnp.broadcast_to(lat[8 + r:9 + r, :], (8, K))
            for s in range(SWEEPS):
                act[s, lat_row[n] + r] = jnp.where(wide > s, 1.0, 0.0)
    for r in range(R):
        for s in range(SWEEPS):
            act[s, r + H] = jnp.full((8, K), jnp.where(counts[r] > s, 1.0, 0.0), jnp.float32)
    if lon:
        put_lon_kappa(kap, flags, *lon)


def put_lon_kappa(kap, flags, lon_a, lon_b):
    odd = flags[0]
    lon_odd = flags[2]
    lat_ok = (None, flags[1] == 1)
    lat_row = (jnp.where(odd == 1, 0, R + H), jnp.where(odd == 1, R + H, 0))
    lon_col = (jnp.where(lon_odd == 1, 0, C + H), jnp.where(lon_odd == 1, C + H, 0))
    for m, lon in ((0, lon_a), (1, lon_b)):
        src = (jnp.where(lon_odd == 1, LANES - H, 0), jnp.where(lon_odd == 1, 0, LANES - H))[m]
        own = lon[R * H:R * H + R, :].T
        tail = lon[OWN_ROWS + 2 * H * H:, :].T
        low, high = own[:H, :], own[LANES - H:, :]
        edge = jnp.where(src == 0, low, high)
        tail = jnp.where(src == 0, tail[:H, :], tail[LANES - H:, :])
        if m == 1:
            edge = jnp.where(flags[3] == 1, edge, 0.0)
            tail = jnp.where(flags[3] == 1, tail, 0.0)
        for r in range(R):
            kap[pl.ds(at(r + H, 4) + lon_col[m], H), :] = jnp.broadcast_to(edge[:, r:r + 1], (H, K))
        for n in range(2):
            for r in range(H):
                part = jnp.broadcast_to(tail[:, n * H + r:n * H + r + 1], (H, K))
                if n == 1:
                    part = jnp.where(lat_ok[1], part, 0.0)
                kap[pl.ds(OFF + (lat_row[n] + r) * CB + 4 + lon_col[m], H), :] = part


def sweep(src, dst, kap, act, s):
    first = s + 1
    count = RE - 2 * first

    def body(i, _):
        r = first + 2 * i
        base = pl.multiple_of(r * CB, 8)
        a0 = act[s, r]
        a1 = act[s, r + 1]
        for t in range(CB // 8):
            o = base + OFF + t * 8
            up = src[pl.ds(o - CB, 8), :]
            c0 = src[pl.ds(o, 8), :]
            c1 = src[pl.ds(o + CB, 8), :]
            dn = src[pl.ds(o + 2 * CB, 8), :]
            l0 = src[pl.ds(o - 1, 8), :]
            r0 = src[pl.ds(o + 1, 8), :]
            l1 = src[pl.ds(o + CB - 1, 8), :]
            r1 = src[pl.ds(o + CB + 1, 8), :]
            lap0 = (up + c1) + (l0 + r0) - 4.0 * c0
            lap1 = (c0 + dn) + (l1 + r1) - 4.0 * c1
            dst[pl.ds(o, 8), :] = c0 + (a0 * kap[pl.ds(o, 8), :]) * lap0
            dst[pl.ds(o + CB, 8), :] = c1 + (a1 * kap[pl.ds(o + CB, 8), :]) * lap1
        return 0

    lax.fori_loop(0, count // 2, body, 0)


def coeffs(flags, counts, kappa, tail_a, tail_b, after, *lon):
    return pl.pallas_call(
        coeffs_kernel,
        in_specs=[smem_spec()] * 2 + [vmem_spec()] * 3 + [pl.BlockSpec(memory_space=pl.ANY)] + [vmem_spec()] * len(lon),
        out_specs=[vmem_spec()] * 2,
        out_shape=[held(NROW + 16, K), held(SWEEPS, RE, 8, K)],
        compiler_params=pltpu.CompilerParams(vmem_limit_bytes=8 * 1024 * 1024),
        cost_estimate=pl.CostEstimate(flops=0, bytes_accessed=4 * 1024 * 1024, transcendentals=0),
        name="coeffs",
    )(flags, counts, kappa, tail_a, tail_b, after, *lon)


def places_kernel(count_ref, cell_ref, owner_ref, row_ref, place_ref, seen):
    for i in range(LON_OWNERS):
        seen[i] = 0
    count = count_ref[0]

    def one(t, _):
        owner = owner_ref[0, t]
        rank = seen[owner]
        live = t < count
        seen[owner] = rank + jnp.where(live, 1, 0)
        place_ref[t] = jnp.where(live, owner * CAP + rank, PLACES)
        cell = cell_ref[t]
        row_ref[t] = OFF + 8 + H * CB + (cell >> 8) * CB + (cell & (C - 1))
        return 0

    lax.fori_loop(0, SLOTS, one, 0, unroll=8)


def places(count, cell, owner):
    return pl.pallas_call(
        places_kernel,
        in_specs=[smem_spec()] * 3,
        out_specs=[smem_spec()] * 2,
        out_shape=[jax.ShapeDtypeStruct((SLOTS,), jnp.int32)] * 2,
        scratch_shapes=[pltpu.SMEM((LON_OWNERS,), jnp.int32)],
        cost_estimate=pl.CostEstimate(flops=0, bytes_accessed=4 * 1024 * 1024, transcendentals=0),
        compiler_params=pltpu.CompilerParams(vmem_limit_bytes=1024 * 1024),
        name="places",
    )(count, cell, owner)


def smooth_kernel(flags, cell_ref, place_ref, y_ref, kap_in, act, lat_a, lat_b, lon_a, lon_b,
                  out_ref, tail_a, tail_b, kap, buf_a, buf_b, rows_ref):
    put_lon_kappa(kap, flags, lon_a, lon_b)
    for r in range(R):
        buf_a[pl.ds(at(r + H, 8), C), :] = y_ref[r]
    put_halos(buf_a, flags, lat_a, lat_b, lon_a, lon_b)
    tail_a[...] = lat_a[H * C:, :]
    tail_b[...] = lat_b[H * C:, :]
    bufs = (buf_a, buf_b)
    for s in range(SWEEPS):
        sweep(bufs[s % 2], bufs[(s + 1) % 2], kap, act, s)
    rows_ref[...] = jnp.zeros_like(rows_ref)

    def copy(i, _):
        for j in range(8):
            t = i * 8 + j
            rows_ref[pl.ds(place_ref[t], 1), :] = buf_a[pl.ds(cell_ref[t], 1), :]
        return 0

    lax.fori_loop(0, SLOTS // 8, copy, 0)
    out_ref[...] = rows_ref[:PLACES]


def smooth(flags, cell, place, y, kap, act, halos):
    return pl.pallas_call(
        smooth_kernel,
        in_specs=[smem_spec()] * 3 + [vmem_spec()] * 7,
        out_specs=[vmem_spec()] * 4,
        out_shape=[f32(PLACES, K), f32(16, K), f32(16, K), held(NROW + 16, K)],
        input_output_aliases={4: 3},
        scratch_shapes=[
            pltpu.VMEM((NROW + 16, K), jnp.float32),
            pltpu.VMEM((NROW + 16, K), jnp.float32),
            pltpu.VMEM((PLACES + 8, K), jnp.float32),
        ],
        compiler_params=params(),
        name="smooth",
    )(flags, cell, place, *in_vmem(y, kap, act), *halos)


def weigh_kernel(b_ref, r_hbm, out_ref, r_ref, sems):
    width = PLACES // WEIGH_PARTS

    def copy(n):
        return pltpu.make_async_copy(r_hbm.at[:, pl.ds(n * width, width)], r_ref.at[n], sems.at[n])

    for n in range(WEIGH_PARTS):
        copy(n).start()
    b = b_ref[...].T
    high = b.astype(jnp.bfloat16)
    low = (b - high.astype(jnp.float32)).astype(jnp.bfloat16)
    both = jnp.concatenate([high, low], axis=0)
    for n in range(WEIGH_PARTS):
        copy(n).wait()
        r = r_ref[n]
        r_high = r.astype(jnp.bfloat16)
        r_low = (r - r_high.astype(jnp.float32)).astype(jnp.bfloat16)
        one = jnp.dot(both, r_high, preferred_element_type=jnp.float32)
        two = jnp.dot(high, r_low, preferred_element_type=jnp.float32)
        out_ref[n * width:(n + 1) * width, :] = (one[:K] + (one[K:] + two)).T


def weigh(buffer, r):
    return pl.pallas_call(
        weigh_kernel,
        in_specs=[vmem_spec(), hbm_spec()],
        out_specs=vmem_spec(),
        out_shape=f32(PLACES, K),
        scratch_shapes=[
            pltpu.VMEM((WEIGH_PARTS, PLACES, PLACES // WEIGH_PARTS), jnp.float32),
            pltpu.SemaphoreType.DMA((WEIGH_PARTS,)),
        ],
        compiler_params=pltpu.CompilerParams(vmem_limit_bytes=12 * 1024 * 1024),
        name="weigh",
    )(buffer, in_hbm(r))


def spread_kernel(flags, cell_ref, place_ref, count_ref, ret_ref, field, pay_a, pay_b, own_a, own_b):
    field[...] = jnp.zeros_like(field)

    def add(t, _):
        i = pl.ds(cell_ref[t], 1)
        field[i, :] = field[i, :] + ret_ref[pl.ds(place_ref[t], 1), :]
        return 0

    lax.fori_loop(0, count_ref[0], add, 0)
    odd = flags[0]
    lon_odd = flags[2]
    for pay, low in ((pay_a, odd), (pay_b, 1 - odd)):
        first = jnp.where(low == 1, H, R)
        for r in range(H):
            start = pl.multiple_of(OFF + (first + r) * CB + 8, 8)
            pay[r * C:(r + 1) * C, :] = field[pl.ds(start, C), :]
    for own, low in ((own_a, lon_odd), (own_b, 1 - lon_odd)):
        col = jnp.where(low == 1, 8, 4 + C)
        for r in range(R):
            own[r * H:(r + 1) * H, :] = field[pl.ds(at(r + H, 0) + col, H), :]


def spread(flags, cell, place, count, returned):
    return pl.pallas_call(
        spread_kernel,
        in_specs=[smem_spec()] * 4 + [vmem_spec()],
        out_specs=[vmem_spec()] * 5,
        out_shape=[held(NROW + 16, K), f32(H * C, K), f32(H * C, K), held(R * H, K), held(R * H, K)],
        compiler_params=pltpu.CompilerParams(vmem_limit_bytes=10 * 1024 * 1024),
        name="spread",
    )(flags, cell, place, count, returned)


def finish_kernel(flags, field, kap, act, lat_a, lat_b, lon_a, lon_b, p_hbm, out_hbm, gram_ref,
                  buf_a, buf_b, chunk, in_sems, out_sems):
    def part(ref, n):
        half, block = n // 4, n % 4
        return ref.at[:, pl.ds(block * 8, 8), pl.ds(half * LANES, LANES)]

    def copy_in(n):
        return pltpu.make_async_copy(part(p_hbm, n), chunk.at[n], in_sems.at[n])

    def copy_out(n):
        return pltpu.make_async_copy(chunk.at[n], part(out_hbm, n), out_sems.at[n])

    for n in range(8):
        copy_in(n).start()
    buf_a[...] = field[...]
    put_halos(buf_a, flags, lat_a, lat_b, lon_a, lon_b)
    bufs = (buf_a, buf_b)
    for s in range(SWEEPS):
        sweep(bufs[s % 2], bufs[(s + 1) % 2], kap, act, s)
    flat = chunk.reshape(8 * K * 8, LANES)
    contract = (((1,), (1,)), ((), ()))
    hh = jnp.zeros((K, K), jnp.float32)
    hl = jnp.zeros((K, K), jnp.float32)
    for n in range(8):
        half, block = n // 4, n % 4
        copy_in(n).wait()
        for i in range(0, 8, 2):
            parts = []
            for j in range(2):
                where = pl.ds(n * K * 8 + i + j, K, stride=8)
                start = at(block * 8 + i + j + H, 8) + half * LANES
                sk = flat[where, :] + buf_a[pl.ds(start, LANES), :].T
                flat[where, :] = sk
                parts.append(sk)
            sk = jnp.concatenate(parts, axis=1)
            high = sk.astype(jnp.bfloat16)
            low = (sk - high.astype(jnp.float32)).astype(jnp.bfloat16)
            hh = hh + lax.dot_general(high, high, contract, preferred_element_type=jnp.float32)
            hl = hl + lax.dot_general(high, low, contract, preferred_element_type=jnp.float32)
        copy_out(n).start()
    gram = hh + (hl + hl.T)
    top = gram[:HALF]
    turned = pltpu.roll(gram[HALF:], HALF, 1)
    row = lax.broadcasted_iota(jnp.int32, (HALF, K), 0)
    lane = lax.broadcasted_iota(jnp.int32, (HALF, K), 1)
    gram_ref[:HALF, :] = jnp.where((lane < HALF) & (row > lane), turned, top)
    gram_ref[HALF:, :] = jnp.broadcast_to(jnp.sum(jnp.where(row == lane, turned, 0.0), axis=0, keepdims=True), (8, K))
    for n in range(8):
        copy_out(n).wait()


def finish(flags, field, kap, act, halos, probes):
    return pl.pallas_call(
        finish_kernel,
        in_specs=[smem_spec()] + [vmem_spec()] * 7 + [hbm_spec()],
        out_specs=[hbm_spec(), vmem_spec()],
        out_shape=[f32(K, R, C), f32(HALF + 8, K)],
        scratch_shapes=[
            pltpu.VMEM((NROW + 16, K), jnp.float32),
            pltpu.VMEM((NROW + 16, K), jnp.float32),
            pltpu.VMEM((8, K, 8, LANES), jnp.float32),
            pltpu.SemaphoreType.DMA((8,)),
            pltpu.SemaphoreType.DMA((8,)),
        ],
        compiler_params=params(),
        name="finish",
    )(flags, *in_vmem(field, kap, act), *halos, in_hbm(probes))


def pairs(size, first):
    return [(i, (i + 1) % size if (i - first) % 2 == 0 else (i - 1) % size) for i in range(size)]


def swap(a, b, axis):
    size = lax.axis_size(axis)
    return lax.ppermute(a, axis, pairs(size, 0)), lax.ppermute(b, axis, pairs(size, 1))


def factor_kernel(scale, x_ref, g1_ref, g2_ref, g3_ref, out_ref, a_ref):
    total = ((x_ref[...] + g1_ref[...]) + (g2_ref[...] + g3_ref[...])) * scale
    top = total[:HALF]
    a_ref[:HALF, :] = top
    lower = top.T[:HALF]
    row = lax.broadcasted_iota(jnp.int32, (HALF, HALF), 0)
    lane = lax.broadcasted_iota(jnp.int32, (HALF, HALF), 1)
    lower = jnp.where(row == lane, jnp.broadcast_to(total[HALF:HALF + 1, :HALF], (HALF, HALF)), lower)
    a_ref[HALF:, :] = jnp.concatenate([jnp.zeros((HALF, HALF), jnp.float32), lower], axis=1)
    sub = lax.broadcasted_iota(jnp.int32, (8, K), 0)
    col = lax.broadcasted_iota(jnp.int32, (8, K), 1)
    for q in range(K // 8):
        c = 8 * q
        panel = a_ref[c:c + 8, :]
        if q > 0:
            done = out_ref[:c, :]
            panel = panel - lax.dot_general(
                done[:, c:c + 8], done, (((0,), (0,)), ((), ())),
                precision=lax.Precision.HIGHEST, preferred_element_type=jnp.float32)
        b = [[jnp.broadcast_to(panel[i:i + 1, c + m:c + m + 1], (8, K)) if m >= i else None for m in range(8)]
             for i in range(8)]
        rows = [jnp.broadcast_to(panel[i:i + 1, :], (8, K)) for i in range(8)]
        result = jnp.zeros((8, K), jnp.float32)
        for i in range(8):
            inv = 1.0 / jnp.sqrt(b[i][i]) if EXACT else lax.rsqrt(b[i][i])
            u = [b[i][m] * inv if m > i else None for m in range(8)]
            for m in range(i + 1, 8):
                for k in range(m, 8):
                    b[m][k] = b[m][k] - u[m] * u[k]
            rows[i] = rows[i] * inv
            for m in range(i + 1, 8):
                rows[m] = rows[m] - u[m] * rows[i]
            result = jnp.where(sub == i, rows[i], result)
        out_ref[c:c + 8, :] = jnp.where(col >= sub + c, result, 0.0)


def factor(scale, parts):
    return pl.pallas_call(
        functools.partial(factor_kernel, scale),
        in_specs=[vmem_spec()] * 4,
        out_specs=vmem_spec(),
        out_shape=f32(K, K),
        scratch_shapes=[pltpu.VMEM((K, K), jnp.float32)],
        compiler_params=pltpu.CompilerParams(vmem_limit_bytes=8 * 1024 * 1024),
        name="factor",
    )(*parts)


def gather_sums(x):
    def stage(x, axis, steps):
        size = lax.axis_size(axis)
        return (x, *[lax.ppermute(x, axis, [(i, i ^ d) for i in range(size)]) for d in steps])

    def total(x, g1, g2, g3):
        return (x + g1) + (g2 + g3)

    x, g1 = stage(x, "lat", (1,))
    x = total(*stage(x + g1, "lat", (2, 4, 6)))
    x = total(*stage(x, "lon", (1, 2, 3)))
    return stage(x, "lon", (4, 8, 12))


def shards(probes, kappa, sweep_counts, obs_cell, obs_owner, obs_count, r_inv):
    n_lat, n_lon = lax.axis_size("lat"), lax.axis_size("lon")
    lat, lon = lax.axis_index("lat"), lax.axis_index("lon")
    flags = jnp.stack([
        lat % 2, ((lat > 0) & (lat < n_lat - 1)).astype(jnp.int32),
        lon % 2, ((lon > 0) & (lon < n_lon - 1)).astype(jnp.int32),
    ]).astype(jnp.int32)
    lat_a, lat_b = swap(*edge_pack(sweep_counts, kappa, probes), "lat")
    y, own_a, own_b = turn(flags, kappa, probes)
    count = obs_count.reshape(1)
    cell, place = places(count, obs_cell, obs_owner.reshape(1, SLOTS))
    lon_a, lon_b = swap(*corner(flags, own_a, own_b, lat_a, lat_b, place), "lon")
    kap, act = coeffs(flags, sweep_counts, kappa, lat_a[H * C:], lat_b[H * C:], count)
    outgoing, tail_a, tail_b, _ = smooth(flags, cell, place, y, kap, act, (lat_a, lat_b, lon_a, lon_b))
    buffer = lax.all_to_all(outgoing, "lon", split_axis=0, concat_axis=0, tiled=True)
    mixed = weigh(buffer, r_inv[0, 0])
    returned = lax.all_to_all(mixed, "lon", split_axis=0, concat_axis=0, tiled=True)
    field, pay_a, pay_b, own_a, own_b = spread(flags, cell, place, count, returned)
    kap, act = coeffs(flags, sweep_counts, kappa, tail_a, tail_b, pay_a, lon_a, lon_b)
    lat_a, lat_b = swap(pay_a, pay_b, "lat")
    back = (lat_a, lat_b) + swap(*corner(flags, own_a, own_b, lat_a, lat_b, act), "lon")
    sketch, gram = finish(flags, field, kap, act, back, probes)
    cells_all = R * C * n_lat * n_lon
    r_factor = factor(1.0 / cells_all, gather_sums(gram))
    return (sketch, r_factor)


def solution(mesh):
    return jax.shard_map(
        shards,
        mesh=mesh,
        in_specs=(
            P(None, "lat", "lon"),
            P("lat", "lon"),
            P("lat"),
            P(("lat", "lon")),
            P(("lat", "lon"), None),
            P("lat", "lon"),
            P("lat", "lon", None, None),
        ),
        out_specs=(P(None, "lat", "lon"), P()),
        check_vma=False,
    )
```

```python
import functools

import jax
import jax.numpy as jnp
from jax import lax
from jax.experimental import pallas as pl
from jax.experimental.pallas import tpu as pltpu
from jax.sharding import PartitionSpec as P

SWEEPS = 4
CAP = 48
K = 128
R = 32
C = 256
H = 4
RE = R + 2 * H
CB = C + 16
NROW = RE * CB
OFF = 8
SLOTS = 384
PLACES = 768
LANES = 128
VMEM_LIMIT = 30 * 1024 * 1024
LAT_ROWS = H * C + 16
OWN_ROWS = R * H + R
LON_OWNERS = 16
WEIGH_PARTS = 3
HALF = 64
EXACT = False


def vmem_spec():
    return pl.BlockSpec(memory_space=pltpu.VMEM)


def smem_spec():
    return pl.BlockSpec(memory_space=pltpu.SMEM)


def hbm_spec():
    return pl.BlockSpec(memory_space=pltpu.HBM)


def params():
    return pltpu.CompilerParams(vmem_limit_bytes=VMEM_LIMIT)


def f32(*shape):
    return jax.ShapeDtypeStruct(shape, jnp.float32)


def held(*shape):
    return pltpu.VMEM(shape, jnp.float32)


def in_vmem(*arrays):
    return tuple(pltpu.with_memory_space_constraint(a, pltpu.VMEM) for a in arrays)


def in_hbm(array):
    return pltpu.with_memory_space_constraint(array, pltpu.HBM)


def at(r, c):
    return OFF + r * CB + c


def edge_pack_kernel(counts_hbm, kappa_hbm, p_hbm, pay_a, pay_b, chunk, kappa_ref, counts, sems):
    odd = lax.axis_index("lat") % 2
    first = (jnp.where(odd == 1, 0, R - H), jnp.where(odd == 1, R - H, 0))
    copies = []
    for side in range(2):
        block = pl.multiple_of(jnp.where(first[side] == 0, 0, R - 8), 8)
        for half in range(2):
            n = side * 2 + half
            copies.append(pltpu.make_async_copy(
                p_hbm.at[:, pl.ds(block, 8), pl.ds(half * LANES, LANES)], chunk.at[n], sems.at[n]))
    small = [pltpu.make_async_copy(kappa_hbm, kappa_ref, sems.at[4]),
             pltpu.make_async_copy(counts_hbm, counts, sems.at[5])]
    for copy in small + copies:
        copy.start()
    for copy in small:
        copy.wait()
    flat = chunk.reshape(4 * K * 8, LANES)
    for side, pay in ((0, pay_a), (1, pay_b)):
        within = jnp.where(first[side] == 0, 0, 8 - H)
        for r in range(H):
            for half in range(2):
                lanes = slice(half * LANES, (half + 1) * LANES)
                pay[H * C + 2 * r + half:H * C + 2 * r + half + 1, :] = jnp.where(
                    first[side] == 0, kappa_ref[r:r + 1, lanes], kappa_ref[R - H + r:R - H + r + 1, lanes])
            value = counts[first[side] + r].astype(jnp.float32)
            pay[H * C + 8 + r:H * C + 9 + r, :] = jnp.full((1, K), value, jnp.float32)
        pay[H * C + 8 + H:, :] = jnp.zeros((4, K), jnp.float32)
        for half in range(2):
            n = side * 2 + half
            copies[n].wait()
            for r in range(H):
                pay[r * C + half * LANES:r * C + (half + 1) * LANES, :] = flat[
                    pl.ds(n * K * 8 + within + r, K, stride=8), :].T


def edge_pack(counts, kappa, probes):
    return pl.pallas_call(
        edge_pack_kernel,
        in_specs=[hbm_spec()] * 3,
        out_specs=[vmem_spec()] * 2,
        out_shape=[f32(LAT_ROWS, K)] * 2,
        scratch_shapes=[
            pltpu.VMEM((4, K, 8, LANES), jnp.float32),
            pltpu.VMEM((R, C), jnp.float32),
            pltpu.SMEM((R,), jnp.int32),
            pltpu.SemaphoreType.DMA((6,)),
        ],
        compiler_params=pltpu.CompilerParams(vmem_limit_bytes=8 * 1024 * 1024),
        name="edge_pack",
    )(in_hbm(counts), in_hbm(kappa), in_hbm(probes))


def turn_kernel(flags, kappa_ref, p_hbm, ext, own_a, own_b, chunk, sems):
    def copy(n):
        half, block = n // 4, n % 4
        return pltpu.make_async_copy(
            p_hbm.at[:, pl.ds(block * 8, 8), pl.ds(half * LANES, LANES)], chunk.at[n], sems.at[n])

    for n in range(8):
        copy(n).start()
    flat = chunk.reshape(8 * K * 8, LANES)
    for n in range(8):
        copy(n).wait()
        half, block = n // 4, n % 4
        for i in range(8):
            r = block * 8 + i
            ext[pl.ds(at(r + H, 8) + half * LANES, LANES), :] = flat[pl.ds(n * K * 8 + i, K, stride=8), :].T
    odd = flags[2]
    for own, low in ((own_a, odd), (own_b, 1 - odd)):
        col = jnp.where(low == 1, 0, C - H)
        lane = pl.multiple_of(jnp.where(low == 1, 0, LANES), LANES)
        for r in range(R):
            own[r * H:(r + 1) * H, :] = ext[pl.ds(at(r + H, 8) + col, H), :]
        own[R * H:, :] = kappa_ref[:, pl.ds(lane, LANES)]


def turn(flags, kappa, probes):
    return pl.pallas_call(
        turn_kernel,
        in_specs=[smem_spec(), vmem_spec(), hbm_spec()],
        out_specs=[vmem_spec()] * 3,
        out_shape=[held(NROW + 16, K), held(OWN_ROWS, K), held(OWN_ROWS, K)],
        scratch_shapes=[pltpu.VMEM((8, K, 8, LANES), jnp.float32), pltpu.SemaphoreType.DMA((8,))],
        compiler_params=pltpu.CompilerParams(vmem_limit_bytes=12 * 1024 * 1024),
        cost_estimate=pl.CostEstimate(flops=0, bytes_accessed=12 * 1024 * 1024, transcendentals=0),
        name="turn",
    )(flags, kappa, in_hbm(probes))


def corner_kernel(flags, own_a, own_b, lat_a, lat_b, after, pay_a, pay_b):
    odd = flags[2]
    own_rows = own_a.shape[0]
    for own, pay, low in ((own_a, pay_a, odd), (own_b, pay_b, 1 - odd)):
        col = jnp.where(low == 1, 0, C - H)
        pay[:own_rows, :] = own[...]
        base = own_rows
        for lat in (lat_a, lat_b):
            for r in range(H):
                pay[base:base + H, :] = lat[pl.ds(r * C + col, H), :]
                base += H
        if own_rows > R * H:
            for lat in (lat_a, lat_b):
                for r in range(H):
                    pay[base:base + 1, :] = lat[pl.ds(H * C + 2 * r + 1 - low, 1), :]
                    base += 1


def corner(flags, own_a, own_b, lat_a, lat_b, after):
    rows = own_a.shape[0] + 2 * H * H + (2 * H if own_a.shape[0] > R * H else 0)
    return pl.pallas_call(
        corner_kernel,
        in_specs=[smem_spec()] + [vmem_spec()] * 4 + [pl.BlockSpec(memory_space=pl.ANY)],
        out_specs=[vmem_spec()] * 2,
        out_shape=[f32(rows, K)] * 2,
        compiler_params=pltpu.CompilerParams(vmem_limit_bytes=8 * 1024 * 1024),
        name="corner",
    )(flags, *in_vmem(own_a, own_b), lat_a, lat_b, after)


def put_halos(buf, flags, lat_a, lat_b, lon_a, lon_b):
    odd = flags[0]
    lon_odd = flags[2]
    lat_ok = (None, flags[1] == 1)
    lon_ok = (None, flags[3] == 1)
    lat_row = (jnp.where(odd == 1, 0, R + H), jnp.where(odd == 1, R + H, 0))
    lon_col = (jnp.where(lon_odd == 1, 0, C + H), jnp.where(lon_odd == 1, C + H, 0))

    def keep(ok, x):
        return x if ok is None else jnp.where(ok, x, 0.0)

    own_rows = lon_a.shape[0] - 2 * H * H
    own_rows = R * H if own_rows == R * H else OWN_ROWS
    for n, lat in ((0, lat_a), (1, lat_b)):
        for r in range(H):
            start = pl.multiple_of(OFF + (lat_row[n] + r) * CB + 8, 8)
            buf[pl.ds(start, C), :] = keep(lat_ok[n], lat[r * C:(r + 1) * C, :])
    for m, lon in ((0, lon_a), (1, lon_b)):
        for r in range(R):
            start = at(r + H, 4) + lon_col[m]
            buf[pl.ds(start, H), :] = keep(lon_ok[m], lon[r * H:(r + 1) * H, :])
        for n in range(2):
            for r in range(H):
                part = own_rows + (n * H + r) * H
                start = OFF + (lat_row[n] + r) * CB + 4 + lon_col[m]
                buf[pl.ds(start, H), :] = keep(lat_ok[n], keep(lon_ok[m], lon[part:part + H, :]))


def put_own_kappa(kap, act, counts, kappa_ref):
    kap_t = kappa_ref[...].T
    for r in range(R):
        kap[pl.ds(at(r + H, 8), C), :] = jnp.broadcast_to(kap_t[:, r:r + 1], (C, K))
        for s in range(SWEEPS):
            act[s, r + H] = jnp.full((8, K), jnp.where(counts[r] > s, 1.0, 0.0), jnp.float32)


def put_lat_kappa(kap, act, flags, tail_a, tail_b):
    odd = flags[0]
    lat_ok = (None, flags[1] == 1)
    lat_row = (jnp.where(odd == 1, 0, R + H), jnp.where(odd == 1, R + H, 0))
    for n, lat in ((0, tail_a), (1, tail_b)):
        turned = lat[:8, :].T
        if n == 1:
            turned = jnp.where(lat_ok[1], turned, 0.0)
        for r in range(H):
            for h in range(2):
                start = pl.multiple_of(OFF + (lat_row[n] + r) * CB + 8 + h * LANES, 8)
                kap[pl.ds(start, LANES), :] = jnp.broadcast_to(turned[:, 2 * r + h:2 * r + h + 1], (LANES, K))
            wide = jnp.broadcast_to(lat[8 + r:9 + r, :], (8, K))
            for s in range(SWEEPS):
                act[s, lat_row[n] + r] = jnp.where(wide > s, 1.0, 0.0)


def put_lon_kappa(kap, flags, lon_a, lon_b):
    odd = flags[0]
    lon_odd = flags[2]
    lat_ok = (None, flags[1] == 1)
    lat_row = (jnp.where(odd == 1, 0, R + H), jnp.where(odd == 1, R + H, 0))
    lon_col = (jnp.where(lon_odd == 1, 0, C + H), jnp.where(lon_odd == 1, C + H, 0))
    for m, lon in ((0, lon_a), (1, lon_b)):
        src = (jnp.where(lon_odd == 1, LANES - H, 0), jnp.where(lon_odd == 1, 0, LANES - H))[m]
        own = lon[R * H:R * H + R, :].T
        tail = lon[OWN_ROWS + 2 * H * H:, :].T
        low, high = own[:H, :], own[LANES - H:, :]
        edge = jnp.where(src == 0, low, high)
        tail = jnp.where(src == 0, tail[:H, :], tail[LANES - H:, :])
        if m == 1:
            edge = jnp.where(flags[3] == 1, edge, 0.0)
            tail = jnp.where(flags[3] == 1, tail, 0.0)
        for r in range(R):
            kap[pl.ds(at(r + H, 4) + lon_col[m], H), :] = jnp.broadcast_to(edge[:, r:r + 1], (H, K))
        for n in range(2):
            for r in range(H):
                part = jnp.broadcast_to(tail[:, n * H + r:n * H + r + 1], (H, K))
                if n == 1:
                    part = jnp.where(lat_ok[1], part, 0.0)
                kap[pl.ds(OFF + (lat_row[n] + r) * CB + 4 + lon_col[m], H), :] = part


def relax(src, dst, kap, act, s, r, tiles):
    base = pl.multiple_of(r * CB, 8)
    a0 = act[s, r]
    a1 = act[s, r + 1]
    for t in tiles:
        o = base + OFF + t * 8
        up = src[pl.ds(o - CB, 8), :]
        c0 = src[pl.ds(o, 8), :]
        c1 = src[pl.ds(o + CB, 8), :]
        dn = src[pl.ds(o + 2 * CB, 8), :]
        l0 = src[pl.ds(o - 1, 8), :]
        r0 = src[pl.ds(o + 1, 8), :]
        l1 = src[pl.ds(o + CB - 1, 8), :]
        r1 = src[pl.ds(o + CB + 1, 8), :]
        lap0 = (up + c1) + (l0 + r0) - 4.0 * c0
        lap1 = (c0 + dn) + (l1 + r1) - 4.0 * c1
        dst[pl.ds(o, 8), :] = c0 + (a0 * kap[pl.ds(o, 8), :]) * lap0
        dst[pl.ds(o + CB, 8), :] = c1 + (a1 * kap[pl.ds(o + CB, 8), :]) * lap1


INNER = tuple(range(1, CB // 8 - 1))
EDGE = (0, 1, CB // 8 - 2, CB // 8 - 1)


def inner_kernel(ext, kap, act, *levels):
    src = ext
    for s in range(SWEEPS):
        t = s + 1

        def body(i, _):
            relax(src, levels[s], kap, act, s, t + H + 2 * i, INNER)
            return 0

        lax.fori_loop(0, (R - 2 * t) // 2, body, 0)
        src = levels[s]


def inner(ext, kap, act):
    return pl.pallas_call(
        inner_kernel,
        in_specs=[vmem_spec()] * 3,
        out_specs=[vmem_spec()] * SWEEPS,
        out_shape=[held(NROW + 16, K)] * SWEEPS,
        compiler_params=pltpu.CompilerParams(vmem_limit_bytes=2 * 1024 * 1024),
        cost_estimate=pl.CostEstimate(flops=0, bytes_accessed=16 * 1024 * 1024, transcendentals=0),
        name="inner",
    )(*in_vmem(ext, kap, act))


def outer(levels, kap, act):
    for s in range(SWEEPS):
        t = s + 1
        tiles = INNER if t == SWEEPS else tuple(range(CB // 8))
        sides = tuple(c for c in EDGE if c in tiles)

        def ends(i, _):
            relax(levels[s], levels[t], kap, act, s, jnp.where(i < 2, t + 2 * i, R + H - t + 2 * i - 4), tiles)
            return 0

        def middle(i, _):
            relax(levels[s], levels[t], kap, act, s, t + H + 2 * i, sides)
            return 0

        lax.fori_loop(0, 4, ends, 0)
        lax.fori_loop(0, (R - 2 * t) // 2, middle, 0, unroll=2)


def coeffs_kernel(flags, counts, kappa_ref, after, *rest):
    *halos, kap, act = rest
    put_own_kappa(kap, act, counts, kappa_ref)
    if halos:
        put_lat_kappa(kap, act, flags, *halos[:2])
        put_lon_kappa(kap, flags, *halos[2:])


def coeffs(flags, counts, kappa, after, *halos):
    return pl.pallas_call(
        coeffs_kernel,
        in_specs=[smem_spec()] * 2 + [vmem_spec(), pl.BlockSpec(memory_space=pl.ANY)] + [vmem_spec()] * len(halos),
        out_specs=[vmem_spec()] * 2,
        out_shape=[held(NROW + 16, K), held(SWEEPS, RE, 8, K)],
        compiler_params=pltpu.CompilerParams(vmem_limit_bytes=8 * 1024 * 1024),
        cost_estimate=pl.CostEstimate(flops=0, bytes_accessed=4 * 1024 * 1024, transcendentals=0),
        name="coeffs",
    )(flags, counts, kappa, after, *halos)


def places_kernel(count_ref, cell_ref, owner_ref, after, row_ref, place_ref, seen):
    for i in range(LON_OWNERS):
        seen[i] = 0
    count = count_ref[0]

    def one(t, _):
        owner = owner_ref[0, t]
        rank = seen[owner]
        live = t < count
        seen[owner] = rank + jnp.where(live, 1, 0)
        place_ref[t] = jnp.where(live, owner * CAP + rank, PLACES)
        cell = cell_ref[t]
        row_ref[t] = OFF + 8 + H * CB + (cell >> 8) * CB + (cell & (C - 1))
        return 0

    lax.fori_loop(0, SLOTS, one, 0, unroll=8)


def places(count, cell, owner, after):
    return pl.pallas_call(
        places_kernel,
        in_specs=[smem_spec()] * 3 + [pl.BlockSpec(memory_space=pl.ANY)],
        out_specs=[smem_spec()] * 2,
        out_shape=[jax.ShapeDtypeStruct((SLOTS,), jnp.int32)] * 2,
        scratch_shapes=[pltpu.SMEM((LON_OWNERS,), jnp.int32)],
        cost_estimate=pl.CostEstimate(flops=0, bytes_accessed=4 * 1024 * 1024, transcendentals=0),
        compiler_params=pltpu.CompilerParams(vmem_limit_bytes=1024 * 1024),
        name="places",
    )(count, cell, owner, after)


def smooth_kernel(flags, cell_ref, place_ref, *refs):
    (ext_in, l1_in, l2_in, l3_in, l4_in, kap_in, act_in, lat_a, lat_b, lon_a, lon_b,
     out_ref, tail_a, tail_b, ext, l1, l2, l3, l4, kap, act, rows_ref) = refs
    tail_a[...] = lat_a[H * C:, :]
    tail_b[...] = lat_b[H * C:, :]
    put_lat_kappa(kap, act, flags, tail_a, tail_b)
    put_lon_kappa(kap, flags, lon_a, lon_b)
    put_halos(ext, flags, lat_a, lat_b, lon_a, lon_b)
    outer((ext, l1, l2, l3, l4), kap, act)
    rows_ref[...] = jnp.zeros_like(rows_ref)

    def copy(i, _):
        for j in range(8):
            t = i * 8 + j
            rows_ref[pl.ds(place_ref[t], 1), :] = l4[pl.ds(cell_ref[t], 1), :]
        return 0

    lax.fori_loop(0, SLOTS // 8, copy, 0)
    out_ref[...] = rows_ref[:PLACES]


def smooth(flags, cell, place, ext, levels, kap, act, halos):
    return pl.pallas_call(
        smooth_kernel,
        in_specs=[smem_spec()] * 3 + [vmem_spec()] * 11,
        out_specs=[vmem_spec()] * 10,
        out_shape=[f32(PLACES, K), f32(16, K), f32(16, K)] + [held(NROW + 16, K)] * 6 + [held(SWEEPS, RE, 8, K)],
        input_output_aliases={3 + i: 3 + i for i in range(7)},
        scratch_shapes=[pltpu.VMEM((PLACES + 8, K), jnp.float32)],
        compiler_params=pltpu.CompilerParams(vmem_limit_bytes=8 * 1024 * 1024),
        name="smooth",
    )(flags, cell, place, *in_vmem(ext, *levels, kap, act), *halos)[:3]


def weigh_kernel(b_ref, r_hbm, out_ref, r_ref, sems):
    width = PLACES // WEIGH_PARTS

    def copy(n):
        return pltpu.make_async_copy(r_hbm.at[:, pl.ds(n * width, width)], r_ref.at[n], sems.at[n])

    for n in range(WEIGH_PARTS):
        copy(n).start()
    b = b_ref[...].T
    high = b.astype(jnp.bfloat16)
    low = (b - high.astype(jnp.float32)).astype(jnp.bfloat16)
    both = jnp.concatenate([high, low], axis=0)
    for n in range(WEIGH_PARTS):
        copy(n).wait()
        r = r_ref[n]
        r_high = r.astype(jnp.bfloat16)
        r_low = (r - r_high.astype(jnp.float32)).astype(jnp.bfloat16)
        one = jnp.dot(both, r_high, preferred_element_type=jnp.float32)
        two = jnp.dot(high, r_low, preferred_element_type=jnp.float32)
        out_ref[n * width:(n + 1) * width, :] = (one[:K] + (one[K:] + two)).T


def weigh(buffer, r):
    return pl.pallas_call(
        weigh_kernel,
        in_specs=[vmem_spec(), hbm_spec()],
        out_specs=vmem_spec(),
        out_shape=f32(PLACES, K),
        scratch_shapes=[
            pltpu.VMEM((WEIGH_PARTS, PLACES, PLACES // WEIGH_PARTS), jnp.float32),
            pltpu.SemaphoreType.DMA((WEIGH_PARTS,)),
        ],
        compiler_params=pltpu.CompilerParams(vmem_limit_bytes=12 * 1024 * 1024),
        name="weigh",
    )(buffer, in_hbm(r))


def spread_kernel(flags, cell_ref, place_ref, count_ref, ret_ref, field, pay_a, pay_b, own_a, own_b):
    field[...] = jnp.zeros_like(field)

    def add(t, _):
        i = pl.ds(cell_ref[t], 1)
        field[i, :] = field[i, :] + ret_ref[pl.ds(place_ref[t], 1), :]
        return 0

    lax.fori_loop(0, count_ref[0], add, 0)
    odd = flags[0]
    lon_odd = flags[2]
    for pay, low in ((pay_a, odd), (pay_b, 1 - odd)):
        first = jnp.where(low == 1, H, R)
        for r in range(H):
            start = pl.multiple_of(OFF + (first + r) * CB + 8, 8)
            pay[r * C:(r + 1) * C, :] = field[pl.ds(start, C), :]
    for own, low in ((own_a, lon_odd), (own_b, 1 - lon_odd)):
        col = jnp.where(low == 1, 8, 4 + C)
        for r in range(R):
            own[r * H:(r + 1) * H, :] = field[pl.ds(at(r + H, 0) + col, H), :]


def spread(flags, cell, place, count, returned):
    return pl.pallas_call(
        spread_kernel,
        in_specs=[smem_spec()] * 4 + [vmem_spec()],
        out_specs=[vmem_spec()] * 5,
        out_shape=[held(NROW + 16, K), f32(H * C, K), f32(H * C, K), held(R * H, K), held(R * H, K)],
        compiler_params=pltpu.CompilerParams(vmem_limit_bytes=10 * 1024 * 1024),
        name="spread",
    )(flags, cell, place, count, returned)


def finish_kernel(flags, *refs):
    (ext_in, l1_in, l2_in, l3_in, l4_in, kap, act, lat_a, lat_b, lon_a, lon_b, p_hbm,
     out_hbm, gram_ref, ext, l1, l2, l3, l4, chunk, in_sems, out_sems) = refs

    def part(ref, n):
        half, block = n // 4, n % 4
        return ref.at[:, pl.ds(block * 8, 8), pl.ds(half * LANES, LANES)]

    def copy_in(n):
        return pltpu.make_async_copy(part(p_hbm, n), chunk.at[n], in_sems.at[n])

    def copy_out(n):
        return pltpu.make_async_copy(chunk.at[n], part(out_hbm, n), out_sems.at[n])

    for n in range(8):
        copy_in(n).start()
    put_halos(ext, flags, lat_a, lat_b, lon_a, lon_b)
    outer((ext, l1, l2, l3, l4), kap, act)
    flat = chunk.reshape(8 * K * 8, LANES)
    contract = (((1,), (1,)), ((), ()))
    hh = jnp.zeros((K, K), jnp.float32)
    hl = jnp.zeros((K, K), jnp.float32)
    for n in range(8):
        half, block = n // 4, n % 4
        copy_in(n).wait()
        for i in range(0, 8, 2):
            parts = []
            for j in range(2):
                where = pl.ds(n * K * 8 + i + j, K, stride=8)
                start = at(block * 8 + i + j + H, 8) + half * LANES
                sk = flat[where, :] + l4[pl.ds(start, LANES), :].T
                flat[where, :] = sk
                parts.append(sk)
            sk = jnp.concatenate(parts, axis=1)
            high = sk.astype(jnp.bfloat16)
            low = (sk - high.astype(jnp.float32)).astype(jnp.bfloat16)
            hh = hh + lax.dot_general(high, high, contract, preferred_element_type=jnp.float32)
            hl = hl + lax.dot_general(high, low, contract, preferred_element_type=jnp.float32)
        copy_out(n).start()
    gram = hh + (hl + hl.T)
    top = gram[:HALF]
    turned = pltpu.roll(gram[HALF:], HALF, 1)
    row = lax.broadcasted_iota(jnp.int32, (HALF, K), 0)
    lane = lax.broadcasted_iota(jnp.int32, (HALF, K), 1)
    gram_ref[:HALF, :] = jnp.where((lane < HALF) & (row > lane), turned, top)
    gram_ref[HALF:, :] = jnp.broadcast_to(jnp.sum(jnp.where(row == lane, turned, 0.0), axis=0, keepdims=True), (8, K))
    for n in range(8):
        copy_out(n).wait()


def finish(flags, ext, levels, kap, act, halos, probes):
    return pl.pallas_call(
        finish_kernel,
        in_specs=[smem_spec()] + [vmem_spec()] * 11 + [hbm_spec()],
        out_specs=[hbm_spec()] + [vmem_spec()] * 6,
        out_shape=[f32(K, R, C), f32(HALF + 8, K)] + [held(NROW + 16, K)] * 5,
        input_output_aliases={1 + i: 2 + i for i in range(5)},
        scratch_shapes=[
            pltpu.VMEM((8, K, 8, LANES), jnp.float32),
            pltpu.SemaphoreType.DMA((8,)),
            pltpu.SemaphoreType.DMA((8,)),
        ],
        compiler_params=pltpu.CompilerParams(vmem_limit_bytes=12 * 1024 * 1024),
        name="finish",
    )(flags, *in_vmem(ext, *levels, kap, act), *halos, in_hbm(probes))[:2]


def pairs(size, first):
    return [(i, (i + 1) % size if (i - first) % 2 == 0 else (i - 1) % size) for i in range(size)]


def swap(a, b, axis):
    size = lax.axis_size(axis)
    return lax.ppermute(a, axis, pairs(size, 0)), lax.ppermute(b, axis, pairs(size, 1))


def factor_kernel(scale, x_ref, g1_ref, g2_ref, g3_ref, out_ref, a_ref):
    total = ((x_ref[...] + g1_ref[...]) + (g2_ref[...] + g3_ref[...])) * scale
    top = total[:HALF]
    a_ref[:HALF, :] = top
    lower = top.T[:HALF]
    row = lax.broadcasted_iota(jnp.int32, (HALF, HALF), 0)
    lane = lax.broadcasted_iota(jnp.int32, (HALF, HALF), 1)
    lower = jnp.where(row == lane, jnp.broadcast_to(total[HALF:HALF + 1, :HALF], (HALF, HALF)), lower)
    a_ref[HALF:, :] = jnp.concatenate([jnp.zeros((HALF, HALF), jnp.float32), lower], axis=1)
    sub = lax.broadcasted_iota(jnp.int32, (8, K), 0)
    col = lax.broadcasted_iota(jnp.int32, (8, K), 1)
    for q in range(K // 8):
        c = 8 * q
        panel = a_ref[c:c + 8, :]
        if q > 0:
            done = out_ref[:c, :]
            panel = panel - lax.dot_general(
                done[:, c:c + 8], done, (((0,), (0,)), ((), ())),
                precision=lax.Precision.HIGHEST, preferred_element_type=jnp.float32)
        b = [[jnp.broadcast_to(panel[i:i + 1, c + m:c + m + 1], (8, K)) if m >= i else None for m in range(8)]
             for i in range(8)]
        rows = [jnp.broadcast_to(panel[i:i + 1, :], (8, K)) for i in range(8)]
        result = jnp.zeros((8, K), jnp.float32)
        for i in range(8):
            inv = 1.0 / jnp.sqrt(b[i][i]) if EXACT else lax.rsqrt(b[i][i])
            u = [b[i][m] * inv if m > i else None for m in range(8)]
            for m in range(i + 1, 8):
                for k in range(m, 8):
                    b[m][k] = b[m][k] - u[m] * u[k]
            rows[i] = rows[i] * inv
            for m in range(i + 1, 8):
                rows[m] = rows[m] - u[m] * rows[i]
            result = jnp.where(sub == i, rows[i], result)
        out_ref[c:c + 8, :] = jnp.where(col >= sub + c, result, 0.0)


def factor(scale, parts):
    return pl.pallas_call(
        functools.partial(factor_kernel, scale),
        in_specs=[vmem_spec()] * 4,
        out_specs=vmem_spec(),
        out_shape=f32(K, K),
        scratch_shapes=[pltpu.VMEM((K, K), jnp.float32)],
        compiler_params=pltpu.CompilerParams(vmem_limit_bytes=8 * 1024 * 1024),
        name="factor",
    )(*parts)


def gather_sums(x):
    def stage(x, axis, steps):
        size = lax.axis_size(axis)
        return (x, *[lax.ppermute(x, axis, [(i, i ^ d) for i in range(size)]) for d in steps])

    def total(x, g1, g2, g3):
        return (x + g1) + (g2 + g3)

    x, g1 = stage(x, "lat", (1,))
    x = total(*stage(x + g1, "lat", (2, 4, 6)))
    x = total(*stage(x, "lon", (1, 2, 3)))
    return stage(x, "lon", (4, 8, 12))


def shards(probes, kappa, sweep_counts, obs_cell, obs_owner, obs_count, r_inv):
    n_lat, n_lon = lax.axis_size("lat"), lax.axis_size("lon")
    lat, lon = lax.axis_index("lat"), lax.axis_index("lon")
    flags = jnp.stack([
        lat % 2, ((lat > 0) & (lat < n_lat - 1)).astype(jnp.int32),
        lon % 2, ((lon > 0) & (lon < n_lon - 1)).astype(jnp.int32),
    ]).astype(jnp.int32)
    lat_a, lat_b = swap(*edge_pack(sweep_counts, kappa, probes), "lat")
    ext, own_a, own_b = turn(flags, kappa, probes)
    kap, act = coeffs(flags, sweep_counts, kappa, own_a)
    levels = inner(ext, kap, act)
    count = obs_count.reshape(1)
    lon_pay = corner(flags, own_a, own_b, lat_a, lat_b, levels[-1])
    cell, place = places(count, obs_cell, obs_owner.reshape(1, SLOTS), lon_pay[0])
    lon_a, lon_b = swap(*lon_pay, "lon")
    outgoing, tail_a, tail_b = smooth(flags, cell, place, ext, levels, kap, act, (lat_a, lat_b, lon_a, lon_b))
    buffer = lax.all_to_all(outgoing, "lon", split_axis=0, concat_axis=0, tiled=True)
    mixed = weigh(buffer, r_inv[0, 0])
    returned = lax.all_to_all(mixed, "lon", split_axis=0, concat_axis=0, tiled=True)
    field, pay_a, pay_b, own_a, own_b = spread(flags, cell, place, count, returned)
    kap, act = coeffs(flags, sweep_counts, kappa, pay_a, tail_a, tail_b, lon_a, lon_b)
    levels = inner(field, kap, act)
    lat_a, lat_b = swap(pay_a, pay_b, "lat")
    back = (lat_a, lat_b) + swap(*corner(flags, own_a, own_b, lat_a, lat_b, levels[-1]), "lon")
    sketch, gram = finish(flags, field, levels, kap, act, back, probes)
    cells_all = R * C * n_lat * n_lon
    r_factor = factor(1.0 / cells_all, gather_sums(gram))
    return (sketch, r_factor)


def solution(mesh):
    return jax.shard_map(
        shards,
        mesh=mesh,
        in_specs=(
            P(None, "lat", "lon"),
            P("lat", "lon"),
            P("lat"),
            P(("lat", "lon")),
            P(("lat", "lon"), None),
            P("lat", "lon"),
            P("lat", "lon", None, None),
        ),
        out_specs=(P(None, "lat", "lon"), P()),
        check_vma=False,
    )
```

```python
import functools

import jax
import jax.numpy as jnp
from jax import lax
from jax.experimental import pallas as pl
from jax.experimental.pallas import tpu as pltpu
from jax.sharding import PartitionSpec as P

SWEEPS = 4
CAP = 48
K = 128
R = 32
C = 256
H = 4
RE = R + 2 * H
CB = C + 16
NROW = RE * CB
OFF = 8
SLOTS = 384
PLACES = 768
LANES = 128
VMEM_LIMIT = 30 * 1024 * 1024
LAT_ROWS = H * C + 16
OWN_ROWS = R * H + R
WEIGH_PARTS = 3
HALF = 64


def vmem_spec():
    return pl.BlockSpec(memory_space=pltpu.VMEM)


def smem_spec():
    return pl.BlockSpec(memory_space=pltpu.SMEM)


def hbm_spec():
    return pl.BlockSpec(memory_space=pltpu.HBM)


def params():
    return pltpu.CompilerParams(vmem_limit_bytes=VMEM_LIMIT)


def f32(*shape):
    return jax.ShapeDtypeStruct(shape, jnp.float32)


def held(*shape):
    return pltpu.VMEM(shape, jnp.float32)


def in_vmem(*arrays):
    return tuple(pltpu.with_memory_space_constraint(a, pltpu.VMEM) for a in arrays)


def in_hbm(array):
    return pltpu.with_memory_space_constraint(array, pltpu.HBM)


def at(r, c):
    return OFF + r * CB + c


def edge_pack_kernel(counts_hbm, kappa_hbm, p_hbm, pay_a, pay_b, chunk, kappa_ref, counts, sems):
    odd = lax.axis_index("lat") % 2
    first = (jnp.where(odd == 1, 0, R - H), jnp.where(odd == 1, R - H, 0))
    copies = []
    for side in range(2):
        block = pl.multiple_of(jnp.where(first[side] == 0, 0, R - 8), 8)
        for half in range(2):
            n = side * 2 + half
            copies.append(pltpu.make_async_copy(
                p_hbm.at[:, pl.ds(block, 8), pl.ds(half * LANES, LANES)], chunk.at[n], sems.at[n]))
    small = [pltpu.make_async_copy(kappa_hbm, kappa_ref, sems.at[4]),
             pltpu.make_async_copy(counts_hbm, counts, sems.at[5])]
    for copy in small + copies:
        copy.start()
    for copy in small:
        copy.wait()
    flat = chunk.reshape(4 * K * 8, LANES)
    for side, pay in ((0, pay_a), (1, pay_b)):
        within = jnp.where(first[side] == 0, 0, 8 - H)
        for r in range(H):
            for half in range(2):
                lanes = slice(half * LANES, (half + 1) * LANES)
                pay[H * C + 2 * r + half:H * C + 2 * r + half + 1, :] = jnp.where(
                    first[side] == 0, kappa_ref[r:r + 1, lanes], kappa_ref[R - H + r:R - H + r + 1, lanes])
            value = counts[first[side] + r].astype(jnp.float32)
            pay[H * C + 8 + r:H * C + 9 + r, :] = jnp.full((1, K), value, jnp.float32)
        pay[H * C + 8 + H:, :] = jnp.zeros((4, K), jnp.float32)
        for half in range(2):
            n = side * 2 + half
            copies[n].wait()
            for r in range(H):
                pay[r * C + half * LANES:r * C + (half + 1) * LANES, :] = flat[
                    pl.ds(n * K * 8 + within + r, K, stride=8), :].T


def edge_pack(counts, kappa, probes):
    return pl.pallas_call(
        edge_pack_kernel,
        in_specs=[hbm_spec()] * 3,
        out_specs=[vmem_spec()] * 2,
        out_shape=[f32(LAT_ROWS, K)] * 2,
        scratch_shapes=[
            pltpu.VMEM((4, K, 8, LANES), jnp.float32),
            pltpu.VMEM((R, C), jnp.float32),
            pltpu.SMEM((R,), jnp.int32),
            pltpu.SemaphoreType.DMA((6,)),
        ],
        compiler_params=pltpu.CompilerParams(vmem_limit_bytes=8 * 1024 * 1024),
        name="edge_pack",
    )(in_hbm(counts), in_hbm(kappa), in_hbm(probes))


def turn_kernel(flags, kappa_ref, p_hbm, ext, own_a, own_b, chunk, sems):
    def copy(n):
        half, block = n // 4, n % 4
        return pltpu.make_async_copy(
            p_hbm.at[:, pl.ds(block * 8, 8), pl.ds(half * LANES, LANES)], chunk.at[n], sems.at[n])

    for n in range(8):
        copy(n).start()
    flat = chunk.reshape(8 * K * 8, LANES)
    for n in range(8):
        copy(n).wait()
        half, block = n // 4, n % 4
        for i in range(8):
            r = block * 8 + i
            ext[pl.ds(at(r + H, 8) + half * LANES, LANES), :] = flat[pl.ds(n * K * 8 + i, K, stride=8), :].T
    odd = flags[2]
    for own, low in ((own_a, odd), (own_b, 1 - odd)):
        col = jnp.where(low == 1, 0, C - H)
        lane = pl.multiple_of(jnp.where(low == 1, 0, LANES), LANES)
        for r in range(R):
            own[r * H:(r + 1) * H, :] = ext[pl.ds(at(r + H, 8) + col, H), :]
        own[R * H:, :] = kappa_ref[:, pl.ds(lane, LANES)]


def turn(flags, kappa, probes):
    return pl.pallas_call(
        turn_kernel,
        in_specs=[smem_spec(), vmem_spec(), hbm_spec()],
        out_specs=[vmem_spec()] * 3,
        out_shape=[held(NROW + 16, K), held(OWN_ROWS, K), held(OWN_ROWS, K)],
        scratch_shapes=[pltpu.VMEM((8, K, 8, LANES), jnp.float32), pltpu.SemaphoreType.DMA((8,))],
        compiler_params=pltpu.CompilerParams(vmem_limit_bytes=12 * 1024 * 1024),
        cost_estimate=pl.CostEstimate(flops=0, bytes_accessed=12 * 1024 * 1024, transcendentals=0),
        name="turn",
    )(flags, kappa, in_hbm(probes))


def corner_kernel(flags, own_a, own_b, lat_a, lat_b, after, pay_a, pay_b):
    odd = flags[2]
    own_rows = own_a.shape[0]
    for own, pay, low in ((own_a, pay_a, odd), (own_b, pay_b, 1 - odd)):
        col = jnp.where(low == 1, 0, C - H)
        pay[:own_rows, :] = own[...]
        base = own_rows
        for lat in (lat_a, lat_b):
            for r in range(H):
                pay[base:base + H, :] = lat[pl.ds(r * C + col, H), :]
                base += H
        if own_rows > R * H:
            for lat in (lat_a, lat_b):
                for r in range(H):
                    pay[base:base + 1, :] = lat[pl.ds(H * C + 2 * r + 1 - low, 1), :]
                    base += 1


def corner(flags, own_a, own_b, lat_a, lat_b, after):
    rows = own_a.shape[0] + 2 * H * H + (2 * H if own_a.shape[0] > R * H else 0)
    return pl.pallas_call(
        corner_kernel,
        in_specs=[smem_spec()] + [vmem_spec()] * 4 + [pl.BlockSpec(memory_space=pl.ANY)],
        out_specs=[vmem_spec()] * 2,
        out_shape=[f32(rows, K)] * 2,
        compiler_params=pltpu.CompilerParams(vmem_limit_bytes=8 * 1024 * 1024),
        name="corner",
    )(flags, *in_vmem(own_a, own_b), lat_a, lat_b, after)


def put_halos(buf, flags, lat_a, lat_b, lon_a, lon_b):
    odd = flags[0]
    lon_odd = flags[2]
    lat_ok = (None, flags[1] == 1)
    lon_ok = (None, flags[3] == 1)
    lat_row = (jnp.where(odd == 1, 0, R + H), jnp.where(odd == 1, R + H, 0))
    lon_col = (jnp.where(lon_odd == 1, 0, C + H), jnp.where(lon_odd == 1, C + H, 0))

    def keep(ok, x):
        return x if ok is None else jnp.where(ok, x, 0.0)

    own_rows = lon_a.shape[0] - 2 * H * H
    own_rows = R * H if own_rows == R * H else OWN_ROWS
    for n, lat in ((0, lat_a), (1, lat_b)):
        for r in range(H):
            start = pl.multiple_of(OFF + (lat_row[n] + r) * CB + 8, 8)
            buf[pl.ds(start, C), :] = keep(lat_ok[n], lat[r * C:(r + 1) * C, :])
    for m, lon in ((0, lon_a), (1, lon_b)):
        for r in range(R):
            start = at(r + H, 4) + lon_col[m]
            buf[pl.ds(start, H), :] = keep(lon_ok[m], lon[r * H:(r + 1) * H, :])
        for n in range(2):
            for r in range(H):
                part = own_rows + (n * H + r) * H
                start = OFF + (lat_row[n] + r) * CB + 4 + lon_col[m]
                buf[pl.ds(start, H), :] = keep(lat_ok[n], keep(lon_ok[m], lon[part:part + H, :]))


def put_own_kappa(kap, act, counts, kappa_ref):
    kap_t = kappa_ref[...].T
    for r in range(R):
        kap[pl.ds(at(r + H, 8), C), :] = jnp.broadcast_to(kap_t[:, r:r + 1], (C, K))
        for s in range(SWEEPS):
            act[s, r + H] = jnp.full((8, K), jnp.where(counts[r] > s, 1.0, 0.0), jnp.float32)


def put_lat_kappa(kap, act, flags, tail_a, tail_b):
    odd = flags[0]
    lat_ok = (None, flags[1] == 1)
    lat_row = (jnp.where(odd == 1, 0, R + H), jnp.where(odd == 1, R + H, 0))
    for n, lat in ((0, tail_a), (1, tail_b)):
        turned = lat[:8, :].T
        if n == 1:
            turned = jnp.where(lat_ok[1], turned, 0.0)
        for r in range(H):
            for h in range(2):
                start = pl.multiple_of(OFF + (lat_row[n] + r) * CB + 8 + h * LANES, 8)
                kap[pl.ds(start, LANES), :] = jnp.broadcast_to(turned[:, 2 * r + h:2 * r + h + 1], (LANES, K))
            wide = jnp.broadcast_to(lat[8 + r:9 + r, :], (8, K))
            for s in range(SWEEPS):
                act[s, lat_row[n] + r] = jnp.where(wide > s, 1.0, 0.0)


def put_lon_kappa(kap, flags, lon_a, lon_b):
    odd = flags[0]
    lon_odd = flags[2]
    lat_ok = (None, flags[1] == 1)
    lat_row = (jnp.where(odd == 1, 0, R + H), jnp.where(odd == 1, R + H, 0))
    lon_col = (jnp.where(lon_odd == 1, 0, C + H), jnp.where(lon_odd == 1, C + H, 0))
    for m, lon in ((0, lon_a), (1, lon_b)):
        src = (jnp.where(lon_odd == 1, LANES - H, 0), jnp.where(lon_odd == 1, 0, LANES - H))[m]
        own = lon[R * H:R * H + R, :].T
        tail = lon[OWN_ROWS + 2 * H * H:, :].T
        low, high = own[:H, :], own[LANES - H:, :]
        edge = jnp.where(src == 0, low, high)
        tail = jnp.where(src == 0, tail[:H, :], tail[LANES - H:, :])
        if m == 1:
            edge = jnp.where(flags[3] == 1, edge, 0.0)
            tail = jnp.where(flags[3] == 1, tail, 0.0)
        for r in range(R):
            kap[pl.ds(at(r + H, 4) + lon_col[m], H), :] = jnp.broadcast_to(edge[:, r:r + 1], (H, K))
        for n in range(2):
            for r in range(H):
                part = jnp.broadcast_to(tail[:, n * H + r:n * H + r + 1], (H, K))
                if n == 1:
                    part = jnp.where(lat_ok[1], part, 0.0)
                kap[pl.ds(OFF + (lat_row[n] + r) * CB + 4 + lon_col[m], H), :] = part


def relax(src, dst, kap, act, s, r, tiles):
    base = pl.multiple_of(r * CB, 8)
    a0 = act[s, r]
    a1 = act[s, r + 1]
    for t in tiles:
        o = base + OFF + t * 8
        up = src[pl.ds(o - CB, 8), :]
        c0 = src[pl.ds(o, 8), :]
        c1 = src[pl.ds(o + CB, 8), :]
        dn = src[pl.ds(o + 2 * CB, 8), :]
        l0 = src[pl.ds(o - 1, 8), :]
        r0 = src[pl.ds(o + 1, 8), :]
        l1 = src[pl.ds(o + CB - 1, 8), :]
        r1 = src[pl.ds(o + CB + 1, 8), :]
        lap0 = (up + c1) + (l0 + r0) - 4.0 * c0
        lap1 = (c0 + dn) + (l1 + r1) - 4.0 * c1
        dst[pl.ds(o, 8), :] = c0 + (a0 * kap[pl.ds(o, 8), :]) * lap0
        dst[pl.ds(o + CB, 8), :] = c1 + (a1 * kap[pl.ds(o + CB, 8), :]) * lap1


INNER = tuple(range(1, CB // 8 - 1))
EDGE = (0, 1, CB // 8 - 2, CB // 8 - 1)


def inner_kernel(ext, kap, act, *levels):
    src = ext
    for s in range(SWEEPS):
        t = s + 1

        def body(i, _):
            relax(src, levels[s], kap, act, s, t + H + 2 * i, INNER)
            return 0

        lax.fori_loop(0, (R - 2 * t) // 2, body, 0)
        src = levels[s]


def inner(ext, kap, act):
    return pl.pallas_call(
        inner_kernel,
        in_specs=[vmem_spec()] * 3,
        out_specs=[vmem_spec()] * SWEEPS,
        out_shape=[held(NROW + 16, K)] * SWEEPS,
        compiler_params=pltpu.CompilerParams(vmem_limit_bytes=2 * 1024 * 1024),
        cost_estimate=pl.CostEstimate(flops=0, bytes_accessed=16 * 1024 * 1024, transcendentals=0),
        name="inner",
    )(*in_vmem(ext, kap, act))


def outer(levels, kap, act):
    for s in range(SWEEPS):
        t = s + 1
        tiles = INNER if t == SWEEPS else tuple(range(CB // 8))
        sides = tuple(c for c in EDGE if c in tiles)

        def ends(i, _):
            relax(levels[s], levels[t], kap, act, s, jnp.where(i < 2, t + 2 * i, R + H - t + 2 * i - 4), tiles)
            return 0

        def middle(i, _):
            relax(levels[s], levels[t], kap, act, s, t + H + 2 * i, sides)
            return 0

        lax.fori_loop(0, 4, ends, 0)
        lax.fori_loop(0, (R - 2 * t) // 2, middle, 0, unroll=2)


def coeffs_kernel(flags, counts, kappa_ref, after, *rest):
    *halos, kap, act = rest
    put_own_kappa(kap, act, counts, kappa_ref)
    if halos:
        put_lat_kappa(kap, act, flags, *halos[:2])
        put_lon_kappa(kap, flags, *halos[2:])


def coeffs(flags, counts, kappa, after, *halos):
    return pl.pallas_call(
        coeffs_kernel,
        in_specs=[smem_spec()] * 2 + [vmem_spec(), pl.BlockSpec(memory_space=pl.ANY)] + [vmem_spec()] * len(halos),
        out_specs=[vmem_spec()] * 2,
        out_shape=[held(NROW + 16, K), held(SWEEPS, RE, 8, K)],
        compiler_params=pltpu.CompilerParams(vmem_limit_bytes=8 * 1024 * 1024),
        cost_estimate=pl.CostEstimate(flops=0, bytes_accessed=4 * 1024 * 1024, transcendentals=0),
        name="coeffs",
    )(flags, counts, kappa, after, *halos)


def places_kernel(count_ref, cell_ref, owner_ref, after, row_ref, place_ref):
    count = count_ref[0]
    owner = owner_ref[...]
    cell = cell_ref[...]
    row_ref[...] = OFF + 8 + H * CB + (cell >> 8) * CB + (cell & (C - 1))
    owners = jnp.broadcast_to(owner, (SLOTS, SLOTS))
    later = lax.broadcasted_iota(jnp.int32, (SLOTS, SLOTS), 1)
    earlier = lax.broadcasted_iota(jnp.int32, (SLOTS, SLOTS), 0)
    column = jnp.broadcast_to(owner.astype(jnp.float32), (8, SLOTS)).T[:, :1].astype(jnp.int32)
    same = (owners == column) & (earlier < later)
    rank = jnp.sum(jnp.where(same, 1.0, 0.0), axis=0, keepdims=True).astype(jnp.int32)
    slot = lax.broadcasted_iota(jnp.int32, (1, SLOTS), 1)
    place_ref[...] = jnp.where(slot < count, owner * CAP + rank, PLACES)


def places(count, cell, owner, after):
    return pl.pallas_call(
        places_kernel,
        in_specs=[smem_spec()] + [vmem_spec()] * 2 + [pl.BlockSpec(memory_space=pl.ANY)],
        out_specs=[vmem_spec()] * 2,
        out_shape=[jax.ShapeDtypeStruct((1, SLOTS), jnp.int32)] * 2,
        cost_estimate=pl.CostEstimate(flops=0, bytes_accessed=4 * 1024 * 1024, transcendentals=0),
        compiler_params=pltpu.CompilerParams(vmem_limit_bytes=4 * 1024 * 1024),
        name="places",
    )(count, cell, owner, after)


def smooth_kernel(flags, cell_ref, place_ref, *refs):
    (ext_in, l1_in, l2_in, l3_in, l4_in, kap_in, act_in, lat_a, lat_b, lon_a, lon_b,
     out_ref, tail_a, tail_b, ext, l1, l2, l3, l4, kap, act, rows_ref) = refs
    tail_a[...] = lat_a[H * C:, :]
    tail_b[...] = lat_b[H * C:, :]
    put_lat_kappa(kap, act, flags, tail_a, tail_b)
    put_lon_kappa(kap, flags, lon_a, lon_b)
    put_halos(ext, flags, lat_a, lat_b, lon_a, lon_b)
    outer((ext, l1, l2, l3, l4), kap, act)
    rows_ref[...] = jnp.zeros_like(rows_ref)

    def copy(i, _):
        for j in range(8):
            t = i * 8 + j
            rows_ref[pl.ds(place_ref[0, t], 1), :] = l4[pl.ds(cell_ref[0, t], 1), :]
        return 0

    lax.fori_loop(0, SLOTS // 8, copy, 0)
    out_ref[...] = rows_ref[:PLACES]


def smooth(flags, cell, place, ext, levels, kap, act, halos):
    return pl.pallas_call(
        smooth_kernel,
        in_specs=[smem_spec()] * 3 + [vmem_spec()] * 11,
        out_specs=[vmem_spec()] * 10,
        out_shape=[f32(PLACES, K), f32(16, K), f32(16, K)] + [held(NROW + 16, K)] * 6 + [held(SWEEPS, RE, 8, K)],
        input_output_aliases={3 + i: 3 + i for i in range(7)},
        scratch_shapes=[pltpu.VMEM((PLACES + 8, K), jnp.float32)],
        compiler_params=pltpu.CompilerParams(vmem_limit_bytes=8 * 1024 * 1024),
        name="smooth",
    )(flags, cell, place, *in_vmem(ext, *levels, kap, act), *halos)[:3]


def weigh_kernel(b_ref, r_hbm, out_ref, r_ref, sems):
    width = PLACES // WEIGH_PARTS

    def copy(n):
        return pltpu.make_async_copy(r_hbm.at[:, pl.ds(n * width, width)], r_ref.at[n], sems.at[n])

    for n in range(WEIGH_PARTS):
        copy(n).start()
    b = b_ref[...].T
    high = b.astype(jnp.bfloat16)
    low = (b - high.astype(jnp.float32)).astype(jnp.bfloat16)
    both = jnp.concatenate([high, low], axis=0)
    for n in range(WEIGH_PARTS):
        copy(n).wait()
        r = r_ref[n]
        r_high = r.astype(jnp.bfloat16)
        r_low = (r - r_high.astype(jnp.float32)).astype(jnp.bfloat16)
        one = jnp.dot(both, r_high, preferred_element_type=jnp.float32)
        two = jnp.dot(high, r_low, preferred_element_type=jnp.float32)
        out_ref[n * width:(n + 1) * width, :] = (one[:K] + (one[K:] + two)).T


def weigh(buffer, r):
    return pl.pallas_call(
        weigh_kernel,
        in_specs=[vmem_spec(), hbm_spec()],
        out_specs=vmem_spec(),
        out_shape=f32(PLACES, K),
        scratch_shapes=[
            pltpu.VMEM((WEIGH_PARTS, PLACES, PLACES // WEIGH_PARTS), jnp.float32),
            pltpu.SemaphoreType.DMA((WEIGH_PARTS,)),
        ],
        compiler_params=pltpu.CompilerParams(vmem_limit_bytes=12 * 1024 * 1024),
        name="weigh",
    )(buffer, in_hbm(r))


def spread_kernel(flags, cell_ref, place_ref, count_ref, ret_ref, field, pay_a, pay_b, own_a, own_b):
    field[...] = jnp.zeros_like(field)

    count = count_ref[0]

    def add(i, _):
        rows, cells = [], []
        for j in range(8):
            t = i * 8 + j
            live = t < count
            rows.append(ret_ref[pl.ds(jnp.where(live, place_ref[0, t], 0), 1), :])
            cells.append(jnp.where(live, cell_ref[0, t], NROW + OFF))
        for row, cell in zip(rows, cells):
            field[pl.ds(cell, 1), :] = field[pl.ds(cell, 1), :] + row
        return 0

    lax.fori_loop(0, (count + 7) // 8, add, 0)
    odd = flags[0]
    lon_odd = flags[2]
    for pay, low in ((pay_a, odd), (pay_b, 1 - odd)):
        first = jnp.where(low == 1, H, R)
        for r in range(H):
            start = pl.multiple_of(OFF + (first + r) * CB + 8, 8)
            pay[r * C:(r + 1) * C, :] = field[pl.ds(start, C), :]
    for own, low in ((own_a, lon_odd), (own_b, 1 - lon_odd)):
        col = jnp.where(low == 1, 8, 4 + C)
        for r in range(R):
            own[r * H:(r + 1) * H, :] = field[pl.ds(at(r + H, 0) + col, H), :]


def spread(flags, cell, place, count, returned):
    return pl.pallas_call(
        spread_kernel,
        in_specs=[smem_spec()] * 4 + [vmem_spec()],
        out_specs=[vmem_spec()] * 5,
        out_shape=[held(NROW + 16, K), f32(H * C, K), f32(H * C, K), held(R * H, K), held(R * H, K)],
        compiler_params=pltpu.CompilerParams(vmem_limit_bytes=10 * 1024 * 1024),
        name="spread",
    )(flags, cell, place, count, returned)


def finish_kernel(flags, *refs):
    (ext_in, l1_in, l2_in, l3_in, l4_in, kap, act, lat_a, lat_b, lon_a, lon_b, p_hbm,
     out_hbm, gram_ref, ext, l1, l2, l3, l4, chunk, in_sems, out_sems) = refs

    def part(ref, n):
        half, block = n // 4, n % 4
        return ref.at[:, pl.ds(block * 8, 8), pl.ds(half * LANES, LANES)]

    def copy_in(n):
        return pltpu.make_async_copy(part(p_hbm, n), chunk.at[n], in_sems.at[n])

    def copy_out(n):
        return pltpu.make_async_copy(chunk.at[n], part(out_hbm, n), out_sems.at[n])

    for n in range(8):
        copy_in(n).start()
    put_halos(ext, flags, lat_a, lat_b, lon_a, lon_b)
    outer((ext, l1, l2, l3, l4), kap, act)
    flat = chunk.reshape(8 * K * 8, LANES)
    contract = (((1,), (1,)), ((), ()))
    hh = jnp.zeros((K, K), jnp.float32)
    hl = jnp.zeros((K, K), jnp.float32)
    for n in range(8):
        half, block = n // 4, n % 4
        copy_in(n).wait()
        for i in range(0, 8, 2):
            parts = []
            for j in range(2):
                where = pl.ds(n * K * 8 + i + j, K, stride=8)
                start = at(block * 8 + i + j + H, 8) + half * LANES
                sk = flat[where, :] + l4[pl.ds(start, LANES), :].T
                flat[where, :] = sk
                parts.append(sk)
            sk = jnp.concatenate(parts, axis=1)
            high = sk.astype(jnp.bfloat16)
            low = (sk - high.astype(jnp.float32)).astype(jnp.bfloat16)
            hh = hh + lax.dot_general(high, high, contract, preferred_element_type=jnp.float32)
            hl = hl + lax.dot_general(high, low, contract, preferred_element_type=jnp.float32)
        copy_out(n).start()
    gram = hh + (hl + hl.T)
    top = gram[:HALF]
    turned = pltpu.roll(gram[HALF:], HALF, 1)
    row = lax.broadcasted_iota(jnp.int32, (HALF, K), 0)
    lane = lax.broadcasted_iota(jnp.int32, (HALF, K), 1)
    gram_ref[:HALF, :] = jnp.where((lane < HALF) & (row > lane), turned, top)
    gram_ref[HALF:, :] = jnp.broadcast_to(jnp.sum(jnp.where(row == lane, turned, 0.0), axis=0, keepdims=True), (8, K))
    for n in range(8):
        copy_out(n).wait()


def finish(flags, ext, levels, kap, act, halos, probes):
    return pl.pallas_call(
        finish_kernel,
        in_specs=[smem_spec()] + [vmem_spec()] * 11 + [hbm_spec()],
        out_specs=[hbm_spec()] + [vmem_spec()] * 6,
        out_shape=[f32(K, R, C), f32(HALF + 8, K)] + [held(NROW + 16, K)] * 5,
        input_output_aliases={1 + i: 2 + i for i in range(5)},
        scratch_shapes=[
            pltpu.VMEM((8, K, 8, LANES), jnp.float32),
            pltpu.SemaphoreType.DMA((8,)),
            pltpu.SemaphoreType.DMA((8,)),
        ],
        compiler_params=pltpu.CompilerParams(vmem_limit_bytes=12 * 1024 * 1024),
        name="finish",
    )(flags, *in_vmem(ext, *levels, kap, act), *halos, in_hbm(probes))[:2]


def pairs(size, first):
    return [(i, (i + 1) % size if (i - first) % 2 == 0 else (i - 1) % size) for i in range(size)]


def swap(a, b, axis):
    size = lax.axis_size(axis)
    return lax.ppermute(a, axis, pairs(size, 0)), lax.ppermute(b, axis, pairs(size, 1))


def factor_kernel(scale, x_ref, g1_ref, g2_ref, g3_ref, out_ref, a_ref):
    total = ((x_ref[...] + g1_ref[...]) + (g2_ref[...] + g3_ref[...])) * scale
    top = total[:HALF]
    a_ref[:HALF, :] = top
    lower = top.T[:HALF]
    row = lax.broadcasted_iota(jnp.int32, (HALF, HALF), 0)
    lane = lax.broadcasted_iota(jnp.int32, (HALF, HALF), 1)
    lower = jnp.where(row == lane, jnp.broadcast_to(total[HALF:HALF + 1, :HALF], (HALF, HALF)), lower)
    a_ref[HALF:, :] = jnp.concatenate([jnp.zeros((HALF, HALF), jnp.float32), lower], axis=1)
    sub = lax.broadcasted_iota(jnp.int32, (8, K), 0)
    col = lax.broadcasted_iota(jnp.int32, (8, K), 1)
    wide = lambda x: jnp.broadcast_to(x, (8, K))
    panels, last = [], None
    for q in range(K // 8):
        c = 8 * q
        panel = a_ref[c:c + 8, :]
        if q > 1:
            done = jnp.concatenate(panels[:q - 1], axis=0)
            panel = panel - lax.dot_general(
                done[:, c:c + 8], done, (((0,), (0,)), ((), ())),
                precision=lax.Precision.HIGHEST, preferred_element_type=jnp.float32)
        b = {(i, m): wide(panel[i:i + 1, c + m:c + m + 1]) for i in range(8) for m in range(i, 8)}
        rows = [wide(panel[i:i + 1, :]) for i in range(8)]
        if q > 0:
            for k in range(8):
                e = [wide(last[k][:, c + m:c + m + 1]) for m in range(8)]
                for i in range(8):
                    for m in range(i, 8):
                        b[i, m] = b[i, m] - e[i] * e[m]
                    rows[i] = rows[i] - e[i] * last[k]
        result = jnp.zeros((8, K), jnp.float32)
        for i in range(8):
            inv = lax.rsqrt(b[i, i])
            u = {m: b[i, m] * inv for m in range(i + 1, 8)}
            for m in range(i + 1, 8):
                for k in range(m, 8):
                    b[m, k] = b[m, k] - u[m] * u[k]
            rows[i] = rows[i] * inv
            for m in range(i + 1, 8):
                rows[m] = rows[m] - u[m] * rows[i]
            result = jnp.where(sub == i, rows[i], result)
        last = rows
        panels.append(result)
        out_ref[c:c + 8, :] = jnp.where(col >= sub + c, result, 0.0)


def factor(scale, parts):
    return pl.pallas_call(
        functools.partial(factor_kernel, scale),
        in_specs=[vmem_spec()] * 4,
        out_specs=vmem_spec(),
        out_shape=f32(K, K),
        scratch_shapes=[pltpu.VMEM((K, K), jnp.float32)],
        compiler_params=pltpu.CompilerParams(vmem_limit_bytes=8 * 1024 * 1024),
        name="factor",
    )(*parts)


def gather_sums(x):
    def stage(x, axis, steps):
        size = lax.axis_size(axis)
        return (x, *[lax.ppermute(x, axis, [(i, i ^ d) for i in range(size)]) for d in steps])

    def total(x, g1, g2, g3):
        return (x + g1) + (g2 + g3)

    x, g1 = stage(x, "lat", (1,))
    x = total(*stage(x + g1, "lat", (2, 4, 6)))
    x = total(*stage(x, "lon", (1, 2, 3)))
    return stage(x, "lon", (4, 8, 12))


def shards(probes, kappa, sweep_counts, obs_cell, obs_owner, obs_count, r_inv):
    n_lat, n_lon = lax.axis_size("lat"), lax.axis_size("lon")
    lat, lon = lax.axis_index("lat"), lax.axis_index("lon")
    flags = jnp.stack([
        lat % 2, ((lat > 0) & (lat < n_lat - 1)).astype(jnp.int32),
        lon % 2, ((lon > 0) & (lon < n_lon - 1)).astype(jnp.int32),
    ]).astype(jnp.int32)
    lat_a, lat_b = swap(*edge_pack(sweep_counts, kappa, probes), "lat")
    ext, own_a, own_b = turn(flags, kappa, probes)
    kap, act = coeffs(flags, sweep_counts, kappa, own_a)
    levels = inner(ext, kap, act)
    count = obs_count.reshape(1)
    lon_pay = corner(flags, own_a, own_b, lat_a, lat_b, levels[-1])
    cell, place = places(count, obs_cell.reshape(1, SLOTS), obs_owner.reshape(1, SLOTS), lon_pay[0])
    lon_a, lon_b = swap(*lon_pay, "lon")
    outgoing, tail_a, tail_b = smooth(flags, cell, place, ext, levels, kap, act, (lat_a, lat_b, lon_a, lon_b))
    buffer = lax.all_to_all(outgoing, "lon", split_axis=0, concat_axis=0, tiled=True)
    mixed = weigh(buffer, r_inv[0, 0])
    returned = lax.all_to_all(mixed, "lon", split_axis=0, concat_axis=0, tiled=True)
    field, pay_a, pay_b, own_a, own_b = spread(flags, cell, place, count, returned)
    kap, act = coeffs(flags, sweep_counts, kappa, pay_a, tail_a, tail_b, lon_a, lon_b)
    levels = inner(field, kap, act)
    lat_a, lat_b = swap(pay_a, pay_b, "lat")
    back = (lat_a, lat_b) + swap(*corner(flags, own_a, own_b, lat_a, lat_b, levels[-1]), "lon")
    sketch, gram = finish(flags, field, levels, kap, act, back, probes)
    cells_all = R * C * n_lat * n_lon
    r_factor = factor(1.0 / cells_all, gather_sums(gram))
    return (sketch, r_factor)


def solution(mesh):
    return jax.shard_map(
        shards,
        mesh=mesh,
        in_specs=(
            P(None, "lat", "lon"),
            P("lat", "lon"),
            P("lat"),
            P(("lat", "lon")),
            P(("lat", "lon"), None),
            P("lat", "lon"),
            P("lat", "lon", None, None),
        ),
        out_specs=(P(None, "lat", "lon"), P()),
        check_vma=False,
    )
```

```python
import functools

import jax
import jax.numpy as jnp
from jax import lax
from jax.experimental import pallas as pl
from jax.experimental.pallas import tpu as pltpu
from jax.sharding import PartitionSpec as P

SWEEPS = 4
CAP = 48
K = 128
R = 32
C = 256
H = 4
RE = R + 2 * H
CB = C + 16
NROW = RE * CB
OFF = 8
SLOTS = 384
PLACES = 768
LANES = 128
VMEM_LIMIT = 30 * 1024 * 1024
LAT_ROWS = H * C + 16
OWN_ROWS = R * H + R
WEIGH_PARTS = 3
HALF = 64


def vmem_spec():
    return pl.BlockSpec(memory_space=pltpu.VMEM)


def smem_spec():
    return pl.BlockSpec(memory_space=pltpu.SMEM)


def hbm_spec():
    return pl.BlockSpec(memory_space=pltpu.HBM)


def params():
    return pltpu.CompilerParams(vmem_limit_bytes=VMEM_LIMIT)


def f32(*shape):
    return jax.ShapeDtypeStruct(shape, jnp.float32)


def held(*shape):
    return pltpu.VMEM(shape, jnp.float32)


def in_vmem(*arrays):
    return tuple(pltpu.with_memory_space_constraint(a, pltpu.VMEM) for a in arrays)


def in_hbm(array):
    return pltpu.with_memory_space_constraint(array, pltpu.HBM)


def at(r, c):
    return OFF + r * CB + c


def edge_pack_kernel(counts_hbm, kappa_hbm, p_hbm, pay_a, pay_b, chunk, kappa_ref, counts, sems):
    odd = lax.axis_index("lat") % 2
    first = (jnp.where(odd == 1, 0, R - H), jnp.where(odd == 1, R - H, 0))
    copies = []
    for side in range(2):
        block = pl.multiple_of(jnp.where(first[side] == 0, 0, R - 8), 8)
        for half in range(2):
            n = side * 2 + half
            copies.append(pltpu.make_async_copy(
                p_hbm.at[:, pl.ds(block, 8), pl.ds(half * LANES, LANES)], chunk.at[n], sems.at[n]))
    small = [pltpu.make_async_copy(kappa_hbm, kappa_ref, sems.at[4]),
             pltpu.make_async_copy(counts_hbm, counts, sems.at[5])]
    for copy in small + copies:
        copy.start()
    for copy in small:
        copy.wait()
    flat = chunk.reshape(4 * K * 8, LANES)
    for side, pay in ((0, pay_a), (1, pay_b)):
        within = jnp.where(first[side] == 0, 0, 8 - H)
        for r in range(H):
            for half in range(2):
                lanes = slice(half * LANES, (half + 1) * LANES)
                pay[H * C + 2 * r + half:H * C + 2 * r + half + 1, :] = jnp.where(
                    first[side] == 0, kappa_ref[r:r + 1, lanes], kappa_ref[R - H + r:R - H + r + 1, lanes])
            value = counts[first[side] + r].astype(jnp.float32)
            pay[H * C + 8 + r:H * C + 9 + r, :] = jnp.full((1, K), value, jnp.float32)
        pay[H * C + 8 + H:, :] = jnp.zeros((4, K), jnp.float32)
        for half in range(2):
            n = side * 2 + half
            copies[n].wait()
            for r in range(H):
                pay[r * C + half * LANES:r * C + (half + 1) * LANES, :] = flat[
                    pl.ds(n * K * 8 + within + r, K, stride=8), :].T


def edge_pack(counts, kappa, probes):
    return pl.pallas_call(
        edge_pack_kernel,
        in_specs=[hbm_spec()] * 3,
        out_specs=[vmem_spec()] * 2,
        out_shape=[f32(LAT_ROWS, K)] * 2,
        scratch_shapes=[
            pltpu.VMEM((4, K, 8, LANES), jnp.float32),
            pltpu.VMEM((R, C), jnp.float32),
            pltpu.SMEM((R,), jnp.int32),
            pltpu.SemaphoreType.DMA((6,)),
        ],
        compiler_params=pltpu.CompilerParams(vmem_limit_bytes=8 * 1024 * 1024),
        name="edge_pack",
    )(in_hbm(counts), in_hbm(kappa), in_hbm(probes))


def turn_kernel(flags, kappa_ref, p_hbm, ext, own_a, own_b, chunk, sems):
    def copy(n):
        half, block = n // 4, n % 4
        return pltpu.make_async_copy(
            p_hbm.at[:, pl.ds(block * 8, 8), pl.ds(half * LANES, LANES)], chunk.at[n], sems.at[n])

    for n in range(8):
        copy(n).start()
    flat = chunk.reshape(8 * K * 8, LANES)
    for n in range(8):
        copy(n).wait()
        half, block = n // 4, n % 4
        for i in range(8):
            r = block * 8 + i
            ext[pl.ds(at(r + H, 8) + half * LANES, LANES), :] = flat[pl.ds(n * K * 8 + i, K, stride=8), :].T
    odd = flags[2]
    for own, low in ((own_a, odd), (own_b, 1 - odd)):
        col = jnp.where(low == 1, 0, C - H)
        lane = pl.multiple_of(jnp.where(low == 1, 0, LANES), LANES)
        for r in range(R):
            own[r * H:(r + 1) * H, :] = ext[pl.ds(at(r + H, 8) + col, H), :]
        own[R * H:, :] = kappa_ref[:, pl.ds(lane, LANES)]


def turn(flags, kappa, probes):
    return pl.pallas_call(
        turn_kernel,
        in_specs=[smem_spec(), vmem_spec(), hbm_spec()],
        out_specs=[vmem_spec()] * 3,
        out_shape=[held(NROW + 16, K), held(OWN_ROWS, K), held(OWN_ROWS, K)],
        scratch_shapes=[pltpu.VMEM((8, K, 8, LANES), jnp.float32), pltpu.SemaphoreType.DMA((8,))],
        compiler_params=pltpu.CompilerParams(vmem_limit_bytes=6 * 1024 * 1024),
        cost_estimate=pl.CostEstimate(flops=0, bytes_accessed=12 * 1024 * 1024, transcendentals=0),
        name="turn",
    )(flags, kappa, in_hbm(probes))


def corner_kernel(flags, own_a, own_b, lat_a, lat_b, after, pay_a, pay_b):
    odd = flags[2]
    own_rows = own_a.shape[0]
    for own, pay, low in ((own_a, pay_a, odd), (own_b, pay_b, 1 - odd)):
        col = jnp.where(low == 1, 0, C - H)
        pay[:own_rows, :] = own[...]
        base = own_rows
        for lat in (lat_a, lat_b):
            for r in range(H):
                pay[base:base + H, :] = lat[pl.ds(r * C + col, H), :]
                base += H
        if own_rows > R * H:
            for lat in (lat_a, lat_b):
                for r in range(H):
                    pay[base:base + 1, :] = lat[pl.ds(H * C + 2 * r + 1 - low, 1), :]
                    base += 1


def corner(flags, own_a, own_b, lat_a, lat_b, after):
    rows = own_a.shape[0] + 2 * H * H + (2 * H if own_a.shape[0] > R * H else 0)
    return pl.pallas_call(
        corner_kernel,
        in_specs=[smem_spec()] + [vmem_spec()] * 4 + [pl.BlockSpec(memory_space=pl.ANY)],
        out_specs=[vmem_spec()] * 2,
        out_shape=[f32(rows, K)] * 2,
        compiler_params=pltpu.CompilerParams(vmem_limit_bytes=2 * 1024 * 1024),
        name="corner",
    )(flags, *in_vmem(own_a, own_b), lat_a, lat_b, after)


def keep(ok, x):
    return x if ok is None else jnp.where(ok, x, 0.0)


def put_lat_halos(buf, flags, lat_a, lat_b):
    odd = flags[0]
    lat_ok = (None, flags[1] == 1)
    lat_row = (jnp.where(odd == 1, 0, R + H), jnp.where(odd == 1, R + H, 0))
    for n, lat in ((0, lat_a), (1, lat_b)):
        for r in range(H):
            start = pl.multiple_of(OFF + (lat_row[n] + r) * CB + 8, 8)
            buf[pl.ds(start, C), :] = keep(lat_ok[n], lat[r * C:(r + 1) * C, :])


def put_lon_halos(buf, flags, lon_a, lon_b):
    odd = flags[0]
    lon_odd = flags[2]
    lat_ok = (None, flags[1] == 1)
    lon_ok = (None, flags[3] == 1)
    lat_row = (jnp.where(odd == 1, 0, R + H), jnp.where(odd == 1, R + H, 0))
    lon_col = (jnp.where(lon_odd == 1, 0, C + H), jnp.where(lon_odd == 1, C + H, 0))
    own_rows = R * H if lon_a.shape[0] == R * H + 2 * H * H else OWN_ROWS
    for m, lon in ((0, lon_a), (1, lon_b)):
        for r in range(R):
            start = at(r + H, 4) + lon_col[m]
            buf[pl.ds(start, H), :] = keep(lon_ok[m], lon[r * H:(r + 1) * H, :])
        for n in range(2):
            for r in range(H):
                part = own_rows + (n * H + r) * H
                start = OFF + (lat_row[n] + r) * CB + 4 + lon_col[m]
                buf[pl.ds(start, H), :] = keep(lat_ok[n], keep(lon_ok[m], lon[part:part + H, :]))


def put_own_kappa(kap, act, counts, kappa_ref):
    kap_t = kappa_ref[...].T
    for r in range(R):
        kap[pl.ds(at(r + H, 8), C), :] = jnp.broadcast_to(kap_t[:, r:r + 1], (C, K))
        for s in range(SWEEPS):
            act[s, r + H] = jnp.full((8, K), jnp.where(counts[r] > s, 1.0, 0.0), jnp.float32)


def put_lat_kappa(kap, act, flags, tail_a, tail_b):
    odd = flags[0]
    lat_ok = (None, flags[1] == 1)
    lat_row = (jnp.where(odd == 1, 0, R + H), jnp.where(odd == 1, R + H, 0))
    for n, lat in ((0, tail_a), (1, tail_b)):
        turned = lat[:8, :].T
        if n == 1:
            turned = jnp.where(lat_ok[1], turned, 0.0)
        for r in range(H):
            for h in range(2):
                start = pl.multiple_of(OFF + (lat_row[n] + r) * CB + 8 + h * LANES, 8)
                kap[pl.ds(start, LANES), :] = jnp.broadcast_to(turned[:, 2 * r + h:2 * r + h + 1], (LANES, K))
            wide = jnp.broadcast_to(lat[8 + r:9 + r, :], (8, K))
            for s in range(SWEEPS):
                act[s, lat_row[n] + r] = jnp.where(wide > s, 1.0, 0.0)


def put_lon_kappa(kap, flags, lon_a, lon_b):
    odd = flags[0]
    lon_odd = flags[2]
    lat_ok = (None, flags[1] == 1)
    lat_row = (jnp.where(odd == 1, 0, R + H), jnp.where(odd == 1, R + H, 0))
    lon_col = (jnp.where(lon_odd == 1, 0, C + H), jnp.where(lon_odd == 1, C + H, 0))
    for m, lon in ((0, lon_a), (1, lon_b)):
        src = (jnp.where(lon_odd == 1, LANES - H, 0), jnp.where(lon_odd == 1, 0, LANES - H))[m]
        own = lon[R * H:R * H + R, :].T
        tail = lon[OWN_ROWS + 2 * H * H:, :].T
        low, high = own[:H, :], own[LANES - H:, :]
        edge = jnp.where(src == 0, low, high)
        tail = jnp.where(src == 0, tail[:H, :], tail[LANES - H:, :])
        if m == 1:
            edge = jnp.where(flags[3] == 1, edge, 0.0)
            tail = jnp.where(flags[3] == 1, tail, 0.0)
        for r in range(R):
            kap[pl.ds(at(r + H, 4) + lon_col[m], H), :] = jnp.broadcast_to(edge[:, r:r + 1], (H, K))
        for n in range(2):
            for r in range(H):
                part = jnp.broadcast_to(tail[:, n * H + r:n * H + r + 1], (H, K))
                if n == 1:
                    part = jnp.where(lat_ok[1], part, 0.0)
                kap[pl.ds(OFF + (lat_row[n] + r) * CB + 4 + lon_col[m], H), :] = part


def relax(src, dst, kap, act, s, r, tiles):
    base = pl.multiple_of(r * CB, 8)
    a0 = act[s, r]
    a1 = act[s, r + 1]
    for t in tiles:
        o = base + OFF + t * 8
        up = src[pl.ds(o - CB, 8), :]
        c0 = src[pl.ds(o, 8), :]
        c1 = src[pl.ds(o + CB, 8), :]
        dn = src[pl.ds(o + 2 * CB, 8), :]
        l0 = src[pl.ds(o - 1, 8), :]
        r0 = src[pl.ds(o + 1, 8), :]
        l1 = src[pl.ds(o + CB - 1, 8), :]
        r1 = src[pl.ds(o + CB + 1, 8), :]
        lap0 = (up + c1) + (l0 + r0) - 4.0 * c0
        lap1 = (c0 + dn) + (l1 + r1) - 4.0 * c1
        dst[pl.ds(o, 8), :] = c0 + (a0 * kap[pl.ds(o, 8), :]) * lap0
        dst[pl.ds(o + CB, 8), :] = c1 + (a1 * kap[pl.ds(o + CB, 8), :]) * lap1


INNER = tuple(range(1, CB // 8 - 1))
EDGE = (0, 1, CB // 8 - 2, CB // 8 - 1)


def inner_kernel(ext, kap, act, *levels):
    src = ext
    for s in range(SWEEPS):
        t = s + 1

        def body(i, _):
            relax(src, levels[s], kap, act, s, t + H + 2 * i, INNER)
            return 0

        lax.fori_loop(0, (R - 2 * t) // 2, body, 0)
        src = levels[s]


def inner(ext, kap, act):
    return pl.pallas_call(
        inner_kernel,
        in_specs=[vmem_spec()] * 3,
        out_specs=[vmem_spec()] * SWEEPS,
        out_shape=[held(NROW + 16, K)] * SWEEPS,
        compiler_params=pltpu.CompilerParams(vmem_limit_bytes=1024 * 1024),
        cost_estimate=pl.CostEstimate(flops=0, bytes_accessed=16 * 1024 * 1024, transcendentals=0),
        name="inner",
    )(*in_vmem(ext, kap, act))


def sweep_ends(levels, kap, act):
    for s in range(SWEEPS):
        t = s + 1

        def ends(i, _):
            relax(levels[s], levels[t], kap, act, s, jnp.where(i < 2, t + 2 * i, R + H - t + 2 * i - 4), INNER)
            return 0

        lax.fori_loop(0, 4, ends, 0)


def sweep_sides(levels, kap, act):
    for s in range(SWEEPS):
        t = s + 1
        sides = EDGE[1:3] if t == SWEEPS else EDGE

        def body(i, _):
            relax(levels[s], levels[t], kap, act, s, t + 2 * i, sides)
            return 0

        lax.fori_loop(0, (RE - 2 * t) // 2, body, 0, unroll=2)


def ends_kernel(flags, *refs):
    (ext_in, l1_in, l2_in, l3_in, l4_in, kap_in, act_in, lat_a, lat_b, after,
     tail_a, tail_b, ext, l1, l2, l3, l4, kap, act) = refs
    tail_a[...] = lat_a[H * C:, :]
    tail_b[...] = lat_b[H * C:, :]
    put_lat_kappa(kap, act, flags, tail_a, tail_b)
    put_lat_halos(ext, flags, lat_a, lat_b)
    sweep_ends((ext, l1, l2, l3, l4), kap, act)


def ends(flags, ext, levels, kap, act, lat, after):
    tail_a, tail_b, ext, *levels, kap, act = pl.pallas_call(
        ends_kernel,
        in_specs=[smem_spec()] + [vmem_spec()] * 9 + [pl.BlockSpec(memory_space=pl.ANY)],
        out_specs=[vmem_spec()] * 9,
        out_shape=[f32(16, K), f32(16, K)] + [held(NROW + 16, K)] * 6 + [held(SWEEPS, RE, 8, K)],
        input_output_aliases={1 + i: 2 + i for i in range(7)},
        compiler_params=pltpu.CompilerParams(vmem_limit_bytes=2 * 1024 * 1024),
        cost_estimate=pl.CostEstimate(flops=0, bytes_accessed=8 * 1024 * 1024, transcendentals=0),
        name="ends",
    )(flags, *in_vmem(ext, *levels, kap, act), *lat, after)
    return tail_a, tail_b, ext, levels, kap, act


def coeffs_kernel(flags, counts, kappa_ref, after, *rest):
    *halos, kap, act = rest
    put_own_kappa(kap, act, counts, kappa_ref)
    if halos:
        put_lat_kappa(kap, act, flags, *halos[:2])
        put_lon_kappa(kap, flags, *halos[2:])


def coeffs(flags, counts, kappa, after, *halos):
    return pl.pallas_call(
        coeffs_kernel,
        in_specs=[smem_spec()] * 2 + [vmem_spec(), pl.BlockSpec(memory_space=pl.ANY)] + [vmem_spec()] * len(halos),
        out_specs=[vmem_spec()] * 2,
        out_shape=[held(NROW + 16, K), held(SWEEPS, RE, 8, K)],
        compiler_params=pltpu.CompilerParams(vmem_limit_bytes=1024 * 1024),
        cost_estimate=pl.CostEstimate(flops=0, bytes_accessed=4 * 1024 * 1024, transcendentals=0),
        name="coeffs",
    )(flags, counts, kappa, after, *halos)


def places_kernel(count_ref, cell_ref, owner_ref, after, row_ref, place_ref):
    count = count_ref[0]
    owner = owner_ref[...]
    cell = cell_ref[...]
    row_ref[...] = OFF + 8 + H * CB + (cell >> 8) * CB + (cell & (C - 1))
    owners = jnp.broadcast_to(owner, (SLOTS, SLOTS))
    later = lax.broadcasted_iota(jnp.int32, (SLOTS, SLOTS), 1)
    earlier = lax.broadcasted_iota(jnp.int32, (SLOTS, SLOTS), 0)
    column = jnp.broadcast_to(owner.astype(jnp.float32), (8, SLOTS)).T[:, :1].astype(jnp.int32)
    same = (owners == column) & (earlier < later)
    rank = jnp.sum(jnp.where(same, 1.0, 0.0), axis=0, keepdims=True).astype(jnp.int32)
    slot = lax.broadcasted_iota(jnp.int32, (1, SLOTS), 1)
    place_ref[...] = jnp.where(slot < count, owner * CAP + rank, PLACES)


def places(count, cell, owner, after):
    return pl.pallas_call(
        places_kernel,
        in_specs=[smem_spec()] + [vmem_spec()] * 2 + [pl.BlockSpec(memory_space=pl.ANY)],
        out_specs=[vmem_spec()] * 2,
        out_shape=[jax.ShapeDtypeStruct((1, SLOTS), jnp.int32)] * 2,
        cost_estimate=pl.CostEstimate(flops=0, bytes_accessed=4 * 1024 * 1024, transcendentals=0),
        compiler_params=pltpu.CompilerParams(vmem_limit_bytes=2 * 1024 * 1024),
        name="places",
    )(count, cell, owner, after)


def smooth_kernel(flags, cell_ref, place_ref, *refs):
    (ext_in, l1_in, l2_in, l3_in, l4_in, kap_in, act, lon_a, lon_b,
     out_ref, ext, l1, l2, l3, l4, kap, rows_ref) = refs
    put_lon_kappa(kap, flags, lon_a, lon_b)
    put_lon_halos(ext, flags, lon_a, lon_b)
    sweep_sides((ext, l1, l2, l3, l4), kap, act)
    rows_ref[...] = jnp.zeros_like(rows_ref)

    def copy(i, _):
        for j in range(8):
            t = i * 8 + j
            rows_ref[pl.ds(place_ref[0, t], 1), :] = l4[pl.ds(cell_ref[0, t], 1), :]
        return 0

    lax.fori_loop(0, SLOTS // 8, copy, 0)
    out_ref[...] = rows_ref[:PLACES]


def smooth(flags, cell, place, ext, levels, kap, act, lon):
    return pl.pallas_call(
        smooth_kernel,
        in_specs=[smem_spec()] * 3 + [vmem_spec()] * 9,
        out_specs=[vmem_spec()] * 7,
        out_shape=[f32(PLACES, K)] + [held(NROW + 16, K)] * 6,
        input_output_aliases={3 + i: 1 + i for i in range(6)},
        scratch_shapes=[pltpu.VMEM((PLACES + 8, K), jnp.float32)],
        compiler_params=pltpu.CompilerParams(vmem_limit_bytes=2 * 1024 * 1024),
        name="smooth",
    )(flags, cell, place, *in_vmem(ext, *levels, kap, act), *lon)[0]


def weigh_kernel(b_ref, r_hbm, out_ref, r_ref, sems):
    width = PLACES // WEIGH_PARTS

    def copy(n):
        return pltpu.make_async_copy(r_hbm.at[:, pl.ds(n * width, width)], r_ref.at[n], sems.at[n])

    for n in range(WEIGH_PARTS):
        copy(n).start()
    b = b_ref[...].T
    high = b.astype(jnp.bfloat16)
    low = (b - high.astype(jnp.float32)).astype(jnp.bfloat16)
    both = jnp.concatenate([high, low], axis=0)
    for n in range(WEIGH_PARTS):
        copy(n).wait()
        r = r_ref[n]
        r_high = r.astype(jnp.bfloat16)
        r_low = (r - r_high.astype(jnp.float32)).astype(jnp.bfloat16)
        one = jnp.dot(both, r_high, preferred_element_type=jnp.float32)
        two = jnp.dot(high, r_low, preferred_element_type=jnp.float32)
        out_ref[n * width:(n + 1) * width, :] = (one[:K] + (one[K:] + two)).T


def weigh(buffer, r):
    return pl.pallas_call(
        weigh_kernel,
        in_specs=[vmem_spec(), hbm_spec()],
        out_specs=vmem_spec(),
        out_shape=f32(PLACES, K),
        scratch_shapes=[
            pltpu.VMEM((WEIGH_PARTS, PLACES, PLACES // WEIGH_PARTS), jnp.float32),
            pltpu.SemaphoreType.DMA((WEIGH_PARTS,)),
        ],
        compiler_params=pltpu.CompilerParams(vmem_limit_bytes=6 * 1024 * 1024),
        name="weigh",
    )(buffer, in_hbm(r))


def spread_kernel(flags, cell_ref, place_ref, count_ref, ret_ref, field, pay_a, pay_b, own_a, own_b):
    field[...] = jnp.zeros_like(field)

    count = count_ref[0]

    def add(i, _):
        rows, cells = [], []
        for j in range(8):
            t = i * 8 + j
            live = t < count
            rows.append(ret_ref[pl.ds(jnp.where(live, place_ref[0, t], 0), 1), :])
            cells.append(jnp.where(live, cell_ref[0, t], NROW + OFF))
        for row, cell in zip(rows, cells):
            field[pl.ds(cell, 1), :] = field[pl.ds(cell, 1), :] + row
        return 0

    lax.fori_loop(0, (count + 7) // 8, add, 0)
    odd = flags[0]
    lon_odd = flags[2]
    for pay, low in ((pay_a, odd), (pay_b, 1 - odd)):
        first = jnp.where(low == 1, H, R)
        for r in range(H):
            start = pl.multiple_of(OFF + (first + r) * CB + 8, 8)
            pay[r * C:(r + 1) * C, :] = field[pl.ds(start, C), :]
    for own, low in ((own_a, lon_odd), (own_b, 1 - lon_odd)):
        col = jnp.where(low == 1, 8, 4 + C)
        for r in range(R):
            own[r * H:(r + 1) * H, :] = field[pl.ds(at(r + H, 0) + col, H), :]


def spread(flags, cell, place, count, returned):
    return pl.pallas_call(
        spread_kernel,
        in_specs=[smem_spec()] * 4 + [vmem_spec()],
        out_specs=[vmem_spec()] * 5,
        out_shape=[held(NROW + 16, K), f32(H * C, K), f32(H * C, K), held(R * H, K), held(R * H, K)],
        compiler_params=pltpu.CompilerParams(vmem_limit_bytes=2 * 1024 * 1024),
        name="spread",
    )(flags, cell, place, count, returned)


def gram_terms(sk):
    high = sk.astype(jnp.bfloat16)
    low = (sk - high.astype(jnp.float32)).astype(jnp.bfloat16)
    dot = lambda a, b: lax.dot_general(a, b, (((1,), (1,)), ((), ())), preferred_element_type=jnp.float32)
    return dot(high, high), dot(high, low)


def part(ref, n):
    half, block = n // 4, n % 4
    return ref.at[:, pl.ds(block * 8, 8), pl.ds(half * LANES, LANES)]


def bulk_kernel(flags, *refs):
    (ext_in, l1_in, l2_in, l3_in, l4_in, kap, act, lat_a, lat_b, after, p_hbm,
     ext, l1, l2, l3, l4, chunk, hh_ref, hl_ref, sems) = refs

    def copy_in(n):
        return pltpu.make_async_copy(part(p_hbm, n), chunk.at[n], sems.at[n])

    for n in range(8):
        copy_in(n).start()
    put_lat_halos(ext, flags, lat_a, lat_b)
    sweep_ends((ext, l1, l2, l3, l4), kap, act)
    flat = chunk.reshape(8 * K * 8, LANES)
    lane = lax.broadcasted_iota(jnp.int32, (K, LANES), 1)
    hh = jnp.zeros((K, K), jnp.float32)
    hl = jnp.zeros((K, K), jnp.float32)
    for n in range(8):
        half, block = n // 4, n % 4
        ready = lane >= 8 if half == 0 else lane < LANES - 8
        copy_in(n).wait()
        for i in range(0, 8, 2):
            parts = []
            for j in range(2):
                where = pl.ds(n * K * 8 + i + j, K, stride=8)
                start = at(block * 8 + i + j + H, 8) + half * LANES
                raw = flat[where, :]
                sk = raw + jnp.where(ready, l4[pl.ds(start, LANES), :].T, 0.0)
                flat[where, :] = sk
                parts.append(jnp.where(ready, sk, 0.0))
            one, two = gram_terms(jnp.concatenate(parts, axis=1))
            hh = hh + one
            hl = hl + two
    hh_ref[...] = hh
    hl_ref[...] = hl


def bulk(flags, ext, levels, kap, act, lat, after, probes):
    ext, *levels, chunk, hh, hl = pl.pallas_call(
        bulk_kernel,
        in_specs=[smem_spec()] + [vmem_spec()] * 9 + [pl.BlockSpec(memory_space=pl.ANY), hbm_spec()],
        out_specs=[vmem_spec()] * 8,
        out_shape=[held(NROW + 16, K)] * 5 + [held(8, K, 8, LANES), held(K, K), held(K, K)],
        input_output_aliases={1 + i: i for i in range(5)},
        scratch_shapes=[pltpu.SemaphoreType.DMA((8,))],
        compiler_params=pltpu.CompilerParams(vmem_limit_bytes=2 * 1024 * 1024),
        cost_estimate=pl.CostEstimate(flops=0, bytes_accessed=16 * 1024 * 1024, transcendentals=0),
        name="bulk",
    )(flags, *in_vmem(ext, *levels, kap, act), *lat, after, in_hbm(probes))
    return ext, levels, chunk, hh, hl


def finish_kernel(flags, *refs):
    (ext_in, l1_in, l2_in, l3_in, l4_in, kap, act, chunk_in, hh_ref, hl_ref, lon_a, lon_b,
     gram_ref, ext, l1, l2, l3, l4, chunk) = refs
    put_lon_halos(ext, flags, lon_a, lon_b)
    sweep_sides((ext, l1, l2, l3, l4), kap, act)
    flat = chunk.reshape(8 * K * 8, LANES)
    lane = lax.broadcasted_iota(jnp.int32, (K, LANES), 1)
    hh = hh_ref[...]
    hl = hl_ref[...]
    for block in range(4):
        tiles = []
        for i in range(8):
            r = block * 8 + i + H
            tiles += [l4[pl.ds(at(r, C), 8), :], l4[pl.ds(at(r, 8), 8), :]]
        turned = jnp.concatenate(tiles, axis=0).T
        for i in range(0, 8, 2):
            parts = []
            for j in range(2):
                moved = pltpu.roll(turned, (LANES - 16 * (i + j) - 8) % LANES, 1)
                first = pl.ds(block * K * 8 + i + j, K, stride=8)
                last = pl.ds((4 + block) * K * 8 + i + j, K, stride=8)
                a = flat[first, :] + jnp.where(lane < 8, moved, 0.0)
                b = flat[last, :] + jnp.where(lane >= LANES - 8, moved, 0.0)
                flat[first, :] = a
                flat[last, :] = b
                parts.append(jnp.where(lane < 8, a, jnp.where(lane >= LANES - 8, b, 0.0)))
            one, two = gram_terms(jnp.concatenate(parts, axis=1))
            hh = hh + one
            hl = hl + two
    gram = hh + (hl + hl.T)
    top = gram[:HALF]
    turned = pltpu.roll(gram[HALF:], HALF, 1)
    row = lax.broadcasted_iota(jnp.int32, (HALF, K), 0)
    lane = lax.broadcasted_iota(jnp.int32, (HALF, K), 1)
    gram_ref[:HALF, :] = jnp.where((lane < HALF) & (row > lane), turned, top)
    gram_ref[HALF:, :] = jnp.broadcast_to(jnp.sum(jnp.where(row == lane, turned, 0.0), axis=0, keepdims=True), (8, K))


def finish(flags, ext, levels, kap, act, chunk, hh, hl, lon):
    outs = pl.pallas_call(
        finish_kernel,
        in_specs=[smem_spec()] + [vmem_spec()] * 12,
        out_specs=[vmem_spec()] * 7,
        out_shape=[f32(HALF + 8, K)] + [held(NROW + 16, K)] * 5 + [held(8, K, 8, LANES)],
        input_output_aliases={**{1 + i: 1 + i for i in range(5)}, 8: 6},
        compiler_params=pltpu.CompilerParams(vmem_limit_bytes=3 * 1024 * 1024),
        name="finish",
    )(flags, *in_vmem(ext, *levels, kap, act, chunk, hh, hl), *lon)
    return outs[0], outs[6]


def store_kernel(chunk, after, out_hbm, sems):
    copies = [pltpu.make_async_copy(chunk.at[n], part(out_hbm, n), sems.at[n]) for n in range(8)]
    for copy in copies:
        copy.start()
    for copy in copies:
        copy.wait()


def store(chunk, after):
    return pl.pallas_call(
        store_kernel,
        in_specs=[vmem_spec(), pl.BlockSpec(memory_space=pl.ANY)],
        out_specs=hbm_spec(),
        out_shape=f32(K, R, C),
        scratch_shapes=[pltpu.SemaphoreType.DMA((8,))],
        compiler_params=pltpu.CompilerParams(vmem_limit_bytes=1024 * 1024),
        cost_estimate=pl.CostEstimate(flops=0, bytes_accessed=8 * 1024 * 1024, transcendentals=0),
        name="store",
    )(*in_vmem(chunk), after)


def pairs(size, first):
    return [(i, (i + 1) % size if (i - first) % 2 == 0 else (i - 1) % size) for i in range(size)]


def swap(a, b, axis):
    size = lax.axis_size(axis)
    return lax.ppermute(a, axis, pairs(size, 0)), lax.ppermute(b, axis, pairs(size, 1))


def factor_kernel(scale, x_ref, g1_ref, g2_ref, g3_ref, out_ref, a_ref):
    total = ((x_ref[...] + g1_ref[...]) + (g2_ref[...] + g3_ref[...])) * scale
    top = total[:HALF]
    a_ref[:HALF, :] = top
    lower = top.T[:HALF]
    row = lax.broadcasted_iota(jnp.int32, (HALF, HALF), 0)
    lane = lax.broadcasted_iota(jnp.int32, (HALF, HALF), 1)
    lower = jnp.where(row == lane, jnp.broadcast_to(total[HALF:HALF + 1, :HALF], (HALF, HALF)), lower)
    a_ref[HALF:, :] = jnp.concatenate([jnp.zeros((HALF, HALF), jnp.float32), lower], axis=1)
    sub = lax.broadcasted_iota(jnp.int32, (8, K), 0)
    col = lax.broadcasted_iota(jnp.int32, (8, K), 1)
    wide = lambda x: jnp.broadcast_to(x, (8, K))
    panels, last = [], None
    for q in range(K // 8):
        c = 8 * q
        panel = a_ref[c:c + 8, :]
        if q > 1:
            done = jnp.concatenate(panels[:q - 1], axis=0)
            panel = panel - lax.dot_general(
                done[:, c:c + 8], done, (((0,), (0,)), ((), ())),
                precision=lax.Precision.HIGHEST, preferred_element_type=jnp.float32)
        b = {(i, m): wide(panel[i:i + 1, c + m:c + m + 1]) for i in range(8) for m in range(i, 8)}
        rows = [wide(panel[i:i + 1, :]) for i in range(8)]
        if q > 0:
            for k in range(8):
                e = [wide(last[k][:, c + m:c + m + 1]) for m in range(8)]
                for i in range(8):
                    for m in range(i, 8):
                        b[i, m] = b[i, m] - e[i] * e[m]
                    rows[i] = rows[i] - e[i] * last[k]
        result = jnp.zeros((8, K), jnp.float32)
        for i in range(8):
            inv = lax.rsqrt(b[i, i])
            u = {m: b[i, m] * inv for m in range(i + 1, 8)}
            for m in range(i + 1, 8):
                for k in range(m, 8):
                    b[m, k] = b[m, k] - u[m] * u[k]
            rows[i] = rows[i] * inv
            for m in range(i + 1, 8):
                rows[m] = rows[m] - u[m] * rows[i]
            result = jnp.where(sub == i, rows[i], result)
        last = rows
        panels.append(result)
        out_ref[c:c + 8, :] = jnp.where(col >= sub + c, result, 0.0)


def factor(scale, parts):
    return pl.pallas_call(
        functools.partial(factor_kernel, scale),
        in_specs=[vmem_spec()] * 4,
        out_specs=vmem_spec(),
        out_shape=f32(K, K),
        scratch_shapes=[pltpu.VMEM((K, K), jnp.float32)],
        compiler_params=pltpu.CompilerParams(vmem_limit_bytes=8 * 1024 * 1024),
        name="factor",
    )(*parts)


def gather_sums(x):
    def stage(x, axis, steps):
        size = lax.axis_size(axis)
        return (x, *[lax.ppermute(x, axis, [(i, i ^ d) for i in range(size)]) for d in steps])

    def total(x, g1, g2, g3):
        return (x + g1) + (g2 + g3)

    x, g1 = stage(x, "lat", (1,))
    x = x + g1
    early = x
    x = total(*stage(x, "lat", (2, 4, 6)))
    x = total(*stage(x, "lon", (1, 2, 3)))
    return early, stage(x, "lon", (4, 8, 12))


def shards(probes, kappa, sweep_counts, obs_cell, obs_owner, obs_count, r_inv):
    n_lat, n_lon = lax.axis_size("lat"), lax.axis_size("lon")
    lat, lon = lax.axis_index("lat"), lax.axis_index("lon")
    flags = jnp.stack([
        lat % 2, ((lat > 0) & (lat < n_lat - 1)).astype(jnp.int32),
        lon % 2, ((lon > 0) & (lon < n_lon - 1)).astype(jnp.int32),
    ]).astype(jnp.int32)
    lat_a, lat_b = swap(*edge_pack(sweep_counts, kappa, probes), "lat")
    ext, own_a, own_b = turn(flags, kappa, probes)
    kap, act = coeffs(flags, sweep_counts, kappa, own_a)
    levels = inner(ext, kap, act)
    count = obs_count.reshape(1)
    lon_pay = corner(flags, own_a, own_b, lat_a, lat_b, levels[-1])
    cell, place = places(count, obs_cell.reshape(1, SLOTS), obs_owner.reshape(1, SLOTS), lon_pay[0])
    tail_a, tail_b, ext, levels, kap, act = ends(flags, ext, levels, kap, act, (lat_a, lat_b), lon_pay[0])
    lon_a, lon_b = swap(*lon_pay, "lon")
    outgoing = smooth(flags, cell, place, ext, levels, kap, act, (lon_a, lon_b))
    buffer = lax.all_to_all(outgoing, "lon", split_axis=0, concat_axis=0, tiled=True)
    mixed = weigh(buffer, r_inv[0, 0])
    returned = lax.all_to_all(mixed, "lon", split_axis=0, concat_axis=0, tiled=True)
    field, pay_a, pay_b, own_a, own_b = spread(flags, cell, place, count, returned)
    kap, act = coeffs(flags, sweep_counts, kappa, pay_a, tail_a, tail_b, lon_a, lon_b)
    levels = inner(field, kap, act)
    lat_a, lat_b = swap(pay_a, pay_b, "lat")
    lon_pay = corner(flags, own_a, own_b, lat_a, lat_b, levels[-1])
    field, levels, chunk, hh, hl = bulk(flags, field, levels, kap, act, (lat_a, lat_b), lon_pay[0], probes)
    gram, chunk = finish(flags, field, levels, kap, act, chunk, hh, hl, swap(*lon_pay, "lon"))
    early, parts = gather_sums(gram)
    sketch = store(chunk, early)
    cells_all = R * C * n_lat * n_lon
    r_factor = factor(1.0 / cells_all, parts)
    return (sketch, r_factor)


def solution(mesh):
    return jax.shard_map(
        shards,
        mesh=mesh,
        in_specs=(
            P(None, "lat", "lon"),
            P("lat", "lon"),
            P("lat"),
            P(("lat", "lon")),
            P(("lat", "lon"), None),
            P("lat", "lon"),
            P("lat", "lon", None, None),
        ),
        out_specs=(P(None, "lat", "lon"), P()),
        check_vma=False,
    )
```

```python
import functools

import jax
import jax.numpy as jnp
from jax import lax
from jax.experimental import pallas as pl
from jax.experimental.pallas import tpu as pltpu
from jax.sharding import PartitionSpec as P

SWEEPS = 4
CAP = 48
K = 128
R = 32
C = 256
H = 4
RE = R + 2 * H
CB = C + 16
NROW = RE * CB
OFF = 8
SLOTS = 384
PLACES = 768
LANES = 128
VMEM_LIMIT = 30 * 1024 * 1024
LAT_ROWS = H * C + 16
OWN_ROWS = R * H + R
WEIGH_PARTS = 3
HALF = 64


def vmem_spec():
    return pl.BlockSpec(memory_space=pltpu.VMEM)


def smem_spec():
    return pl.BlockSpec(memory_space=pltpu.SMEM)


def hbm_spec():
    return pl.BlockSpec(memory_space=pltpu.HBM)


def params():
    return pltpu.CompilerParams(vmem_limit_bytes=VMEM_LIMIT)


def f32(*shape):
    return jax.ShapeDtypeStruct(shape, jnp.float32)


def held(*shape):
    return pltpu.VMEM(shape, jnp.float32)


def in_vmem(*arrays):
    return tuple(pltpu.with_memory_space_constraint(a, pltpu.VMEM) for a in arrays)


def in_hbm(array):
    return pltpu.with_memory_space_constraint(array, pltpu.HBM)


def at(r, c):
    return OFF + r * CB + c


def edge_pack_kernel(counts_hbm, kappa_hbm, p_hbm, pay_a, pay_b, chunk, kappa_ref, counts, sems):
    odd = lax.axis_index("lat") % 2
    first = (jnp.where(odd == 1, 0, R - H), jnp.where(odd == 1, R - H, 0))
    copies = []
    for side in range(2):
        block = pl.multiple_of(jnp.where(first[side] == 0, 0, R - 8), 8)
        for half in range(2):
            n = side * 2 + half
            copies.append(pltpu.make_async_copy(
                p_hbm.at[:, pl.ds(block, 8), pl.ds(half * LANES, LANES)], chunk.at[n], sems.at[n]))
    small = [pltpu.make_async_copy(kappa_hbm, kappa_ref, sems.at[4]),
             pltpu.make_async_copy(counts_hbm, counts, sems.at[5])]
    for copy in small + copies:
        copy.start()
    for copy in small:
        copy.wait()
    flat = chunk.reshape(4 * K * 8, LANES)
    for side, pay in ((0, pay_a), (1, pay_b)):
        within = jnp.where(first[side] == 0, 0, 8 - H)
        for r in range(H):
            for half in range(2):
                lanes = slice(half * LANES, (half + 1) * LANES)
                pay[H * C + 2 * r + half:H * C + 2 * r + half + 1, :] = jnp.where(
                    first[side] == 0, kappa_ref[r:r + 1, lanes], kappa_ref[R - H + r:R - H + r + 1, lanes])
            value = counts[first[side] + r].astype(jnp.float32)
            pay[H * C + 8 + r:H * C + 9 + r, :] = jnp.full((1, K), value, jnp.float32)
        pay[H * C + 8 + H:, :] = jnp.zeros((4, K), jnp.float32)
        for half in range(2):
            n = side * 2 + half
            copies[n].wait()
            for r in range(H):
                pay[r * C + half * LANES:r * C + (half + 1) * LANES, :] = flat[
                    pl.ds(n * K * 8 + within + r, K, stride=8), :].T


def edge_pack(counts, kappa, probes):
    return pl.pallas_call(
        edge_pack_kernel,
        in_specs=[hbm_spec()] * 3,
        out_specs=[vmem_spec()] * 2,
        out_shape=[f32(LAT_ROWS, K)] * 2,
        scratch_shapes=[
            pltpu.VMEM((4, K, 8, LANES), jnp.float32),
            pltpu.VMEM((R, C), jnp.float32),
            pltpu.SMEM((R,), jnp.int32),
            pltpu.SemaphoreType.DMA((6,)),
        ],
        compiler_params=pltpu.CompilerParams(vmem_limit_bytes=8 * 1024 * 1024),
        name="edge_pack",
    )(in_hbm(counts), in_hbm(kappa), in_hbm(probes))


def turn_kernel(flags, p_hbm, ext, own_a, own_b, chunk, sems):
    def copy(n):
        half, block = n // 4, n % 4
        return pltpu.make_async_copy(
            p_hbm.at[:, pl.ds(block * 8, 8), pl.ds(half * LANES, LANES)], chunk.at[n], sems.at[n])

    for n in range(8):
        copy(n).start()
    flat = chunk.reshape(8 * K * 8, LANES)
    for n in range(8):
        copy(n).wait()
        half, block = n // 4, n % 4
        for i in range(8):
            r = block * 8 + i
            ext[pl.ds(at(r + H, 8) + half * LANES, LANES), :] = flat[pl.ds(n * K * 8 + i, K, stride=8), :].T
    odd = flags[2]
    for own, low in ((own_a, odd), (own_b, 1 - odd)):
        col = jnp.where(low == 1, 0, C - H)
        for r in range(R):
            own[r * H:(r + 1) * H, :] = ext[pl.ds(at(r + H, 8) + col, H), :]


def turn(flags, probes):
    return pl.pallas_call(
        turn_kernel,
        in_specs=[smem_spec(), hbm_spec()],
        out_specs=[vmem_spec()] * 3,
        out_shape=[held(NROW + 16, K), held(R * H, K), held(R * H, K)],
        scratch_shapes=[pltpu.VMEM((8, K, 8, LANES), jnp.float32), pltpu.SemaphoreType.DMA((8,))],
        compiler_params=pltpu.CompilerParams(vmem_limit_bytes=6 * 1024 * 1024),
        cost_estimate=pl.CostEstimate(flops=0, bytes_accessed=12 * 1024 * 1024, transcendentals=0),
        name="turn",
    )(flags, in_hbm(probes))


def corner_kernel(flags, own_a, own_b, lat_a, lat_b, after, *rest):
    *kappa, pay_a, pay_b = rest
    odd = flags[2]
    for own, pay, low in ((own_a, pay_a, odd), (own_b, pay_b, 1 - odd)):
        col = jnp.where(low == 1, 0, C - H)
        pay[:R * H, :] = own[...]
        base = R * H
        if kappa:
            pay[base:base + R, :] = jnp.where(low == 1, kappa[0][:, :LANES], kappa[0][:, LANES:])
            base += R
        for lat in (lat_a, lat_b):
            for r in range(H):
                pay[base:base + H, :] = lat[pl.ds(r * C + col, H), :]
                base += H
        if kappa:
            for lat in (lat_a, lat_b):
                for r in range(H):
                    pay[base:base + 1, :] = lat[pl.ds(H * C + 2 * r + 1 - low, 1), :]
                    base += 1


def corner(flags, own_a, own_b, lat_a, lat_b, after, *kappa):
    rows = R * H + 2 * H * H + (R + 2 * H if kappa else 0)
    return pl.pallas_call(
        corner_kernel,
        in_specs=[smem_spec()] + [vmem_spec()] * 4 + [pl.BlockSpec(memory_space=pl.ANY)] + [vmem_spec()] * len(kappa),
        out_specs=[vmem_spec()] * 2,
        out_shape=[f32(rows, K)] * 2,
        compiler_params=pltpu.CompilerParams(vmem_limit_bytes=2 * 1024 * 1024),
        name="corner",
    )(flags, *in_vmem(own_a, own_b), lat_a, lat_b, after, *kappa)


def keep(ok, x):
    return x if ok is None else jnp.where(ok, x, 0.0)


def put_lat_halos(buf, flags, lat_a, lat_b):
    odd = flags[0]
    lat_ok = (None, flags[1] == 1)
    lat_row = (jnp.where(odd == 1, 0, R + H), jnp.where(odd == 1, R + H, 0))
    for n, lat in ((0, lat_a), (1, lat_b)):
        for r in range(H):
            start = pl.multiple_of(OFF + (lat_row[n] + r) * CB + 8, 8)
            buf[pl.ds(start, C), :] = keep(lat_ok[n], lat[r * C:(r + 1) * C, :])


def put_lon_halos(buf, flags, lon_a, lon_b):
    odd = flags[0]
    lon_odd = flags[2]
    lat_ok = (None, flags[1] == 1)
    lon_ok = (None, flags[3] == 1)
    lat_row = (jnp.where(odd == 1, 0, R + H), jnp.where(odd == 1, R + H, 0))
    lon_col = (jnp.where(lon_odd == 1, 0, C + H), jnp.where(lon_odd == 1, C + H, 0))
    own_rows = R * H if lon_a.shape[0] == R * H + 2 * H * H else OWN_ROWS
    for m, lon in ((0, lon_a), (1, lon_b)):
        for r in range(R):
            start = at(r + H, 4) + lon_col[m]
            buf[pl.ds(start, H), :] = keep(lon_ok[m], lon[r * H:(r + 1) * H, :])
        for n in range(2):
            for r in range(H):
                part = own_rows + (n * H + r) * H
                start = OFF + (lat_row[n] + r) * CB + 4 + lon_col[m]
                buf[pl.ds(start, H), :] = keep(lat_ok[n], keep(lon_ok[m], lon[part:part + H, :]))


def put_own_kappa(kap, act, counts, kappa_ref):
    kap_t = kappa_ref[...].T
    for r in range(R):
        kap[pl.ds(at(r + H, 8), C), :] = jnp.broadcast_to(kap_t[:, r:r + 1], (C, K))
        for s in range(SWEEPS):
            act[s, r + H] = jnp.full((8, K), jnp.where(counts[r] > s, 1.0, 0.0), jnp.float32)


def put_lat_kappa(kap, act, flags, tail_a, tail_b):
    odd = flags[0]
    lat_ok = (None, flags[1] == 1)
    lat_row = (jnp.where(odd == 1, 0, R + H), jnp.where(odd == 1, R + H, 0))
    for n, lat in ((0, tail_a), (1, tail_b)):
        turned = lat[:8, :].T
        if n == 1:
            turned = jnp.where(lat_ok[1], turned, 0.0)
        for r in range(H):
            for h in range(2):
                start = pl.multiple_of(OFF + (lat_row[n] + r) * CB + 8 + h * LANES, 8)
                kap[pl.ds(start, LANES), :] = jnp.broadcast_to(turned[:, 2 * r + h:2 * r + h + 1], (LANES, K))
            wide = jnp.broadcast_to(lat[8 + r:9 + r, :], (8, K))
            for s in range(SWEEPS):
                act[s, lat_row[n] + r] = jnp.where(wide > s, 1.0, 0.0)


def put_lon_kappa(kap, flags, lon_a, lon_b):
    odd = flags[0]
    lon_odd = flags[2]
    lat_ok = (None, flags[1] == 1)
    lat_row = (jnp.where(odd == 1, 0, R + H), jnp.where(odd == 1, R + H, 0))
    lon_col = (jnp.where(lon_odd == 1, 0, C + H), jnp.where(lon_odd == 1, C + H, 0))
    for m, lon in ((0, lon_a), (1, lon_b)):
        src = (jnp.where(lon_odd == 1, LANES - H, 0), jnp.where(lon_odd == 1, 0, LANES - H))[m]
        own = lon[R * H:R * H + R, :].T
        tail = lon[OWN_ROWS + 2 * H * H:, :].T
        low, high = own[:H, :], own[LANES - H:, :]
        edge = jnp.where(src == 0, low, high)
        tail = jnp.where(src == 0, tail[:H, :], tail[LANES - H:, :])
        if m == 1:
            edge = jnp.where(flags[3] == 1, edge, 0.0)
            tail = jnp.where(flags[3] == 1, tail, 0.0)
        for r in range(R):
            kap[pl.ds(at(r + H, 4) + lon_col[m], H), :] = jnp.broadcast_to(edge[:, r:r + 1], (H, K))
        for n in range(2):
            for r in range(H):
                part = jnp.broadcast_to(tail[:, n * H + r:n * H + r + 1], (H, K))
                if n == 1:
                    part = jnp.where(lat_ok[1], part, 0.0)
                kap[pl.ds(OFF + (lat_row[n] + r) * CB + 4 + lon_col[m], H), :] = part


def relax(src, dst, kap, act, s, r, tiles):
    base = pl.multiple_of(r * CB, 8)
    a0 = act[s, r]
    a1 = act[s, r + 1]
    for t in tiles:
        o = base + OFF + t * 8
        up = src[pl.ds(o - CB, 8), :]
        c0 = src[pl.ds(o, 8), :]
        c1 = src[pl.ds(o + CB, 8), :]
        dn = src[pl.ds(o + 2 * CB, 8), :]
        l0 = src[pl.ds(o - 1, 8), :]
        r0 = src[pl.ds(o + 1, 8), :]
        l1 = src[pl.ds(o + CB - 1, 8), :]
        r1 = src[pl.ds(o + CB + 1, 8), :]
        lap0 = (up + c1) + (l0 + r0) - 4.0 * c0
        lap1 = (c0 + dn) + (l1 + r1) - 4.0 * c1
        dst[pl.ds(o, 8), :] = c0 + (a0 * kap[pl.ds(o, 8), :]) * lap0
        dst[pl.ds(o + CB, 8), :] = c1 + (a1 * kap[pl.ds(o + CB, 8), :]) * lap1


INNER = tuple(range(1, CB // 8 - 1))
EDGE = (0, 1, CB // 8 - 2, CB // 8 - 1)


def inner_kernel(ext, kap, act, *levels):
    src = ext
    for s in range(SWEEPS):
        t = s + 1

        def body(i, _):
            relax(src, levels[s], kap, act, s, t + H + 2 * i, INNER)
            return 0

        lax.fori_loop(0, (R - 2 * t) // 2, body, 0)
        src = levels[s]


def inner(ext, kap, act):
    return pl.pallas_call(
        inner_kernel,
        in_specs=[vmem_spec()] * 3,
        out_specs=[vmem_spec()] * SWEEPS,
        out_shape=[held(NROW + 16, K)] * SWEEPS,
        compiler_params=pltpu.CompilerParams(vmem_limit_bytes=1024 * 1024),
        cost_estimate=pl.CostEstimate(flops=0, bytes_accessed=16 * 1024 * 1024, transcendentals=0),
        name="inner",
    )(*in_vmem(ext, kap, act))


def sweep_ends(levels, kap, act):
    for s in range(SWEEPS):
        t = s + 1

        def ends(i, _):
            relax(levels[s], levels[t], kap, act, s, jnp.where(i < 2, t + 2 * i, R + H - t + 2 * i - 4), INNER)
            return 0

        lax.fori_loop(0, 4, ends, 0)


def sweep_sides(levels, kap, act):
    for s in range(SWEEPS):
        t = s + 1
        sides = EDGE[1:3] if t == SWEEPS else EDGE

        def body(i, _):
            relax(levels[s], levels[t], kap, act, s, t + 2 * i, sides)
            return 0

        lax.fori_loop(0, (RE - 2 * t) // 2, body, 0, unroll=2)


def ends_kernel(flags, *refs):
    (ext_in, l1_in, l2_in, l3_in, l4_in, kap_in, act_in, lat_a, lat_b, after,
     tail_a, tail_b, ext, l1, l2, l3, l4, kap, act) = refs
    tail_a[...] = lat_a[H * C:, :]
    tail_b[...] = lat_b[H * C:, :]
    put_lat_kappa(kap, act, flags, tail_a, tail_b)
    put_lat_halos(ext, flags, lat_a, lat_b)
    sweep_ends((ext, l1, l2, l3, l4), kap, act)


def ends(flags, ext, levels, kap, act, lat, after):
    tail_a, tail_b, ext, *levels, kap, act = pl.pallas_call(
        ends_kernel,
        in_specs=[smem_spec()] + [vmem_spec()] * 9 + [pl.BlockSpec(memory_space=pl.ANY)],
        out_specs=[vmem_spec()] * 9,
        out_shape=[f32(16, K), f32(16, K)] + [held(NROW + 16, K)] * 6 + [held(SWEEPS, RE, 8, K)],
        input_output_aliases={1 + i: 2 + i for i in range(7)},
        compiler_params=pltpu.CompilerParams(vmem_limit_bytes=2 * 1024 * 1024),
        cost_estimate=pl.CostEstimate(flops=0, bytes_accessed=8 * 1024 * 1024, transcendentals=0),
        name="ends",
    )(flags, *in_vmem(ext, *levels, kap, act), *lat, after)
    return tail_a, tail_b, ext, levels, kap, act


def coeffs_kernel(flags, counts, kappa_ref, after, *rest):
    *halos, kap, act = rest
    put_own_kappa(kap, act, counts, kappa_ref)
    if halos:
        put_lat_kappa(kap, act, flags, *halos[:2])
        put_lon_kappa(kap, flags, *halos[2:])


def coeffs(flags, counts, kappa, after, *halos):
    return pl.pallas_call(
        coeffs_kernel,
        in_specs=[smem_spec()] * 2 + [vmem_spec(), pl.BlockSpec(memory_space=pl.ANY)] + [vmem_spec()] * len(halos),
        out_specs=[vmem_spec()] * 2,
        out_shape=[held(NROW + 16, K), held(SWEEPS, RE, 8, K)],
        compiler_params=pltpu.CompilerParams(vmem_limit_bytes=1024 * 1024),
        cost_estimate=pl.CostEstimate(flops=0, bytes_accessed=4 * 1024 * 1024, transcendentals=0),
        name="coeffs",
    )(flags, counts, kappa, after, *halos)


def places_kernel(count_ref, cell_ref, owner_ref, after, row_ref, place_ref):
    count = count_ref[0]
    owner = owner_ref[...]
    cell = cell_ref[...]
    row_ref[...] = OFF + 8 + H * CB + (cell >> 8) * CB + (cell & (C - 1))
    owners = jnp.broadcast_to(owner, (SLOTS, SLOTS))
    later = lax.broadcasted_iota(jnp.int32, (SLOTS, SLOTS), 1)
    earlier = lax.broadcasted_iota(jnp.int32, (SLOTS, SLOTS), 0)
    column = jnp.broadcast_to(owner.astype(jnp.float32), (8, SLOTS)).T[:, :1].astype(jnp.int32)
    same = (owners == column) & (earlier < later)
    rank = jnp.sum(jnp.where(same, 1.0, 0.0), axis=0, keepdims=True).astype(jnp.int32)
    slot = lax.broadcasted_iota(jnp.int32, (1, SLOTS), 1)
    place_ref[...] = jnp.where(slot < count, owner * CAP + rank, PLACES)


def places(count, cell, owner, after):
    return pl.pallas_call(
        places_kernel,
        in_specs=[smem_spec()] + [vmem_spec()] * 2 + [pl.BlockSpec(memory_space=pl.ANY)],
        out_specs=[vmem_spec()] * 2,
        out_shape=[jax.ShapeDtypeStruct((1, SLOTS), jnp.int32)] * 2,
        cost_estimate=pl.CostEstimate(flops=0, bytes_accessed=4 * 1024 * 1024, transcendentals=0),
        compiler_params=pltpu.CompilerParams(vmem_limit_bytes=2 * 1024 * 1024),
        name="places",
    )(count, cell, owner, after)


def smooth_kernel(flags, cell_ref, place_ref, *refs):
    (ext_in, l1_in, l2_in, l3_in, l4_in, kap_in, act, lon_a, lon_b,
     out_ref, ext, l1, l2, l3, l4, kap, rows_ref) = refs
    put_lon_kappa(kap, flags, lon_a, lon_b)
    put_lon_halos(ext, flags, lon_a, lon_b)
    sweep_sides((ext, l1, l2, l3, l4), kap, act)
    rows_ref[...] = jnp.zeros_like(rows_ref)

    def copy(i, _):
        for j in range(8):
            t = i * 8 + j
            rows_ref[pl.ds(place_ref[0, t], 1), :] = l4[pl.ds(cell_ref[0, t], 1), :]
        return 0

    lax.fori_loop(0, SLOTS // 8, copy, 0)
    out_ref[...] = rows_ref[:PLACES]


def smooth(flags, cell, place, ext, levels, kap, act, lon):
    return pl.pallas_call(
        smooth_kernel,
        in_specs=[smem_spec()] * 3 + [vmem_spec()] * 9,
        out_specs=[vmem_spec()] * 7,
        out_shape=[f32(PLACES, K)] + [held(NROW + 16, K)] * 6,
        input_output_aliases={3 + i: 1 + i for i in range(6)},
        scratch_shapes=[pltpu.VMEM((PLACES + 8, K), jnp.float32)],
        compiler_params=pltpu.CompilerParams(vmem_limit_bytes=2 * 1024 * 1024),
        name="smooth",
    )(flags, cell, place, *in_vmem(ext, *levels, kap, act), *lon)[0]


def weigh_kernel(b_ref, r_hbm, out_ref, r_ref, sems):
    width = PLACES // WEIGH_PARTS

    def copy(n):
        return pltpu.make_async_copy(r_hbm.at[:, pl.ds(n * width, width)], r_ref.at[n], sems.at[n])

    for n in range(WEIGH_PARTS):
        copy(n).start()
    b = b_ref[...].T
    high = b.astype(jnp.bfloat16)
    low = (b - high.astype(jnp.float32)).astype(jnp.bfloat16)
    both = jnp.concatenate([high, low], axis=0)
    for n in range(WEIGH_PARTS):
        copy(n).wait()
        r = r_ref[n]
        r_high = r.astype(jnp.bfloat16)
        r_low = (r - r_high.astype(jnp.float32)).astype(jnp.bfloat16)
        one = jnp.dot(both, r_high, preferred_element_type=jnp.float32)
        two = jnp.dot(high, r_low, preferred_element_type=jnp.float32)
        out_ref[n * width:(n + 1) * width, :] = (one[:K] + (one[K:] + two)).T


def weigh(buffer, r):
    return pl.pallas_call(
        weigh_kernel,
        in_specs=[vmem_spec(), hbm_spec()],
        out_specs=vmem_spec(),
        out_shape=f32(PLACES, K),
        scratch_shapes=[
            pltpu.VMEM((WEIGH_PARTS, PLACES, PLACES // WEIGH_PARTS), jnp.float32),
            pltpu.SemaphoreType.DMA((WEIGH_PARTS,)),
        ],
        compiler_params=pltpu.CompilerParams(vmem_limit_bytes=6 * 1024 * 1024),
        name="weigh",
    )(buffer, in_hbm(r))


def spread_kernel(flags, cell_ref, place_ref, count_ref, ret_ref, field, pay_a, pay_b, own_a, own_b):
    field[...] = jnp.zeros_like(field)

    count = count_ref[0]

    def add(i, _):
        rows, cells = [], []
        for j in range(8):
            t = i * 8 + j
            live = t < count
            rows.append(ret_ref[pl.ds(jnp.where(live, place_ref[0, t], 0), 1), :])
            cells.append(jnp.where(live, cell_ref[0, t], NROW + OFF))
        for row, cell in zip(rows, cells):
            field[pl.ds(cell, 1), :] = field[pl.ds(cell, 1), :] + row
        return 0

    lax.fori_loop(0, (count + 7) // 8, add, 0)
    odd = flags[0]
    lon_odd = flags[2]
    for pay, low in ((pay_a, odd), (pay_b, 1 - odd)):
        first = jnp.where(low == 1, H, R)
        for r in range(H):
            start = pl.multiple_of(OFF + (first + r) * CB + 8, 8)
            pay[r * C:(r + 1) * C, :] = field[pl.ds(start, C), :]
    for own, low in ((own_a, lon_odd), (own_b, 1 - lon_odd)):
        col = jnp.where(low == 1, 8, 4 + C)
        for r in range(R):
            own[r * H:(r + 1) * H, :] = field[pl.ds(at(r + H, 0) + col, H), :]


def spread(flags, cell, place, count, returned):
    return pl.pallas_call(
        spread_kernel,
        in_specs=[smem_spec()] * 4 + [vmem_spec()],
        out_specs=[vmem_spec()] * 5,
        out_shape=[held(NROW + 16, K), f32(H * C, K), f32(H * C, K), held(R * H, K), held(R * H, K)],
        compiler_params=pltpu.CompilerParams(vmem_limit_bytes=2 * 1024 * 1024),
        name="spread",
    )(flags, cell, place, count, returned)


def gram_terms(sk):
    high = sk.astype(jnp.bfloat16)
    low = (sk - high.astype(jnp.float32)).astype(jnp.bfloat16)
    dot = lambda a, b: lax.dot_general(a, b, (((1,), (1,)), ((), ())), preferred_element_type=jnp.float32)
    return dot(high, high), dot(high, low)


def part(ref, n):
    half, block = n // 4, n % 4
    return ref.at[:, pl.ds(block * 8, 8), pl.ds(half * LANES, LANES)]


def bulk_kernel(flags, *refs):
    (ext_in, l1_in, l2_in, l3_in, l4_in, kap, act, lat_a, lat_b, after, p_hbm,
     ext, l1, l2, l3, l4, chunk, hh_ref, hl_ref, sems) = refs

    def copy_in(n):
        return pltpu.make_async_copy(part(p_hbm, n), chunk.at[n], sems.at[n])

    for n in range(8):
        copy_in(n).start()
    put_lat_halos(ext, flags, lat_a, lat_b)
    sweep_ends((ext, l1, l2, l3, l4), kap, act)
    flat = chunk.reshape(8 * K * 8, LANES)
    lane = lax.broadcasted_iota(jnp.int32, (K, LANES), 1)
    hh = jnp.zeros((K, K), jnp.float32)
    hl = jnp.zeros((K, K), jnp.float32)
    for n in range(8):
        half, block = n // 4, n % 4
        ready = lane >= 8 if half == 0 else lane < LANES - 8
        copy_in(n).wait()
        for i in range(0, 8, 2):
            parts = []
            for j in range(2):
                where = pl.ds(n * K * 8 + i + j, K, stride=8)
                start = at(block * 8 + i + j + H, 8) + half * LANES
                raw = flat[where, :]
                sk = raw + jnp.where(ready, l4[pl.ds(start, LANES), :].T, 0.0)
                flat[where, :] = sk
                parts.append(jnp.where(ready, sk, 0.0))
            one, two = gram_terms(jnp.concatenate(parts, axis=1))
            hh = hh + one
            hl = hl + two
    hh_ref[...] = hh
    hl_ref[...] = hl


def bulk(flags, ext, levels, kap, act, lat, after, probes):
    ext, *levels, chunk, hh, hl = pl.pallas_call(
        bulk_kernel,
        in_specs=[smem_spec()] + [vmem_spec()] * 9 + [pl.BlockSpec(memory_space=pl.ANY), hbm_spec()],
        out_specs=[vmem_spec()] * 8,
        out_shape=[held(NROW + 16, K)] * 5 + [held(8, K, 8, LANES), held(K, K), held(K, K)],
        input_output_aliases={1 + i: i for i in range(5)},
        scratch_shapes=[pltpu.SemaphoreType.DMA((8,))],
        compiler_params=pltpu.CompilerParams(vmem_limit_bytes=2 * 1024 * 1024),
        cost_estimate=pl.CostEstimate(flops=0, bytes_accessed=16 * 1024 * 1024, transcendentals=0),
        name="bulk",
    )(flags, *in_vmem(ext, *levels, kap, act), *lat, after, in_hbm(probes))
    return ext, levels, chunk, hh, hl


def finish_kernel(flags, *refs):
    (ext_in, l1_in, l2_in, l3_in, l4_in, kap, act, chunk_in, hh_ref, hl_ref, lon_a, lon_b,
     gram_ref, ext, l1, l2, l3, l4, chunk) = refs
    put_lon_halos(ext, flags, lon_a, lon_b)
    sweep_sides((ext, l1, l2, l3, l4), kap, act)
    flat = chunk.reshape(8 * K * 8, LANES)
    lane = lax.broadcasted_iota(jnp.int32, (K, LANES), 1)
    hh = hh_ref[...]
    hl = hl_ref[...]
    for block in range(4):
        tiles = []
        for i in range(8):
            r = block * 8 + i + H
            tiles += [l4[pl.ds(at(r, C), 8), :], l4[pl.ds(at(r, 8), 8), :]]
        turned = jnp.concatenate(tiles, axis=0).T
        for i in range(0, 8, 2):
            parts = []
            for j in range(2):
                moved = pltpu.roll(turned, (LANES - 16 * (i + j) - 8) % LANES, 1)
                first = pl.ds(block * K * 8 + i + j, K, stride=8)
                last = pl.ds((4 + block) * K * 8 + i + j, K, stride=8)
                a = flat[first, :] + jnp.where(lane < 8, moved, 0.0)
                b = flat[last, :] + jnp.where(lane >= LANES - 8, moved, 0.0)
                flat[first, :] = a
                flat[last, :] = b
                parts.append(jnp.where(lane < 8, a, jnp.where(lane >= LANES - 8, b, 0.0)))
            one, two = gram_terms(jnp.concatenate(parts, axis=1))
            hh = hh + one
            hl = hl + two
    gram = hh + (hl + hl.T)
    top = gram[:HALF]
    turned = pltpu.roll(gram[HALF:], HALF, 1)
    row = lax.broadcasted_iota(jnp.int32, (HALF, K), 0)
    lane = lax.broadcasted_iota(jnp.int32, (HALF, K), 1)
    gram_ref[:HALF, :] = jnp.where((lane < HALF) & (row > lane), turned, top)
    gram_ref[HALF:, :] = jnp.broadcast_to(jnp.sum(jnp.where(row == lane, turned, 0.0), axis=0, keepdims=True), (8, K))


def finish(flags, ext, levels, kap, act, chunk, hh, hl, lon):
    outs = pl.pallas_call(
        finish_kernel,
        in_specs=[smem_spec()] + [vmem_spec()] * 12,
        out_specs=[vmem_spec()] * 7,
        out_shape=[f32(HALF + 8, K)] + [held(NROW + 16, K)] * 5 + [held(8, K, 8, LANES)],
        input_output_aliases={**{1 + i: 1 + i for i in range(5)}, 8: 6},
        compiler_params=pltpu.CompilerParams(vmem_limit_bytes=3 * 1024 * 1024),
        name="finish",
    )(flags, *in_vmem(ext, *levels, kap, act, chunk, hh, hl), *lon)
    return outs[0], outs[6]


def store_kernel(chunk, after, out_hbm, sems):
    copies = [pltpu.make_async_copy(chunk.at[n], part(out_hbm, n), sems.at[n]) for n in range(8)]
    for copy in copies:
        copy.start()
    for copy in copies:
        copy.wait()


def store(chunk, after):
    return pl.pallas_call(
        store_kernel,
        in_specs=[vmem_spec(), pl.BlockSpec(memory_space=pl.ANY)],
        out_specs=hbm_spec(),
        out_shape=f32(K, R, C),
        scratch_shapes=[pltpu.SemaphoreType.DMA((8,))],
        compiler_params=pltpu.CompilerParams(vmem_limit_bytes=1024 * 1024),
        cost_estimate=pl.CostEstimate(flops=0, bytes_accessed=8 * 1024 * 1024, transcendentals=0),
        name="store",
    )(*in_vmem(chunk), after)


def pairs(size, first):
    return [(i, (i + 1) % size if (i - first) % 2 == 0 else (i - 1) % size) for i in range(size)]


def swap(a, b, axis):
    size = lax.axis_size(axis)
    return lax.ppermute(a, axis, pairs(size, 0)), lax.ppermute(b, axis, pairs(size, 1))


def factor_kernel(scale, x_ref, g1_ref, g2_ref, g3_ref, out_ref, a_ref):
    total = ((x_ref[...] + g1_ref[...]) + (g2_ref[...] + g3_ref[...])) * scale
    top = total[:HALF]
    a_ref[:HALF, :] = top
    lower = top.T[:HALF]
    row = lax.broadcasted_iota(jnp.int32, (HALF, HALF), 0)
    lane = lax.broadcasted_iota(jnp.int32, (HALF, HALF), 1)
    lower = jnp.where(row == lane, jnp.broadcast_to(total[HALF:HALF + 1, :HALF], (HALF, HALF)), lower)
    a_ref[HALF:, :] = jnp.concatenate([jnp.zeros((HALF, HALF), jnp.float32), lower], axis=1)
    sub = lax.broadcasted_iota(jnp.int32, (8, K), 0)
    col = lax.broadcasted_iota(jnp.int32, (8, K), 1)
    wide = lambda x: jnp.broadcast_to(x, (8, K))
    panels, last = [], None
    following = a_ref[0:8, :]
    for q in range(K // 8):
        c = 8 * q
        panel = following
        if q + 1 < K // 8:
            following = a_ref[c + 8:c + 16, :]
            if q > 0:
                done = jnp.concatenate(panels, axis=0)
                following = following - lax.dot_general(
                    done[:, c + 8:c + 16], done, (((0,), (0,)), ((), ())),
                    precision=lax.Precision.HIGHEST, preferred_element_type=jnp.float32)
        b = {(i, m): wide(panel[i:i + 1, c + m:c + m + 1]) for i in range(8) for m in range(i, 8)}
        rows = [wide(panel[i:i + 1, :]) for i in range(8)]
        if q > 0:
            for k in range(8):
                e = [wide(last[k][:, c + m:c + m + 1]) for m in range(8)]
                for i in range(8):
                    for m in range(i, 8):
                        b[i, m] = b[i, m] - e[i] * e[m]
                    rows[i] = rows[i] - e[i] * last[k]
        result = jnp.zeros((8, K), jnp.float32)
        for i in range(8):
            inv = lax.rsqrt(b[i, i])
            u = {m: b[i, m] * inv for m in range(i + 1, 8)}
            for m in range(i + 1, 8):
                for k in range(m, 8):
                    b[m, k] = b[m, k] - u[m] * u[k]
            rows[i] = rows[i] * inv
            for m in range(i + 1, 8):
                rows[m] = rows[m] - u[m] * rows[i]
            result = jnp.where(sub == i, rows[i], result)
        last = rows
        panels.append(result)
        out_ref[c:c + 8, :] = jnp.where(col >= sub + c, result, 0.0)


def factor(scale, parts):
    return pl.pallas_call(
        functools.partial(factor_kernel, scale),
        in_specs=[vmem_spec()] * 4,
        out_specs=vmem_spec(),
        out_shape=f32(K, K),
        scratch_shapes=[pltpu.VMEM((K, K), jnp.float32)],
        compiler_params=pltpu.CompilerParams(vmem_limit_bytes=8 * 1024 * 1024),
        name="factor",
    )(*parts)


def gather_sums(x):
    def stage(x, axis, steps):
        size = lax.axis_size(axis)
        return (x, *[lax.ppermute(x, axis, [(i, i ^ d) for i in range(size)]) for d in steps])

    def total(x, g1, g2, g3):
        return (x + g1) + (g2 + g3)

    x, g1 = stage(x, "lat", (1,))
    x = x + g1
    early = x
    x = total(*stage(x, "lat", (2, 4, 6)))
    x = total(*stage(x, "lon", (1, 2, 3)))
    return early, stage(x, "lon", (4, 8, 12))


def shards(probes, kappa, sweep_counts, obs_cell, obs_owner, obs_count, r_inv):
    n_lat, n_lon = lax.axis_size("lat"), lax.axis_size("lon")
    lat, lon = lax.axis_index("lat"), lax.axis_index("lon")
    flags = jnp.stack([
        lat % 2, ((lat > 0) & (lat < n_lat - 1)).astype(jnp.int32),
        lon % 2, ((lon > 0) & (lon < n_lon - 1)).astype(jnp.int32),
    ]).astype(jnp.int32)
    lat_a, lat_b = swap(*edge_pack(sweep_counts, kappa, probes), "lat")
    ext, own_a, own_b = turn(flags, probes)
    kap, act = coeffs(flags, sweep_counts, kappa, own_a)
    levels = inner(ext, kap, act)
    count = obs_count.reshape(1)
    lon_pay = corner(flags, own_a, own_b, lat_a, lat_b, levels[-1], kappa)
    cell, place = places(count, obs_cell.reshape(1, SLOTS), obs_owner.reshape(1, SLOTS), lon_pay[0])
    tail_a, tail_b, ext, levels, kap, act = ends(flags, ext, levels, kap, act, (lat_a, lat_b), lon_pay[0])
    lon_a, lon_b = swap(*lon_pay, "lon")
    outgoing = smooth(flags, cell, place, ext, levels, kap, act, (lon_a, lon_b))
    buffer = lax.all_to_all(outgoing, "lon", split_axis=0, concat_axis=0, tiled=True)
    mixed = weigh(buffer, r_inv[0, 0])
    returned = lax.all_to_all(mixed, "lon", split_axis=0, concat_axis=0, tiled=True)
    field, pay_a, pay_b, own_a, own_b = spread(flags, cell, place, count, returned)
    kap, act = coeffs(flags, sweep_counts, kappa, pay_a, tail_a, tail_b, lon_a, lon_b)
    levels = inner(field, kap, act)
    lat_a, lat_b = swap(pay_a, pay_b, "lat")
    lon_pay = corner(flags, own_a, own_b, lat_a, lat_b, levels[-1])
    field, levels, chunk, hh, hl = bulk(flags, field, levels, kap, act, (lat_a, lat_b), lon_pay[0], probes)
    gram, chunk = finish(flags, field, levels, kap, act, chunk, hh, hl, swap(*lon_pay, "lon"))
    early, parts = gather_sums(gram)
    sketch = store(chunk, early)
    cells_all = R * C * n_lat * n_lon
    r_factor = factor(1.0 / cells_all, parts)
    return (sketch, r_factor)


def solution(mesh):
    return jax.shard_map(
        shards,
        mesh=mesh,
        in_specs=(
            P(None, "lat", "lon"),
            P("lat", "lon"),
            P("lat"),
            P(("lat", "lon")),
            P(("lat", "lon"), None),
            P("lat", "lon"),
            P("lat", "lon", None, None),
        ),
        out_specs=(P(None, "lat", "lon"), P()),
        check_vma=False,
    )
```
